256 devices in a mesh: cent: 128 (over y, x, z), rep: 2 (over core).
Axes of the slice: x: 4, y: 4, z: 8, core: 2. Of those that a mesh axis runs over, the one named last changes fastest.
Arguments:
- new_vectors: float32 [8192, 1024], P(('cent', 'rep')), may hold values from -6 to 6
- centroids: float32 [65536, 1024], P('cent'), may hold values from -6 to 6
- primary_owner: int32 [8192, 1], P(('cent', 'rep')), may hold values from 0 to 127; in each aligned block of 32 rows (0 to 31, 32 to 63, ...) at most 2 rows name the same one
- primary_row: int32 [8192, 1], P(('cent', 'rep')), may hold values from 0 to 511
- cand_owner: int32 [8192, 4], P(('cent', 'rep')), may hold values from 0 to 127, all different within a row; in each aligned block of 32 rows (0 to 31, 32 to 63, ...) at most 2 rows name the same one
- cand_row: int32 [8192, 256], P(('cent', 'rep')), may hold values from 0 to 511
Outputs:
- spill_loss: float32 [8192, 256], P(('cent', 'rep'))
The draws below stay inside these ranges and needn't reach their ends.
Inputs may be any that keep to these rules, and one draw needn't show every extreme that they name: `primary_owner`: in each aligned block of 32 vectors (the vectors of one device) no shard is named by more than 2 vectors, a bound that some block reaches. `cand_owner`: each vector names 4 different shards; in each aligned block of 32 vectors (the vectors of one device) no shard is named by more than 2 vectors, a bound that some block reaches.
All inputs are finite; a program needn't handle non-finite values.
Results may differ from the reference program's by a relative error of at most 0.00007.
Values sent between devices are 32-bit elements; how exact they have to be, the bound alone decides.
No kernel may reach another device: no remote copies, remote signals or barrier semaphores. Data moves between devices by JAX's collectives and lax.ppermute only.
A program may use at most 64 MiB of HBM per device.

```python
import math
import jax
import jax.numpy as jnp
import numpy as np
from jax import lax

D = 1024
V_DEV = 32
CENT_DEV = 512
CGROUPS = 4
GSIZE = 64
CAND = 256
VECTORS = 8192
CENTROIDS = 65536
PCAP = 2
SCAP = 2
N_CENT = 128


def set_ends(values, rng, low, high):
    place = [jax.random.randint(jax.random.fold_in(rng, axis), (), 0, length) for axis, length in enumerate(values.shape)]
    widest = values.shape.index(max(values.shape))
    next_to = place[:widest] + [(place[widest] + 1) % values.shape[widest]] + place[widest + 1:]
    return values.at[tuple(place)].set(low).at[tuple(next_to)].set(high)


def levels(own_key, shape, cuts, least, high):
    def one(position, parts):
        heights = jax.random.uniform(jax.random.fold_in(jax.random.fold_in(own_key, 6), position), (parts,), jnp.float32, least / len(cuts), high / len(cuts))
        return jnp.repeat(jnp.exp(heights), shape[position] // parts).reshape((-1,) + (1,) * (len(shape) - position - 1))

    loudness = one(*cuts[0])
    for cut in cuts[1:]:
        loudness = loudness * one(*cut)
    return loudness


def deal_out(own_key, own, number, rows, number_of, top, most, skew):
    order = jax.random.permutation(own_key, number_of)
    packed, common = load_shares(number_of, rows * top, most, skew, True), load_shares(number_of, rows * top, most, skew, False)
    places = jnp.arange(number_of)

    def named(lengths, offset_by):
        used = int((lengths > 0).sum())
        fixed = max(1, used // 4)
        passed = fixed + (places - fixed + offset_by * (used - fixed)) % max(1, number_of - fixed)
        return jnp.zeros((number_of,), jnp.int32).at[order[jnp.where(places < fixed, places, passed)]].set(jnp.asarray(lengths, jnp.int32))

    lengths = jnp.where(number % 4 == 0, named(packed, number // 4), named(common, number - number // 4 - 1))
    mixed = jax.random.permutation(jax.random.fold_in(own, 3), number_of)
    donor, receiver = mixed[0:number_of // 2 * 2:2], mixed[1:number_of // 2 * 2:2]
    margin = jnp.minimum(lengths[donor] - 1, most - lengths[receiver]) // 2
    margin = jnp.where((donor == order[0]) | (receiver == order[0]) | (lengths[receiver] == 0), 0, jnp.maximum(margin, 0))
    passed = jax.random.randint(jax.random.fold_in(own, 4), (number_of // 2,), 0, 1 << 20) % (margin + 1)
    lengths = lengths.at[donor].add(-passed).at[receiver].add(passed)
    members = jnp.searchsorted(jnp.cumsum(lengths), jnp.arange(rows * top), side="right").astype(jnp.int32)
    table = members.reshape(top, rows).T
    table = table[jax.random.permutation(jax.random.fold_in(own, 1), rows)]
    offset_by = jax.random.randint(jax.random.fold_in(own, 2), (rows, 1), 0, top)
    return jnp.take_along_axis(table, (jnp.arange(top)[None, :] + offset_by) % top, axis=1)


def load_shares(count, total, limit, slope, full):
    loads = [(1 << 20) // math.isqrt(standing ** slope) + 1 for standing in range(1, count + 1)]
    largest = limit if full else min(limit, max(-(-total // count), total * loads[0] // sum(loads)))
    least = 1 if total - largest >= count - 1 else 0
    counts, spare = [largest] + [least] * (count - 1), total - largest - least * (count - 1)
    while spare > 0:
        free = [i for i in range(1, count) if counts[i] < largest] or [i for i in range(1, count) if counts[i] < limit]
        mass, budget = sum([loads[i] for i in free]), spare
        for i in free:
            more = min(limit - counts[i], max(1, budget * loads[i] // mass), spare)
            counts[i] = counts[i] + more
            spare = spare - more
    return np.array(counts)


def scatter_about(rng, dims, scale, reach, split=(), held_as=jnp.bfloat16):
    values = jax.random.normal(rng, dims, jnp.float32) * scale
    if len(split) > 0:
        values = levels(rng, dims, split, -0.22, 0.18) * values
    return jnp.clip(values, min=-reach, max=reach).astype(held_as)


def setup_inputs(seed: int = 0) -> dict:
    key_list = jax.random.split(jax.random.key(seed), 7)
    new_vectors = scatter_about(key_list[0], (VECTORS, D), 1.0, 6.0, ((0, 256),), jnp.float32)
    centroids = scatter_about(key_list[1], (CENTROIDS, D), 1.0, 6.0, ((0, 128),), jnp.float32)
    primary_owner_keys = jax.random.split(jax.random.fold_in(key_list[2], 1), VECTORS // V_DEV)
    primary_owner_turns = jax.random.permutation(jax.random.fold_in(key_list[2], 3), VECTORS // V_DEV)
    primary_owner = jax.vmap(lambda own, number: deal_out(jax.random.fold_in(key_list[2], 2), own, number, V_DEV, N_CENT, 1, PCAP, 2))(primary_owner_keys, primary_owner_turns).reshape((VECTORS, 1))
    primary_row = set_ends(jax.random.randint(key_list[3], (VECTORS, 1), 0, CENT_DEV), jax.random.fold_in(key_list[3], 1), 0, CENT_DEV - 1).astype(jnp.int32)
    cand_owner_keys = jax.random.split(jax.random.fold_in(key_list[4], 1), VECTORS // V_DEV)
    cand_owner_turns = jax.random.permutation(jax.random.fold_in(key_list[4], 3), VECTORS // V_DEV)
    cand_owner = jax.vmap(lambda own, number: deal_out(jax.random.fold_in(key_list[4], 2), own, number, V_DEV, N_CENT, CGROUPS, SCAP, 2))(cand_owner_keys, cand_owner_turns).reshape((VECTORS, CGROUPS))
    cand_row = set_ends(jax.random.randint(key_list[5], (VECTORS, CAND), 0, CENT_DEV), jax.random.fold_in(key_list[5], 1), 0, CENT_DEV - 1).astype(jnp.int32)
    return {"new_vectors": new_vectors, "centroids": centroids, "primary_owner": primary_owner, "primary_row": primary_row, "cand_owner": cand_owner, "cand_row": cand_row}


amplify = 1.0
tiny = 1e-6


def reference(new_vectors, centroids, primary_owner, primary_row, cand_owner, cand_row):
    prim_ids = (primary_owner[:, 0] * CENT_DEV + primary_row[:, 0]).astype(jnp.int32)
    primary = jnp.take(centroids, prim_ids, axis=0)
    residual = new_vectors - primary
    cand_ids = (jnp.repeat(cand_owner, GSIZE, axis=1) * CENT_DEV + cand_row).astype(jnp.int32)
    norms_all = jnp.sum(centroids * centroids, axis=1)
    blocks = VECTORS // 8

    def one_block(item):
        vectors_in, resid_in, ids_in = item
        picked = jnp.take(centroids, ids_in, axis=0)
        cross_x = jnp.einsum("vd,vcd->vc", vectors_in, picked, precision=lax.Precision.HIGHEST)
        cross_r = jnp.einsum("vd,vcd->vc", resid_in, picked, precision=lax.Precision.HIGHEST)
        sq_x = jnp.sum(vectors_in * vectors_in, axis=1)[:, None]
        sq_r = jnp.sum(resid_in * resid_in, axis=1)[:, None]
        dot_rx = jnp.sum(resid_in * vectors_in, axis=1)[:, None]
        gap = dot_rx - cross_r
        return (sq_x - 2.0 * cross_x + jnp.take(norms_all, ids_in) + amplify * gap * gap / (sq_r + tiny)) / D

    result = lax.map(one_block, (new_vectors.reshape(blocks, 8, D), residual.reshape(blocks, 8, D), cand_ids.reshape(blocks, 8, CAND)))
    return result.reshape(VECTORS, CAND)
```

```python
import jax
import jax.numpy as jnp
from jax import lax
from jax.experimental import pallas as pl
from jax.experimental.pallas import tpu as pltpu
from jax.sharding import Mesh, PartitionSpec as P

D = 1024
V = 32
GROUPS = 4
GSIZE = 64
ROWS = 512
NY, NX, NZ = 4, 4, 8
COLS = NY * NX
COLV = NZ * V
SLOTS = COLS * NZ * 2
K = 32
amplify = 1.0
tiny = 1e-06

F32, BF16, I32 = jnp.float32, jnp.bfloat16, jnp.int32
VMEM = pl.BlockSpec(memory_space=pltpu.VMEM)
SMEM = pl.BlockSpec(memory_space=pltpu.SMEM)
NN = (((1,), (0,)), ((), ()))
NT = (((1,), (1,)), ((), ()))
TN = (((0,), (0,)), ((), ()))


def call(kernel, out_shape, *operands, smem=(), name=None):
    specs = [SMEM if i in smem else VMEM for i in range(len(operands))]
    many = isinstance(out_shape, (list, tuple))
    return pl.pallas_call(
        kernel,
        out_shape=out_shape,
        in_specs=specs,
        out_specs=[VMEM] * len(out_shape) if many else VMEM,
        compiler_params=pltpu.CompilerParams(vmem_limit_bytes=48 * 2**20),
        name=name,
    )(*operands)


def shape(dims, dtype=F32):
    return jax.ShapeDtypeStruct(dims, dtype)


def split3(a):
    hi = a.astype(BF16)
    rest = a - hi.astype(F32)
    mid = rest.astype(BF16)
    lo = (rest - mid.astype(F32)).astype(BF16)
    return hi, mid, lo


def dot(a, b, dims=NN):
    return lax.dot_general(a, b, dims, preferred_element_type=F32)


def pick(onehot, pieces):
    hi, mid, lo = pieces
    return dot(onehot, hi) + dot(onehot, mid) + dot(onehot, lo)


def bits(mask):
    return jnp.where(mask, 1.0, 0.0)


def iota(dims, axis):
    return lax.broadcasted_iota(I32, dims, axis)


def before_same_block(rows):
    u, w = iota((rows, rows), 0), iota((rows, rows), 1)
    return bits((w < u) & ((u >> 5) == (w >> 5))).astype(BF16)


def before_all(rows):
    return bits(iota((rows, rows), 1) < iota((rows, rows), 0)).astype(BF16)


def prepare_kernel(c_ref, pieces_ref, norms_ref):
    c = c_ref[...]
    for i, piece in enumerate(split3(c)):
        pieces_ref[i] = piece
    squares = split3(c * c)
    ones = jnp.ones((8, D), BF16)
    norms_ref[...] = sum(dot(ones, s, NT) for s in squares)


def request_kernel(me_ref, info_ref, out_ref):
    me = me_ref[0]
    lane = iota((COLV, 128), 1)
    owner = info_ref[:, 0:1]
    row = info_ref[:, 1:2].astype(F32)
    hit = (owner == lane * NZ + me) & (lane < COLS)
    hits = bits(hit)
    rank = dot(before_same_block(COLV), hits.astype(BF16))
    sums = [
        jnp.where(hit & (rank == float(k)), row, 0.0).reshape(NZ, V, 128).sum(axis=1)
        for k in range(2)
    ]
    plane_from = bits(((owner & 7) == lane) & (lane < NZ)).astype(BF16)
    wanted = lane < 0
    for g in range(GROUPS):
        wanted = wanted | ((info_ref[:, 2 + g : 3 + g] & 7) == lane)
    plane_to = bits(wanted & (lane < NZ)).astype(BF16)
    most = jnp.max(dot(plane_from, plane_to, TN))
    small = iota((NZ, 128), 1)
    for a in range(COLS):
        tile = jnp.where(
            small == 0,
            sums[0][:, a : a + 1],
            jnp.where(small == 1, sums[1][:, a : a + 1], most),
        )
        out_ref[a] = tile.astype(I32)


def slots_kernel(me_ref, info_ref, out_ref):
    me = me_ref[0]
    lane = iota((COLV, 128), 1)
    hits = []
    for g in range(GROUPS):
        owner = info_ref[:, 2 + g : 3 + g]
        hits.append((owner == lane * NZ + me) & (lane < COLS))
    any_hit = bits(hits[0] | hits[1] | hits[2] | hits[3])
    rank = dot(before_same_block(COLV), any_hit.astype(BF16))
    block = iota((NZ, COLV), 1) >> 5
    mine = block == iota((NZ, COLV), 0)
    for g in range(GROUPS):
        for k in range(2):
            turned = bits(hits[g] & (rank == float(k))).T
            for b in range(COLS):
                tile = jnp.where(mine, turned[b : b + 1, :], 0.0)
                out_ref[g, b * 16 + k * 8 : b * 16 + k * 8 + 8, :] = tile


def relay_kernel(me_ref, turn_ref, info_ref, slots_ref, send_ref, take_ref):
    me = me_ref[0]
    base = (turn_ref[0] * K).astype(F32)
    lane = iota((COLV, 128), 1)
    u = iota((COLV, 1), 0)
    owner = info_ref[:, 0:1]
    hits = bits((owner == lane * NZ + me) & (lane < COLS))
    rank = dot(before_same_block(COLV), hits.astype(BF16))
    rank = jnp.sum(rank * hits, axis=1, keepdims=True)
    here = (owner & 7) == me
    wanted = lane < 0
    to_me = u < 0
    for g in range(GROUPS):
        plane = info_ref[:, 2 + g : 3 + g] & 7
        wanted = wanted | (plane == lane)
        to_me = to_me | (plane == me)
    earlier = before_all(COLV)
    leaves = wanted & (lane < NZ) & here
    order = dot(earlier, bits(leaves).astype(BF16))
    place = jnp.where(leaves, order - base, -1.0).T
    depth = iota((K, COLV), 0).astype(F32)
    rows = jnp.concatenate([bits(place[z : z + 1, :] == depth) for z in range(NZ)], axis=0)
    slot = (owner >> 3) * 16 + rank.astype(I32) * 8 + (u >> 5)
    held = bits((slot == iota((COLV, SLOTS), 1)) & here)
    send_ref[...] = dot(rows.astype(BF16), held.astype(BF16)).astype(BF16)
    comes = ((owner & 7) == lane) & (lane < NZ) & to_me
    order = dot(earlier, bits(comes).astype(BF16)) - base
    fits = comes & (order >= 0.0) & (order < float(K))
    at = jnp.sum(jnp.where(fits, lane.astype(F32) * K + order + 1.0, 0.0), axis=1, keepdims=True)
    found = bits(at == iota((COLV, NZ * K), 1).astype(F32) + 1.0).astype(BF16)
    all_slots = slots_ref[0] + slots_ref[1] + slots_ref[2] + slots_ref[3]
    take_ref[...] = dot(all_slots.astype(BF16), found).astype(BF16)


def fetch_kernel(asked_ref, pieces_ref, out_ref, most_ref):
    column = iota((COLS * NZ, ROWS), 1)
    pieces = [pieces_ref[i] for i in range(3)]
    for k in range(2):
        onehot = bits(asked_ref[:, k : k + 1] == column).astype(BF16)
        out_ref[:, k * 8 : k * 8 + 8, :] = pick(onehot, pieces).reshape(COLS, 8, D)
    most = jnp.max(asked_ref[:, 2:3].astype(F32)).astype(I32)
    most_ref[...] = jnp.full((8, 128), most, I32)


def move_kernel(onehot_ref, in_ref, out_ref):
    out_ref[...] = pick(onehot_ref[...], split3(in_ref[...]))


def vectors_kernel(slots_ref, in_ref, out_ref):
    slots = [slots_ref[g] for g in range(GROUPS)]
    every = (slots[0] + slots[1] + slots[2] + slots[3]).astype(BF16)
    out_ref[:, :D] = pick(every, split3(in_ref[:, :D]))
    rows = jnp.zeros((SLOTS, 128), F32)
    for h in range(2):
        pieces = split3(in_ref[:, D + 128 * h : D + 128 * h + 128])
        rows = rows + jnp.where(iota((SLOTS, 128), 1) < GSIZE, pick(slots[2 * h].astype(BF16), pieces), 0.0)
        odd = pltpu.roll(pick(slots[2 * h + 1].astype(BF16), pieces), GSIZE, 1)
        rows = rows + jnp.where(iota((SLOTS, 128), 1) < GSIZE, odd, 0.0)
    out_ref[:, D:] = rows


def lookup(table, rows):
    low, high = rows & 127, rows >> 7
    found = jnp.zeros(rows.shape, F32)
    for i in range(ROWS // 128):
        part = jnp.take_along_axis(table[:, 128 * i : 128 * i + 128], low, axis=1)
        found = jnp.where(high == i, part, found)
    return found


def scores(a, pieces_ref):
    hi, mid, lo = split3(a)
    chi, cmid, clo = (pieces_ref[i] for i in range(3))
    small = dot(mid, cmid, NT) + dot(lo, chi, NT) + dot(hi, clo, NT)
    return dot(hi, chi, NT) + (dot(hi, cmid, NT) + dot(mid, chi, NT) + small)


def near_kernel(x_ref, pieces_ref, norms_ref, out_ref):
    x = x_ref[:, :D]
    rows = x_ref[:, D:].astype(I32)
    square = jnp.sum(x * x, axis=1, keepdims=True)
    table = square - 2.0 * scores(x, pieces_ref) + norms_ref[0:1, :]
    out_ref[...] = lookup(table, rows)


def loss_kernel(p_ref, x_ref, near_ref, pieces_ref, out_ref):
    x = x_ref[:, :D]
    rows = x_ref[:, D:].astype(I32)
    r = x - p_ref[...]
    rx = jnp.sum(r * x, axis=1, keepdims=True)
    rr = jnp.sum(r * r, axis=1, keepdims=True)
    gap = rx - lookup(scores(r, pieces_ref), rows)
    loss = (near_ref[...] + amplify * gap * gap / (rr + tiny)) / D
    loss = loss.reshape(COLS, 2, NZ, 128)
    second = pltpu.roll(loss[:, 1].reshape(COLS * NZ, 128), GSIZE, 1)
    first = loss[:, 0].reshape(COLS * NZ, 128)
    out_ref[...] = jnp.where(iota((COLS * NZ, 128), 1) < GSIZE, first, second)


def collect_kernel(owner_ref, in_ref, out_ref):
    lane = iota((V, 128), 1)
    hits = [owner_ref[:, g : g + 1] == lane for g in range(GROUPS)]
    rank = dot(before_same_block(V), bits(hits[0] | hits[1] | hits[2] | hits[3]).astype(BF16))
    a = in_ref[...]
    plain, rolled = split3(a), split3(pltpu.roll(a, GSIZE, 1))
    for h in range(2):
        halves = []
        for g in (2 * h, 2 * h + 1):
            first = bits(hits[g] & (rank == 0.0)).astype(BF16)
            second = bits(hits[g] & (rank == 1.0)).astype(BF16)
            if g % 2 == 0:
                halves.append(pick(first, plain) + pick(second, rolled))
            else:
                halves.append(pick(first, rolled) + pick(second, plain))
        out_ref[:, 128 * h : 128 * h + 128] = jnp.where(lane < GSIZE, halves[0], halves[1])


def swap(a, axes):
    return lax.all_to_all(a, axes, split_axis=0, concat_axis=0, tiled=True)


def shards(new_vectors, centroids, primary_owner, primary_row, cand_owner, cand_row):
    plane = ("y", "x")
    me = lax.axis_index("z").astype(I32).reshape(1)
    info = jnp.concatenate([primary_owner, primary_row, cand_owner], axis=1)
    info = jnp.pad(info, ((0, 0), (0, 128 - info.shape[1])))
    with jax.named_scope("column_info"):
        info = swap(jnp.broadcast_to(info[None], (NZ, V, 128)), "z").reshape(COLV, 128)
    with jax.named_scope("column_vectors"):
        wide = jnp.concatenate([new_vectors, cand_row.astype(F32)], axis=1)
        column = swap(jnp.broadcast_to(wide[None], (NZ,) + wide.shape), "z").reshape(COLV, D + 256)
    pieces, norms = call(
        prepare_kernel, [shape((3, ROWS, D), BF16), shape((8, ROWS))], centroids, name="prepare"
    )
    with jax.named_scope("requests"):
        asks = call(request_kernel, shape((COLS, NZ, 128), I32), me, info, smem=(0,), name="request")
        asked = swap(asks, plane).reshape(COLS * NZ, 128)
    slots = call(slots_kernel, shape((GROUPS, SLOTS, COLV)), me, info, smem=(0,), name="slots")

    def relay(turn):
        return call(
            relay_kernel,
            [shape((NZ * K, SLOTS), BF16), shape((SLOTS, NZ * K), BF16)],
            me,
            turn.reshape(1),
            info,
            slots,
            smem=(0, 1),
            name="relay",
        )

    send, take = relay(jnp.int32(0))
    with jax.named_scope("primary_rows"):
        found, most = call(
            fetch_kernel, [shape((COLS, 16, D)), shape((8, 128), I32)], asked, pieces, name="fetch"
        )
        fetched = swap(found, plane).reshape(SLOTS, D)
        most = most[0, 0]
        most = jnp.maximum(most, lax.ppermute(most.reshape(1, 1), "rep", [(0, 1), (1, 0)])[0, 0])

    def across(send, take):
        out = call(move_kernel, shape((NZ * K, D)), send, fetched, name="send")
        got = swap(out.reshape(NZ, K, D), "z").reshape(NZ * K, D)
        return call(move_kernel, shape((SLOTS, D)), take, got, name="take")

    def more(state):
        turn, total = state
        return turn + 1, total + across(*relay(turn))

    with jax.named_scope("primary_across"):
        primaries = across(send, take)
        _, primaries = lax.while_loop(lambda s: s[0] * K < most, more, (jnp.int32(1), primaries))
    with jax.named_scope("vectors_out"):
        vectors = call(vectors_kernel, shape((SLOTS, D + 128)), slots, column, name="vectors")
        vectors = swap(vectors.reshape(COLS, 16, D + 128), plane).reshape(SLOTS, D + 128)
    near = call(near_kernel, shape((SLOTS, 128)), vectors, pieces, norms, name="near")
    with jax.named_scope("primaries_out"):
        primaries = swap(primaries.reshape(COLS, 16, D), plane).reshape(SLOTS, D)
    losses = call(loss_kernel, shape((COLS * NZ, 128)), primaries, vectors, near, pieces, name="loss")
    with jax.named_scope("losses_back"):
        back = swap(losses.reshape(COLS * NZ, 1, 128), ("y", "x", "z")).reshape(COLS * NZ, 128)
    return call(collect_kernel, shape((V, GROUPS * GSIZE)), cand_owner, back, name="collect")


def solution(mesh):
    fine = Mesh(mesh.devices.reshape(NY, NX, NZ, 2), ("y", "x", "z", "rep"))
    rows = P(("y", "x", "z", "rep"), None)
    in_specs = (rows, P(("y", "x", "z"), None), rows, rows, rows, rows)
    return jax.shard_map(shards, mesh=fine, in_specs=in_specs, out_specs=rows, check_vma=False)
```

```python
import jax
import jax.numpy as jnp
from jax import lax
from jax.experimental import pallas as pl
from jax.experimental.pallas import tpu as pltpu
from jax.sharding import Mesh, PartitionSpec as P

D = 1024
V = 32
GROUPS = 4
GSIZE = 64
ROWS = 512
NY, NX, NZ = 4, 4, 8
COLS = NY * NX
COLV = NZ * V
SLOTS = COLS * NZ * 2
K = 32
amplify = 1.0
tiny = 1e-06

F32, BF16, I32 = jnp.float32, jnp.bfloat16, jnp.int32
VMEM = pl.BlockSpec(memory_space=pltpu.VMEM)
SMEM = pl.BlockSpec(memory_space=pltpu.SMEM)
ANY = pl.BlockSpec(memory_space=pl.ANY)
NN = (((1,), (0,)), ((), ()))
NT = (((1,), (1,)), ((), ()))
TN = (((0,), (0,)), ((), ()))


def call(kernel, out_shape, *operands, smem=(), outside=(), scratch=(), far=False, name=None):
    specs = [SMEM if i in smem else ANY if i in outside else VMEM for i in range(len(operands))]
    many = isinstance(out_shape, (list, tuple))
    out_spec = ANY if far else VMEM
    return pl.pallas_call(
        kernel,
        out_shape=out_shape,
        in_specs=specs,
        out_specs=[out_spec] * len(out_shape) if many else out_spec,
        scratch_shapes=list(scratch),
        compiler_params=pltpu.CompilerParams(vmem_limit_bytes=24 * 2**20),
        name=name,
    )(*operands)


def shape(dims, dtype=F32):
    return jax.ShapeDtypeStruct(dims, dtype)


def split3(a):
    hi = a.astype(BF16)
    rest = a - hi.astype(F32)
    mid = rest.astype(BF16)
    lo = (rest - mid.astype(F32)).astype(BF16)
    return hi, mid, lo


def dot(a, b, dims=NN):
    return lax.dot_general(a, b, dims, preferred_element_type=F32)


def pick(onehot, pieces):
    hi, mid, lo = pieces
    return dot(onehot, hi) + dot(onehot, mid) + dot(onehot, lo)


def bits(mask):
    return jnp.where(mask, 1.0, 0.0)


def iota(dims, axis):
    return lax.broadcasted_iota(I32, dims, axis)


def before_same_block(rows):
    u, w = iota((rows, rows), 0), iota((rows, rows), 1)
    return bits((w < u) & ((u >> 5) == (w >> 5))).astype(BF16)


def before_all(rows):
    return bits(iota((rows, rows), 1) < iota((rows, rows), 0)).astype(BF16)


def prepare_kernel(c_ref, pieces_ref, norms_ref):
    c = c_ref[...]
    for i, piece in enumerate(split3(c)):
        pieces_ref[i] = piece
    squares = split3(c * c)
    ones = jnp.ones((8, D), BF16)
    norms_ref[...] = sum(dot(ones, s, NT) for s in squares)


def info_kernel(owner_ref, row_ref, cand_ref, out_ref):
    tile = jnp.concatenate(
        [owner_ref[...], row_ref[...], cand_ref[...], jnp.zeros((2, V), I32)], axis=0
    )
    tile = jnp.concatenate([tile, jnp.zeros((8, 128 - V), I32)], axis=1)
    for z in range(NZ):
        out_ref[z] = tile


def unpack_kernel(tiles_ref, out_ref):
    quarters = []
    for h in range(2):
        quarters.append(jnp.concatenate([tiles_ref[4 * h + i][:, :V] for i in range(4)], axis=1))
    wide = jnp.concatenate(quarters, axis=1)
    wide = jnp.concatenate([wide, jnp.zeros((120, COLV), I32)], axis=0)
    out_ref[...] = wide.T


def request_kernel(me_ref, tiles_ref, out_ref, info_ref):
    me = me_ref[0]
    unpack_kernel(tiles_ref, info_ref)
    lane = iota((COLV, 128), 1)
    owner = info_ref[:, 0:1]
    row = info_ref[:, 1:2].astype(F32)
    hit = (owner == lane * NZ + me) & (lane < COLS)
    hits = bits(hit)
    rank = dot(before_same_block(COLV), hits.astype(BF16))
    sums = [
        jnp.where(hit & (rank == float(k)), row, 0.0).reshape(NZ, V, 128).sum(axis=1)
        for k in range(2)
    ]
    plane_from = bits(((owner & 7) == lane) & (lane < NZ)).astype(BF16)
    wanted = lane < 0
    for g in range(GROUPS):
        wanted = wanted | ((info_ref[:, 2 + g : 3 + g] & 7) == lane)
    plane_to = bits(wanted & (lane < NZ)).astype(BF16)
    most = jnp.max(dot(plane_from, plane_to, TN))
    small = iota((NZ, 128), 1)
    for a in range(COLS):
        tile = jnp.where(
            small == 0,
            sums[0][:, a : a + 1],
            jnp.where(small == 1, sums[1][:, a : a + 1], most),
        )
        out_ref[a] = tile.astype(I32)


def slots_kernel(me_ref, info_ref, out_ref):
    me = me_ref[0]
    lane = iota((COLV, 128), 1)
    hits = []
    for g in range(GROUPS):
        owner = info_ref[:, 2 + g : 3 + g]
        hits.append((owner == lane * NZ + me) & (lane < COLS))
    any_hit = bits(hits[0] | hits[1] | hits[2] | hits[3])
    rank = dot(before_same_block(COLV), any_hit.astype(BF16))
    block = iota((NZ, COLV), 1) >> 5
    mine = block == iota((NZ, COLV), 0)
    for g in range(GROUPS):
        for k in range(2):
            turned = bits(hits[g] & (rank == float(k))).T
            for b in range(COLS):
                tile = jnp.where(mine, turned[b : b + 1, :], 0.0)
                out_ref[g, b * 16 + k * 8 : b * 16 + k * 8 + 8, :] = tile


def relay_kernel(me_ref, turn_ref, info_ref, slots_ref, send_ref, take_ref):
    me = me_ref[0]
    base = (turn_ref[0] * K).astype(F32)
    lane = iota((COLV, 128), 1)
    u = iota((COLV, 1), 0)
    owner = info_ref[:, 0:1]
    hits = bits((owner == lane * NZ + me) & (lane < COLS))
    rank = dot(before_same_block(COLV), hits.astype(BF16))
    rank = jnp.sum(rank * hits, axis=1, keepdims=True)
    here = (owner & 7) == me
    wanted = lane < 0
    to_me = u < 0
    for g in range(GROUPS):
        plane = info_ref[:, 2 + g : 3 + g] & 7
        wanted = wanted | (((plane - me) & 7) == lane)
        to_me = to_me | (plane == me)
    earlier = before_all(COLV)
    leaves = wanted & (lane < NZ) & here
    order = dot(earlier, bits(leaves).astype(BF16))
    place = jnp.where(leaves, order - base, -1.0).T
    depth = iota((K, COLV), 0).astype(F32)
    rows = jnp.concatenate([bits(place[z : z + 1, :] == depth) for z in range(NZ)], axis=0)
    slot = (owner >> 3) * 16 + rank.astype(I32) * 8 + (u >> 5)
    held = bits((slot == iota((COLV, SLOTS), 1)) & here)
    send_ref[...] = dot(rows.astype(BF16), held.astype(BF16)).astype(BF16)
    comes = (((me - owner) & 7) == lane) & (lane < NZ) & to_me
    order = dot(earlier, bits(comes).astype(BF16)) - base
    fits = comes & (order >= 0.0) & (order < float(K))
    at = jnp.sum(jnp.where(fits, lane.astype(F32) * K + order + 1.0, 0.0), axis=1, keepdims=True)
    found = bits(at == iota((COLV, NZ * K), 1).astype(F32) + 1.0).astype(BF16)
    all_slots = slots_ref[0] + slots_ref[1] + slots_ref[2] + slots_ref[3]
    take_ref[...] = dot(all_slots.astype(BF16), found).astype(BF16)


def fetch_kernel(asked_ref, pieces_ref, *rest):
    out_ref, most_ref, hold, small, sems = rest[-5:]
    column = iota((COLS * NZ, ROWS), 1)
    pieces = [pieces_ref[i] for i in range(3)]
    copies = []
    for k in range(2):
        onehot = bits(asked_ref[:, k : k + 1] == column).astype(BF16)
        hold[k] = pick(onehot, pieces).reshape(COLS, 8, D)
        copies.append(
            pltpu.make_async_copy(hold.at[k], out_ref.at[:, pl.ds(k * 8, 8), :], sems.at[k])
        )
        copies[-1].start()
    most = jnp.max(asked_ref[:, 2:3].astype(F32)).astype(I32)
    small[...] = jnp.full((8, 128), most, I32)
    copies.append(pltpu.make_async_copy(small, most_ref, sems.at[2]))
    copies[-1].start()
    for copy in copies:
        copy.wait()


def send_kernel(onehot_ref, in_ref, *rest):
    outs, hold, sems = rest[-NZ - 2 : -2], rest[-2], rest[-1]
    onehot = onehot_ref[...]
    copies = []
    for c in range(2):
        cut = slice(c * D // 2, (c + 1) * D // 2)
        hold[c] = pick(onehot, split3(in_ref[:, cut]))
        for d in range(NZ):
            copies.append(
                pltpu.make_async_copy(
                    hold.at[c, pl.ds(d * K, K), :], outs[d].at[:, pl.ds(c * D // 2, D // 2)], sems.at[c, d]
                )
            )
            copies[-1].start()
    for copy in copies:
        copy.wait()


def take_kernel(onehot_ref, *rest):
    parts, out_ref, hold, sems = rest[:NZ], rest[NZ], rest[NZ + 1], rest[NZ + 2]
    onehot = onehot_ref[...]
    copies = []
    for c in range(2):
        cut = slice(c * D // 2, (c + 1) * D // 2)
        got = jnp.concatenate([p[:, cut] for p in parts], axis=0)
        hold[c] = pick(onehot, split3(got))
        copies.append(
            pltpu.make_async_copy(hold.at[c], out_ref.at[:, pl.ds(c * D // 2, D // 2)], sems.at[c])
        )
        copies[-1].start()
    for copy in copies:
        copy.wait()


def vectors_kernel(slots_ref, in_ref, out_ref):
    slots = [slots_ref[g] for g in range(GROUPS)]
    every = (slots[0] + slots[1] + slots[2] + slots[3]).astype(BF16)
    out_ref[:, :D] = pick(every, split3(in_ref[:, :D]))
    rows = jnp.zeros((SLOTS, 128), F32)
    for h in range(2):
        pieces = split3(in_ref[:, D + 128 * h : D + 128 * h + 128])
        rows = rows + jnp.where(iota((SLOTS, 128), 1) < GSIZE, pick(slots[2 * h].astype(BF16), pieces), 0.0)
        odd = pltpu.roll(pick(slots[2 * h + 1].astype(BF16), pieces), GSIZE, 1)
        rows = rows + jnp.where(iota((SLOTS, 128), 1) < GSIZE, odd, 0.0)
    out_ref[:, D:] = rows


def lookup(table, rows):
    low, high = rows & 127, rows >> 7
    found = jnp.zeros(rows.shape, F32)
    for i in range(ROWS // 128):
        part = jnp.take_along_axis(table[:, 128 * i : 128 * i + 128], low, axis=1)
        found = jnp.where(high == i, part, found)
    return found


def scores(a, pieces_ref):
    hi, mid, lo = split3(a)
    chi, cmid, clo = (pieces_ref[i] for i in range(3))
    small = dot(mid, cmid, NT) + dot(lo, chi, NT) + dot(hi, clo, NT)
    return dot(hi, chi, NT) + (dot(hi, cmid, NT) + dot(mid, chi, NT) + small)


def near_kernel(x_ref, pieces_ref, norms_ref, out_ref):
    x = x_ref[:, :D]
    rows = x_ref[:, D:].astype(I32)
    square = jnp.sum(x * x, axis=1, keepdims=True)
    table = square - 2.0 * scores(x, pieces_ref) + norms_ref[0:1, :]
    out_ref[...] = lookup(table, rows)


def loss_kernel(p_ref, x_ref, near_ref, pieces_ref, out_ref):
    x = x_ref[:, :D]
    rows = x_ref[:, D:].astype(I32)
    r = x - p_ref[...]
    rx = jnp.sum(r * x, axis=1, keepdims=True)
    rr = jnp.sum(r * r, axis=1, keepdims=True)
    gap = rx - lookup(scores(r, pieces_ref), rows)
    loss = (near_ref[...] + amplify * gap * gap / (rr + tiny)) / D
    loss = loss.reshape(COLS, 2, NZ, 128)
    second = pltpu.roll(loss[:, 1].reshape(COLS * NZ, 128), GSIZE, 1)
    first = loss[:, 0].reshape(COLS * NZ, 128)
    out_ref[...] = jnp.where(iota((COLS * NZ, 128), 1) < GSIZE, first, second)


def collect_kernel(owner_ref, in_ref, out_ref):
    lane = iota((V, 128), 1)
    hits = [owner_ref[:, g : g + 1] == lane for g in range(GROUPS)]
    rank = dot(before_same_block(V), bits(hits[0] | hits[1] | hits[2] | hits[3]).astype(BF16))
    a = in_ref[...]
    plain, rolled = split3(a), split3(pltpu.roll(a, GSIZE, 1))
    for h in range(2):
        halves = []
        for g in (2 * h, 2 * h + 1):
            first = bits(hits[g] & (rank == 0.0)).astype(BF16)
            second = bits(hits[g] & (rank == 1.0)).astype(BF16)
            if g % 2 == 0:
                halves.append(pick(first, plain) + pick(second, rolled))
            else:
                halves.append(pick(first, rolled) + pick(second, plain))
        out_ref[:, 128 * h : 128 * h + 128] = jnp.where(lane < GSIZE, halves[0], halves[1])


def swap(a, axes):
    return lax.all_to_all(a, axes, split_axis=0, concat_axis=0, tiled=True)


def shards(new_vectors, centroids, primary_owner, primary_row, cand_owner, cand_row):
    plane = ("y", "x")
    me = lax.axis_index("z").astype(I32).reshape(1)
    half = pltpu.VMEM((2, SLOTS, D // 2), F32)
    with jax.named_scope("column_info"):
        tiles = call(
            info_kernel,
            shape((NZ, 8, 128), I32),
            primary_owner.T,
            primary_row.T,
            cand_owner.T,
            name="info",
        )
        tiles = swap(tiles, "z")
    with jax.named_scope("column_vectors"):
        wide = jnp.concatenate([new_vectors, cand_row.astype(F32)], axis=1)
        column = lax.all_gather(wide, "z", axis=0, tiled=True)
    pieces, norms = call(
        prepare_kernel, [shape((3, ROWS, D), BF16), shape((8, ROWS))], centroids, name="prepare"
    )
    with jax.named_scope("requests"):
        asks, info = call(
            request_kernel,
            [shape((COLS, NZ, 128), I32), shape((COLV, 128), I32)],
            me,
            tiles,
            smem=(0,),
            name="request",
        )
        asked = swap(asks, plane).reshape(COLS * NZ, 128)
    slots = call(slots_kernel, shape((GROUPS, SLOTS, COLV)), me, info, smem=(0,), name="slots")

    def relay(turn):
        return call(
            relay_kernel,
            [shape((NZ * K, SLOTS), BF16), shape((SLOTS, NZ * K), BF16)],
            me,
            turn.reshape(1),
            info,
            slots,
            smem=(0, 1),
            name="relay",
        )

    send, take = relay(jnp.int32(0))
    with jax.named_scope("primary_rows"):
        found, most = call(
            fetch_kernel,
            [shape((COLS, 16, D)), shape((8, 128), I32)],
            asked,
            pieces,
            send,
            take,
            outside=(2, 3),
            far=True,
            scratch=[
                pltpu.VMEM((2, COLS, 8, D), F32),
                pltpu.VMEM((8, 128), I32),
                pltpu.SemaphoreType.DMA((3,)),
            ],
            name="fetch",
        )
        fetched = swap(found, plane).reshape(SLOTS, D)
        most = most[0, 0]
        most = jnp.maximum(most, lax.ppermute(most.reshape(1, 1), "rep", [(0, 1), (1, 0)])[0, 0])

    def across(send, take):
        parts = call(
            send_kernel,
            [shape((K, D))] * NZ,
            send,
            fetched,
            far=True,
            scratch=[half, pltpu.SemaphoreType.DMA((2, NZ))],
            name="send",
        )
        got = [parts[0]]
        for d in range(1, NZ):
            got.append(lax.ppermute(parts[d], "z", [(z, (z + d) % NZ) for z in range(NZ)]))
        return call(
            take_kernel,
            shape((SLOTS, D)),
            take,
            *got,
            far=True,
            scratch=[half, pltpu.SemaphoreType.DMA((2,))],
            name="take",
        )

    def more(state):
        turn, total = state
        return turn + 1, total + across(*relay(turn))

    with jax.named_scope("vectors_out"):
        vectors = call(vectors_kernel, shape((SLOTS, D + 128)), slots, column, name="vectors")
        vectors = swap(vectors.reshape(COLS, 16, D + 128), plane).reshape(SLOTS, D + 128)
    near = call(near_kernel, shape((SLOTS, 128)), vectors, pieces, norms, name="near")
    with jax.named_scope("primary_across"):
        primaries = across(send, take)
        _, primaries = lax.while_loop(lambda s: s[0] * K < most, more, (jnp.int32(1), primaries))
    with jax.named_scope("primaries_out"):
        primaries = swap(primaries.reshape(COLS, 16, D), plane).reshape(SLOTS, D)
    losses = call(loss_kernel, shape((COLS * NZ, 128)), primaries, vectors, near, pieces, name="loss")
    with jax.named_scope("losses_back"):
        back = swap(losses.reshape(COLS * NZ, 1, 128), ("y", "x", "z")).reshape(COLS * NZ, 128)
    return call(collect_kernel, shape((V, GROUPS * GSIZE)), cand_owner, back, name="collect")


def solution(mesh):
    fine = Mesh(mesh.devices.reshape(NY, NX, NZ, 2), ("y", "x", "z", "rep"))
    rows = P(("y", "x", "z", "rep"), None)
    in_specs = (rows, P(("y", "x", "z"), None), rows, rows, rows, rows)
    return jax.shard_map(shards, mesh=fine, in_specs=in_specs, out_specs=rows, check_vma=False)
```

```python
import jax
import jax.numpy as jnp
from jax import lax
from jax.experimental import pallas as pl
from jax.experimental.pallas import tpu as pltpu
from jax.sharding import Mesh, PartitionSpec as P

D = 1024
V = 32
GROUPS = 4
GSIZE = 64
ROWS = 512
NY, NX, NZ = 4, 4, 8
COLS = NY * NX
COLV = NZ * V
SLOTS = COLS * NZ * 2
SHARDS = COLS * NZ
WIDE = D + 256
K = 32
FIRST = (3, 5)
SECOND = (4, 2, 6, 1, 7)
amplify = 1.0
tiny = 1e-06

F32, BF16, I32 = jnp.float32, jnp.bfloat16, jnp.int32
VMEM = pl.BlockSpec(memory_space=pltpu.VMEM)
SMEM = pl.BlockSpec(memory_space=pltpu.SMEM)
HBM = pl.BlockSpec(memory_space=pltpu.HBM)
NN = (((1,), (0,)), ((), ()))
NT = (((1,), (1,)), ((), ()))
TN = (((0,), (0,)), ((), ()))


def call(kernel, out_shape, *operands, smem=(), far_in=(), far_out=(), scratch=(), name=None):
    specs = [SMEM if i in smem else HBM if i in far_in else VMEM for i in range(len(operands))]
    operands = [
        pltpu.with_memory_space_constraint(a, pltpu.HBM) if i in far_in else a
        for i, a in enumerate(operands)
    ]
    out_shape = [
        pltpu.HBM(o.shape, o.dtype) if i in far_out else o for i, o in enumerate(out_shape)
    ]
    return pl.pallas_call(
        kernel,
        out_shape=out_shape,
        in_specs=specs,
        out_specs=[HBM if i in far_out else VMEM for i in range(len(out_shape))],
        scratch_shapes=list(scratch),
        compiler_params=pltpu.CompilerParams(vmem_limit_bytes=24 * 2**20),
        name=name,
    )(*operands)


def copies_semaphores(n):
    return pltpu.SemaphoreType.DMA((n,))


def start_all(copies):
    for copy in copies:
        copy.start()


def wait_all(copies):
    for copy in copies:
        copy.wait()


def shape(dims, dtype=F32):
    return jax.ShapeDtypeStruct(dims, dtype)


def split3(a):
    hi = a.astype(BF16)
    rest = a - hi.astype(F32)
    mid = rest.astype(BF16)
    lo = (rest - mid.astype(F32)).astype(BF16)
    return hi, mid, lo


def dot(a, b, dims=NN):
    return lax.dot_general(a, b, dims, preferred_element_type=F32)


def pick(onehot, pieces):
    hi, mid, lo = pieces
    return dot(onehot, hi) + dot(onehot, mid) + dot(onehot, lo)


def bits(mask):
    return jnp.where(mask, 1.0, 0.0)


def iota(dims, axis):
    return lax.broadcasted_iota(I32, dims, axis)


def before_same_block(rows):
    u, w = iota((rows, rows), 0), iota((rows, rows), 1)
    return bits((w < u) & ((u >> 5) == (w >> 5))).astype(BF16)


def before_all(rows):
    return bits(iota((rows, rows), 1) < iota((rows, rows), 0)).astype(BF16)


def prepare_kernel(c_ref, pieces_ref, norms_ref):
    c = c_ref[...]
    for i, piece in enumerate(split3(c)):
        pieces_ref[i] = piece
    squares = split3(c * c)
    ones = jnp.ones((8, D), BF16)
    norms_ref[...] = sum(dot(ones, s, NT) for s in squares)


def request_kernel(owner_ref, row_ref, cand_ref, out_ref, owner, row, cand, hold, sems):
    copies = [
        pltpu.make_async_copy(owner_ref, owner, sems.at[0]),
        pltpu.make_async_copy(row_ref, row, sems.at[1]),
        pltpu.make_async_copy(cand_ref, cand, sems.at[2]),
    ]
    start_all(copies)
    shard = iota((SHARDS, V), 0)
    earlier = bits(iota((V, V), 0) < iota((V, V), 1)).astype(BF16)
    lane = iota((SHARDS, 128), 1)
    wait_all(copies)
    hit = owner[...] == shard
    rank = dot(bits(hit).astype(BF16), earlier)
    rows = row[...].astype(F32)
    asks = [
        jnp.sum(jnp.where(hit & (rank == float(k)), rows, 0.0), axis=1, keepdims=True)
        for k in range(2)
    ]
    asks = jnp.where(lane == 0, asks[0], jnp.where(lane == 1, asks[1], 0.0)).astype(I32)
    empty = jnp.zeros((1, V), I32)
    owners = jnp.concatenate([empty, owner[...], empty, empty], axis=1)
    hold[pl.ds(0, SHARDS, stride=2), :] = asks + owners
    cands = jnp.concatenate([cand[g : g + 1, :] for g in range(GROUPS)], axis=1)
    hold[pl.ds(1, SHARDS, stride=2), :] = jnp.broadcast_to(cands, (SHARDS, 128))
    copy = pltpu.make_async_copy(hold, out_ref, sems.at[3])
    copy.start()
    copy.wait()


def wide_kernel(x_ref, rows_ref, asks_ref, out_ref, x, rows, wide, sems):
    copies = [
        pltpu.make_async_copy(x_ref, x, sems.at[0]),
        pltpu.make_async_copy(rows_ref, rows, sems.at[1]),
    ]
    start_all(copies)
    wait_all(copies)
    wide[:, :D] = x[...]
    wide[:, D:] = rows[...].astype(F32)
    copy = pltpu.make_async_copy(wide, out_ref, sems.at[2])
    copy.start()
    copy.wait()


def slots_kernel(me_ref, asked_ref, found_ref, info_ref, slots_ref):
    me, column = me_ref[0], me_ref[1]
    at = pl.multiple_of(column * NZ * 2, NZ * 2)
    tile = asked_ref[pl.ds(at, NZ * 2), :]
    turned = jnp.concatenate([tile, jnp.zeros((128 - NZ * 2, 128), I32)], axis=0).T
    block_lane = iota((V, 128), 1)
    for z in range(NZ):
        block = jnp.where(block_lane == 0, turned[V : 2 * V, 2 * z : 2 * z + 1], 0)
        for g in range(GROUPS):
            cand = turned[g * V : (g + 1) * V, 2 * z + 1 : 2 * z + 2]
            block = jnp.where(block_lane == 1 + g, cand, block)
        info_ref[z * V : (z + 1) * V, :] = block
    lane = iota((COLV, 128), 1)
    hits = []
    for g in range(GROUPS):
        owner = info_ref[:, 1 + g : 2 + g]
        hits.append((owner == lane * NZ + me) & (lane < COLS))
    any_hit = bits(hits[0] | hits[1] | hits[2] | hits[3])
    rank = dot(before_same_block(COLV), any_hit.astype(BF16))
    mine = (iota((NZ, COLV), 1) >> 5) == iota((NZ, COLV), 0)
    for g in range(GROUPS):
        for k in range(2):
            turned = bits(hits[g] & (rank == float(k))).T
            for b in range(COLS):
                part = jnp.where(mine, turned[b : b + 1, :], 0.0)
                slots_ref[g, b * 16 + k * 8 : b * 16 + k * 8 + 8, :] = part


def relay_kernel(me_ref, turn_ref, info_ref, slots_ref, send_ref, take_ref):
    me = me_ref[0]
    base = (turn_ref[0] * K).astype(F32)
    lane = iota((COLV, 128), 1)
    u = iota((COLV, 1), 0)
    info = info_ref[...]
    owner = info[:, 0:1]
    hits = bits((owner == lane * NZ + me) & (lane < COLS))
    rank = dot(before_same_block(COLV), hits.astype(BF16))
    rank = jnp.sum(rank * hits, axis=1, keepdims=True)
    here = (owner & 7) == me
    wanted = lane < 0
    to_me = u < 0
    for g in range(GROUPS):
        plane = info[:, 1 + g : 2 + g] & 7
        wanted = wanted | (plane == lane)
        to_me = to_me | (plane == me)
    earlier = before_all(COLV)
    leaves = wanted & (lane < NZ) & here
    order = dot(earlier, bits(leaves).astype(BF16))
    place = jnp.where(leaves, order - base, -1.0).T
    depth = iota((K, COLV), 0).astype(F32)
    rows = jnp.concatenate([bits(place[z : z + 1, :] == depth) for z in range(NZ)], axis=0)
    slot = (owner >> 3) * 16 + rank.astype(I32) * 8 + (u >> 5)
    held = bits((slot == iota((COLV, SLOTS), 1)) & here)
    send_ref[...] = dot(rows.astype(BF16), held.astype(BF16)).astype(BF16)
    comes = ((owner & 7) == lane) & (lane < NZ) & to_me
    order = dot(earlier, bits(comes).astype(BF16)) - base
    fits = comes & (order >= 0.0) & (order < float(K))
    at = jnp.sum(jnp.where(fits, lane.astype(F32) * K + order + 1.0, 0.0), axis=1, keepdims=True)
    found = bits(at == iota((COLV, NZ * K), 1).astype(F32) + 1.0).astype(BF16)
    all_slots = slots_ref[0] + slots_ref[1] + slots_ref[2] + slots_ref[3]
    take_ref[...] = dot(all_slots.astype(BF16), found).astype(BF16)


def fetch_kernel(asked_ref, pieces_ref, *rest):
    out_ref, hold, sems = rest[-3:]
    column = iota((SHARDS, ROWS), 1)
    asked = asked_ref[pl.ds(0, SHARDS, stride=2), :]
    pieces = [pieces_ref[i] for i in range(3)]
    copies = []
    for k in range(2):
        onehot = bits(asked[:, k : k + 1] == column).astype(BF16)
        hold[k] = pick(onehot, pieces).reshape(COLS, 8, D)
        copies.append(
            pltpu.make_async_copy(hold.at[k], out_ref.at[:, pl.ds(k * 8, 8), :], sems.at[k])
        )
        copies[-1].start()
    wait_all(copies)


CUTS = 4
WIDTH = D // CUTS


def move_kernel(onehot_ref, in_ref, *rest):
    out_ref, got, hold, in_sems, out_sems = rest[-5:]

    def cut(ref, c):
        return ref.at[:, pl.ds(c * WIDTH, WIDTH)]

    ins = [pltpu.make_async_copy(cut(in_ref, c), got.at[c], in_sems.at[c]) for c in range(CUTS)]
    outs = [pltpu.make_async_copy(hold.at[c], cut(out_ref, c), out_sems.at[c]) for c in range(CUTS)]
    start_all(ins)
    onehot = onehot_ref[...]
    for c in range(CUTS):
        ins[c].wait()
        hold[c] = pick(onehot, split3(got[c]))
        outs[c].start()
    wait_all(outs)


def vectors_kernel(here_ref, me_ref, slots_ref, info_ref, *rest):
    parts, outs, column_ref, hold, sems = rest[:NZ], rest[-COLS - 3 : -3], rest[-3], rest[-2], rest[-1]
    y, x, me = here_ref[0], here_ref[1], me_ref[0]
    copies = []
    for d in range(NZ):
        at = pl.multiple_of(((me - d) & 7) * V, V)
        copies.append(
            pltpu.make_async_copy(parts[d], column_ref.at[pl.ds(at, V), :], sems.at[d])
        )
    start_all(copies)
    wait_all(copies)
    slots = [slots_ref[g] for g in range(GROUPS)]
    every = (slots[0] + slots[1] + slots[2] + slots[3]).astype(BF16)
    hold[:, :D] = pick(every, split3(column_ref[:, :D]))
    lane = iota((SLOTS, 128), 1)
    rows = jnp.zeros((SLOTS, 128), F32)
    for h in range(2):
        pieces = split3(column_ref[:, D + 128 * h : D + 128 * h + 128])
        even = pick(slots[2 * h].astype(BF16), pieces)
        odd = pltpu.roll(pick(slots[2 * h + 1].astype(BF16), pieces), GSIZE, 1)
        rows = rows + even_lanes(even) + even_lanes(odd)
    info = info_ref[...]
    plane_from = bits(((info[:, 0:1] & 7) == lane) & (lane < NZ)).astype(BF16)
    wanted = lane < 0
    for g in range(GROUPS):
        wanted = wanted | ((info[:, 1 + g : 2 + g] & 7) == lane)
    plane_to = bits(wanted & (lane < NZ)).astype(BF16)
    most = jnp.max(dot(plane_from, plane_to, TN))
    hold[:, D:] = jnp.where(lane < GSIZE, rows, most)
    copies = []
    for d in range(COLS):
        there = ((y + d // NX) & (NY - 1)) * NX + ((x + d % NX) & (NX - 1))
        at = pl.multiple_of(there * 16, 16)
        copies.append(pltpu.make_async_copy(hold.at[pl.ds(at, 16), :], outs[d], sems.at[d]))
    start_all(copies)
    wait_all(copies)


def even_lanes(a):
    return jnp.where(iota(a.shape, 1) < GSIZE, a, 0.0)


def merge_kernel(here_ref, *rest):
    parts, out_ref, most_ref, sems = rest[:COLS], rest[-3], rest[-2], rest[-1]
    y, x = here_ref[0], here_ref[1]
    copies = []
    for d in range(COLS):
        there = ((y - d // NX) & (NY - 1)) * NX + ((x - d % NX) & (NX - 1))
        at = pl.multiple_of(there * 16, 16)
        copies.append(pltpu.make_async_copy(parts[d], out_ref.at[pl.ds(at, 16), :], sems.at[d]))
    start_all(copies)
    wait_all(copies)
    most = jnp.max(out_ref[:, D + GSIZE : D + 128])
    most_ref[...] = jnp.full((8, 128), most, F32).astype(I32)


def lookup(table, rows):
    low, high = rows & 127, rows >> 7
    found = jnp.zeros(rows.shape, F32)
    for i in range(ROWS // 128):
        part = jnp.take_along_axis(table[:, 128 * i : 128 * i + 128], low, axis=1)
        found = jnp.where(high == i, part, found)
    return found


def scores(a, pieces_ref):
    hi, mid, lo = split3(a)
    chi, cmid, clo = (pieces_ref[i] for i in range(3))
    small = dot(mid, cmid, NT) + dot(lo, chi, NT) + dot(hi, clo, NT)
    return dot(hi, chi, NT) + (dot(hi, cmid, NT) + dot(mid, chi, NT) + small)


def near_kernel(x_ref, pieces_ref, norms_ref, out_ref):
    x = x_ref[:, :D]
    rows = x_ref[:, D:].astype(I32) & (ROWS - 1)
    square = jnp.sum(x * x, axis=1, keepdims=True)
    table = square - 2.0 * scores(x, pieces_ref) + norms_ref[0:1, :]
    out_ref[...] = lookup(table, rows)


def loss_kernel(p_ref, x_ref, near_ref, pieces_ref, out_ref, got, sems):
    ins = [
        pltpu.make_async_copy(p_ref.at[:, pl.ds(c * WIDTH, WIDTH)], got.at[c], sems.at[c])
        for c in range(CUTS)
    ]
    start_all(ins)
    rows = x_ref[:, D:].astype(I32) & (ROWS - 1)
    rx, rr, table = 0.0, 0.0, 0.0
    for c in range(CUTS):
        at = slice(c * WIDTH, (c + 1) * WIDTH)
        ins[c].wait()
        x = x_ref[:, at]
        r = x - got[c]
        rx = rx + jnp.sum(r * x, axis=1, keepdims=True)
        rr = rr + jnp.sum(r * r, axis=1, keepdims=True)
        hi = r.astype(BF16)
        mid = (r - hi.astype(F32)).astype(BF16)
        chi, cmid = pieces_ref[0, :, at], pieces_ref[1, :, at]
        table = table + (dot(hi, chi, NT) + (dot(hi, cmid, NT) + dot(mid, chi, NT)))
    gap = rx - lookup(table, rows)
    loss = (near_ref[...] + amplify * gap * gap / (rr + tiny)) / D
    loss = loss.reshape(COLS, 2, NZ, 128)
    second = pltpu.roll(loss[:, 1].reshape(COLS * NZ, 128), GSIZE, 1)
    first = loss[:, 0].reshape(COLS * NZ, 128)
    out_ref[...] = jnp.where(iota((COLS * NZ, 128), 1) < GSIZE, first, second)


def collect_kernel(owner_ref, in_ref, out_ref):
    lane = iota((V, 128), 1)
    hits = [owner_ref[:, g : g + 1] == lane for g in range(GROUPS)]
    rank = dot(before_same_block(V), bits(hits[0] | hits[1] | hits[2] | hits[3]).astype(BF16))
    a = in_ref[...]
    plain, rolled = split3(a), split3(pltpu.roll(a, GSIZE, 1))
    for h in range(2):
        halves = []
        for g in (2 * h, 2 * h + 1):
            first = bits(hits[g] & (rank == 0.0)).astype(BF16)
            second = bits(hits[g] & (rank == 1.0)).astype(BF16)
            if g % 2 == 0:
                halves.append(pick(first, plain) + pick(second, rolled))
            else:
                halves.append(pick(first, rolled) + pick(second, plain))
        out_ref[:, 128 * h : 128 * h + 128] = jnp.where(lane < GSIZE, halves[0], halves[1])


def swap(a, axes):
    return lax.all_to_all(a, axes, split_axis=0, concat_axis=0, tiled=True)


def shards(new_vectors, centroids, primary_owner, primary_row, cand_owner, cand_row):
    plane = ("y", "x")
    z, y, x = (lax.axis_index(n).astype(I32) for n in ("z", "y", "x"))
    me = jnp.stack([z, y * NX + x])
    here = jnp.stack([y, x])
    with jax.named_scope("requests"):
        [asks] = call(
            request_kernel,
            [shape((2 * SHARDS, 128), I32)],
            primary_owner.T,
            primary_row.T,
            cand_owner.T,
            far_in=(0, 1, 2),
            far_out=(0,),
            scratch=[
                pltpu.VMEM((1, V), I32),
                pltpu.VMEM((1, V), I32),
                pltpu.VMEM((GROUPS, V), I32),
                pltpu.VMEM((2 * SHARDS, 128), I32),
                copies_semaphores(4),
            ],
            name="request",
        )
        asked = swap(asks.reshape(SHARDS, 2, 128), ("y", "x", "z")).reshape(2 * SHARDS, 128)
    with jax.named_scope("column_vectors"):
        [wide] = call(
            wide_kernel,
            [shape((V, WIDE))],
            new_vectors,
            cand_row,
            asks,
            far_in=(0, 1, 2),
            far_out=(0,),
            scratch=[
                pltpu.VMEM((V, D), F32),
                pltpu.VMEM((V, 256), I32),
                pltpu.VMEM((V, WIDE), F32),
                copies_semaphores(3),
            ],
            name="wide",
        )
        columns = [wide]
        for d in range(1, NZ):
            columns.append(lax.ppermute(wide, "z", [(z, (z + d) % NZ) for z in range(NZ)]))
        first = [columns[d] for d in FIRST]
        second = [columns[d] for d in SECOND]
    pieces, norms = call(
        prepare_kernel, [shape((3, ROWS, D), BF16), shape((8, ROWS))], centroids, name="prepare"
    )
    with jax.named_scope("primary_rows"):
        [found] = call(
            fetch_kernel,
            [shape((COLS, 16, D))],
            asked,
            pieces,
            *first,
            far_in=tuple(range(2, 2 + len(first))),
            far_out=(0,),
            scratch=[pltpu.VMEM((2, COLS, 8, D), F32), copies_semaphores(2)],
            name="fetch",
        )
        fetched = swap(found, plane).reshape(SLOTS, D)
    info, slots = call(
        slots_kernel,
        [shape((COLV, 128), I32), shape((GROUPS, SLOTS, COLV))],
        me,
        asked,
        found,
        smem=(0,),
        far_in=(2,),
        name="slots",
    )

    def relay(turn):
        return call(
            relay_kernel,
            [shape((NZ * K, SLOTS), BF16), shape((SLOTS, NZ * K), BF16)],
            me,
            turn.reshape(1),
            info,
            slots,
            smem=(0, 1),
            name="relay",
        )

    def move(onehot, source, name, after=()):
        [moved] = call(
            move_kernel,
            [shape((SLOTS, D))],
            onehot,
            source,
            *after,
            far_in=tuple(range(1, 2 + len(after))),
            far_out=(0,),
            scratch=[
                pltpu.VMEM((CUTS, SLOTS, WIDTH), F32),
                pltpu.VMEM((CUTS, SLOTS, WIDTH), F32),
                copies_semaphores(CUTS),
                copies_semaphores(CUTS),
            ],
            name=name,
        )
        return moved

    send, take = relay(jnp.int32(0))
    with jax.named_scope("primary_across"):
        leaving = move(send, fetched, "send", after=second)
        got = swap(leaving.reshape(NZ, K, D), "z").reshape(NZ * K, D)
    with jax.named_scope("vectors_out"):
        parts = call(
            vectors_kernel,
            [shape((16, D + 128))] * COLS,
            here,
            me,
            slots,
            info,
            *columns,
            leaving,
            smem=(0, 1),
            far_in=tuple(range(4, NZ + 5)),
            far_out=tuple(range(COLS)),
            scratch=[
                pltpu.VMEM((COLV, WIDE), F32),
                pltpu.VMEM((SLOTS, D + 128), F32),
                copies_semaphores(COLS),
            ],
            name="vectors",
        )
        arrived = [parts[0]]
        for d in range(1, COLS):
            dy, dx = d // NX, d % NX
            pairs = [
                (y * NX + x, (y + dy) % NY * NX + (x + dx) % NX) for y in range(NY) for x in range(NX)
            ]
            arrived.append(lax.ppermute(parts[d], plane, pairs))
        vectors, most = call(
            merge_kernel,
            [shape((SLOTS, D + 128)), shape((8, 128), I32)],
            here,
            *arrived,
            smem=(0,),
            far_in=tuple(range(1, COLS + 1)),
            scratch=[copies_semaphores(COLS)],
            name="merge",
        )
        most = most[:1, :1]
        most = jnp.maximum(most, lax.ppermute(most, "rep", [(0, 1), (1, 0)]))[0, 0]
    with jax.named_scope("primary_across"):
        primaries = move(take, got, "take")

        def more(state):
            turn, total = state
            send, take = relay(turn)
            leaving = move(send, fetched, "send")
            got = swap(leaving.reshape(NZ, K, D), "z").reshape(NZ * K, D)
            return turn + 1, total + move(take, got, "take")

        _, primaries = lax.while_loop(lambda s: s[0] * K < most, more, (jnp.int32(1), primaries))
    [near] = call(near_kernel, [shape((SLOTS, 128))], vectors, pieces, norms, name="near")
    with jax.named_scope("primaries_out"):
        primaries = swap(primaries.reshape(COLS, 16, D), plane).reshape(SLOTS, D)
    [losses] = call(
        loss_kernel,
        [shape((SHARDS, 128))],
        primaries,
        vectors,
        near,
        pieces,
        far_in=(0,),
        scratch=[pltpu.VMEM((CUTS, SLOTS, WIDTH), F32), copies_semaphores(CUTS)],
        name="loss",
    )
    with jax.named_scope("losses_back"):
        back = swap(losses.reshape(SHARDS, 1, 128), ("y", "x", "z")).reshape(SHARDS, 128)
    [result] = call(
        collect_kernel, [shape((V, GROUPS * GSIZE))], cand_owner, back, name="collect"
    )
    return result


def solution(mesh):
    fine = Mesh(mesh.devices.reshape(NY, NX, NZ, 2), ("y", "x", "z", "rep"))
    rows = P(("y", "x", "z", "rep"), None)
    in_specs = (rows, P(("y", "x", "z"), None), rows, rows, rows, rows)
    return jax.shard_map(shards, mesh=fine, in_specs=in_specs, out_specs=rows, check_vma=False)
```

```python
import jax
import jax.numpy as jnp
from jax import lax
from jax.experimental import pallas as pl
from jax.experimental.pallas import tpu as pltpu
from jax.sharding import Mesh, PartitionSpec as P

D = 1024
V = 32
GROUPS = 4
GSIZE = 64
ROWS = 512
NY, NX, NZ = 4, 4, 8
COLS = NY * NX
COLV = NZ * V
SLOTS = COLS * NZ * 2
SHARDS = COLS * NZ
K = 32
PER = 19
amplify = 1.0
tiny = 1e-06

F32, BF16, I32 = jnp.float32, jnp.bfloat16, jnp.int32
VMEM = pl.BlockSpec(memory_space=pltpu.VMEM)
SMEM = pl.BlockSpec(memory_space=pltpu.SMEM)
HBM = pl.BlockSpec(memory_space=pltpu.HBM)
NN = (((1,), (0,)), ((), ()))
NT = (((1,), (1,)), ((), ()))
TN = (((0,), (0,)), ((), ()))


def call(kernel, out_shape, *operands, smem=(), far_in=(), far_out=(), scratch=(), name=None):
    specs = [SMEM if i in smem else HBM if i in far_in else VMEM for i in range(len(operands))]
    operands = [
        pltpu.with_memory_space_constraint(a, pltpu.HBM) if i in far_in else a
        for i, a in enumerate(operands)
    ]
    out_shape = [
        pltpu.HBM(o.shape, o.dtype) if i in far_out else o for i, o in enumerate(out_shape)
    ]
    return pl.pallas_call(
        kernel,
        out_shape=out_shape,
        in_specs=specs,
        out_specs=[HBM if i in far_out else VMEM for i in range(len(out_shape))],
        scratch_shapes=list(scratch),
        compiler_params=pltpu.CompilerParams(vmem_limit_bytes=24 * 2**20),
        name=name,
    )(*operands)


def copies_semaphores(n):
    return pltpu.SemaphoreType.DMA((n,))


def start_all(copies):
    for copy in copies:
        copy.start()


def wait_all(copies):
    for copy in copies:
        copy.wait()


def shape(dims, dtype=F32):
    return jax.ShapeDtypeStruct(dims, dtype)


def split3(a):
    hi = a.astype(BF16)
    rest = a - hi.astype(F32)
    mid = rest.astype(BF16)
    lo = (rest - mid.astype(F32)).astype(BF16)
    return hi, mid, lo


def dot(a, b, dims=NN):
    return lax.dot_general(a, b, dims, preferred_element_type=F32)


def pick(onehot, pieces):
    hi, mid, lo = pieces
    return dot(onehot, hi) + dot(onehot, mid) + dot(onehot, lo)


def bits(mask):
    return jnp.where(mask, 1.0, 0.0)


def iota(dims, axis):
    return lax.broadcasted_iota(I32, dims, axis)


def before_same_block(rows):
    u, w = iota((rows, rows), 0), iota((rows, rows), 1)
    return bits((w < u) & ((u >> 5) == (w >> 5))).astype(BF16)


def before_all(rows):
    return bits(iota((rows, rows), 1) < iota((rows, rows), 0)).astype(BF16)


def prepare_kernel(c_ref, pieces_ref, norms_ref):
    c = c_ref[...]
    for i, piece in enumerate(split3(c)):
        pieces_ref[i] = piece
    squares = split3(c * c)
    ones = jnp.ones((8, D), BF16)
    norms_ref[...] = sum(dot(ones, s, NT) for s in squares)


def request_kernel(owner_ref, row_ref, cand_ref, x_ref, rows_ref, out_ref, owner, row, cand, x, rows, hold, sems):
    copies = [
        pltpu.make_async_copy(a, b, sems.at[i])
        for i, (a, b) in enumerate(
            [(owner_ref, owner), (row_ref, row), (cand_ref, cand), (x_ref, x), (rows_ref, rows)]
        )
    ]
    start_all(copies)
    shard = iota((SHARDS, V), 0)
    earlier = bits(iota((V, V), 0) < iota((V, V), 1)).astype(BF16)
    lane = iota((SHARDS, 128), 1)
    wait_all(copies)
    hit = owner[...] == shard
    rank = dot(bits(hit).astype(BF16), earlier)
    asked = row[...].astype(F32)
    asks = [
        jnp.sum(jnp.where(hit & (rank == float(k)), asked, 0.0), axis=1, keepdims=True)
        for k in range(2)
    ]
    empty = jnp.zeros((1, V), I32)
    owners = jnp.concatenate([empty, owner[...], empty, empty], axis=1).astype(F32)
    line = jnp.where(lane == 0, asks[0], jnp.where(lane == 1, asks[1], 0.0)) + owners
    hold[pl.ds(17, SHARDS, stride=PER), :] = line
    line = jnp.concatenate([cand[g : g + 1, :] for g in range(GROUPS)], axis=1).astype(F32)
    hold[pl.ds(18, SHARDS, stride=PER), :] = jnp.broadcast_to(line, (SHARDS, 128))
    hits = [cand[g : g + 1, :] == shard for g in range(GROUPS)]
    any_hit = hits[0] | hits[1] | hits[2] | hits[3]
    rank = dot(bits(any_hit).astype(BF16), earlier)
    wide = [split3(rows[:, 128 * h : 128 * h + 128].astype(F32))[:2] for h in range(2)]
    lines = []
    for k in range(2):
        sides = [jnp.zeros((SHARDS, 128), F32)] * 2
        for g in range(GROUPS):
            onehot = bits(hits[g] & (rank == float(k))).astype(BF16)
            sides[g % 2] = sides[g % 2] + dot(onehot, wide[g // 2][0]) + dot(onehot, wide[g // 2][1])
        sides[1 - k] = pltpu.roll(sides[1 - k], GSIZE, 1)
        side = even_lanes if k == 0 else odd_lanes
        lines.append(side(sides[0]) + side(sides[1]))
    hold[pl.ds(16, SHARDS, stride=PER), :] = lines[0] + lines[1]
    pieces = split3(x[...])
    for k in range(2):
        sent = pick(bits(any_hit & (rank == float(k))).astype(BF16), pieces)
        for j in range(8):
            hold[pl.ds(8 * k + j, SHARDS, stride=PER), :] = sent[:, 128 * j : 128 * j + 128]
    copy = pltpu.make_async_copy(hold, out_ref, sems.at[5])
    copy.start()
    copy.wait()


def even_lanes(a):
    return jnp.where(iota(a.shape, 1) < GSIZE, a, 0.0)


def odd_lanes(a):
    return jnp.where(iota(a.shape, 1) < GSIZE, 0.0, a)


def slots_kernel(me_ref, got_ref, found_ref, info_ref, slots_ref, most_ref, hold):
    me, column = me_ref[0], me_ref[1]
    owners = got_ref[pl.ds(17, SHARDS, stride=PER), :].astype(I32)
    cands = got_ref[pl.ds(18, SHARDS, stride=PER), :].astype(I32)
    hold[0] = owners
    hold[1] = cands
    at = pl.multiple_of(column * NZ, NZ)
    tile = jnp.concatenate([hold[0, pl.ds(at, NZ), :], hold[1, pl.ds(at, NZ), :]], axis=0)
    turned = jnp.concatenate([tile, jnp.zeros((128 - NZ * 2, 128), I32)], axis=0).T
    block_lane = iota((V, 128), 1)
    for z in range(NZ):
        block = jnp.where(block_lane == 0, turned[V : 2 * V, z : z + 1], 0)
        for g in range(GROUPS):
            cand = turned[g * V : (g + 1) * V, NZ + z : NZ + z + 1]
            block = jnp.where(block_lane == 1 + g, cand, block)
        info_ref[z * V : (z + 1) * V, :] = block
    lane = iota((COLV, 128), 1)
    hit = lane < 0
    for g in range(GROUPS):
        hit = hit | (info_ref[:, 1 + g : 2 + g] == lane * NZ + me)
    hit = hit & (lane < COLS)
    rank = dot(before_same_block(COLV), bits(hit).astype(BF16))
    mine = (iota((NZ, COLV), 1) >> 5) == iota((NZ, COLV), 0)
    for k in range(2):
        turned = bits(hit & (rank == float(k))).T
        for b in range(COLS):
            part = jnp.where(mine, turned[b : b + 1, :], 0.0)
            slots_ref[b * 16 + k * 8 : b * 16 + k * 8 + 8, :] = part
    lane = iota((SHARDS, 128), 1)
    owners = jnp.where((lane >= V) & (lane < 2 * V), owners, 0)
    owners = owners + pltpu.roll(owners, 2 * V, 1)
    owners = (owners + pltpu.roll(owners, V, 1)) & 7
    parts = []
    for b in range(NZ):
        to_plane = bits((cands & 7) == b)
        to_plane = jnp.maximum(to_plane, pltpu.roll(to_plane, 2 * V, 1))
        to_plane = jnp.maximum(to_plane, pltpu.roll(to_plane, V, 1))
        for h in range(2):
            parts.append(jnp.where(owners == (lane >> 5) + 4 * h, to_plane, 0.0).astype(BF16))
    columns = bits((iota((COLS, SHARDS), 1) >> 3) == iota((COLS, SHARDS), 0)).astype(BF16)
    group = bits((iota((128, 128), 0) >> 5) == iota((128, 128), 1)).astype(BF16)
    most = 0.0
    for part in parts:
        most = jnp.maximum(most, jnp.max(dot(dot(columns, part).astype(BF16), group)))
    most_ref[...] = jnp.full((8, 128), most, F32).astype(I32)


def relay_kernel(me_ref, turn_ref, info_ref, slots_ref, send_ref, take_ref):
    me = me_ref[0]
    base = (turn_ref[0] * K).astype(F32)
    lane = iota((COLV, 128), 1)
    u = iota((COLV, 1), 0)
    info = info_ref[...]
    owner = info[:, 0:1]
    hits = bits((owner == lane * NZ + me) & (lane < COLS))
    rank = dot(before_same_block(COLV), hits.astype(BF16))
    rank = jnp.sum(rank * hits, axis=1, keepdims=True)
    here = (owner & 7) == me
    wanted = lane < 0
    to_me = u < 0
    for g in range(GROUPS):
        plane = info[:, 1 + g : 2 + g] & 7
        wanted = wanted | (plane == lane)
        to_me = to_me | (plane == me)
    earlier = before_all(COLV)
    leaves = wanted & (lane < NZ) & here
    order = dot(earlier, bits(leaves).astype(BF16))
    place = jnp.where(leaves, order - base, -1.0).T
    depth = iota((K, COLV), 0).astype(F32)
    rows = jnp.concatenate([bits(place[z : z + 1, :] == depth) for z in range(NZ)], axis=0)
    slot = (owner >> 3) * 16 + rank.astype(I32) * 8 + (u >> 5)
    held = bits((slot == iota((COLV, SLOTS), 1)) & here)
    send_ref[...] = dot(rows.astype(BF16), held.astype(BF16)).astype(BF16)
    comes = ((owner & 7) == lane) & (lane < NZ) & to_me
    order = dot(earlier, bits(comes).astype(BF16)) - base
    fits = comes & (order >= 0.0) & (order < float(K))
    at = jnp.sum(jnp.where(fits, lane.astype(F32) * K + order + 1.0, 0.0), axis=1, keepdims=True)
    found = bits(at == iota((COLV, NZ * K), 1).astype(F32) + 1.0).astype(BF16)
    take_ref[...] = dot(slots_ref[...].astype(BF16), found).astype(BF16)


def fetch_kernel(got_ref, pieces_ref, out_ref, hold, sems):
    column = iota((SHARDS, ROWS), 1)
    asked = got_ref[pl.ds(17, SHARDS, stride=PER), :].astype(I32)
    pieces = [pieces_ref[i] for i in range(3)]
    copies = []
    for k in range(2):
        onehot = bits(asked[:, k : k + 1] == column).astype(BF16)
        hold[k] = pick(onehot, pieces).reshape(COLS, 8, D)
        copies.append(
            pltpu.make_async_copy(hold.at[k], out_ref.at[:, pl.ds(k * 8, 8), :], sems.at[k])
        )
        copies[-1].start()
    wait_all(copies)


def move_kernel(onehot_ref, in_ref, out_ref, hold, sems):
    pieces = split3(in_ref[...])
    half = SLOTS // 2
    copies = []
    for c in range(2):
        hold[c] = pick(onehot_ref[c * half : (c + 1) * half, :], pieces)
        copies.append(
            pltpu.make_async_copy(hold.at[c], out_ref.at[pl.ds(c * half, half), :], sems.at[c])
        )
        copies[-1].start()
    wait_all(copies)


def lookup(table, rows):
    low, high = rows & 127, rows >> 7
    found = jnp.zeros(rows.shape, F32)
    for i in range(ROWS // 128):
        part = jnp.take_along_axis(table[:, 128 * i : 128 * i + 128], low, axis=1)
        found = jnp.where(high == i, part, found)
    return found


def scores(a, pieces_ref):
    hi, mid, lo = split3(a)
    chi, cmid, clo = (pieces_ref[i] for i in range(3))
    small = dot(mid, cmid, NT) + dot(lo, chi, NT) + dot(hi, clo, NT)
    return dot(hi, chi, NT) + (dot(hi, cmid, NT) + dot(mid, chi, NT) + small)


def near_kernel(got_ref, pieces_ref, norms_ref, x_ref, rows_ref, out_ref):
    line = got_ref[pl.ds(16, SHARDS, stride=PER), :]
    for k in range(2):
        at = slice(8 * k, 8 * k + 8)
        for j in range(8):
            part = got_ref[pl.ds(8 * k + j, SHARDS, stride=PER), :]
            x_ref[:, at, 128 * j : 128 * j + 128] = part.reshape(COLS, 8, 128)
        rows_ref[:, at, :] = line.astype(I32).reshape(COLS, 8, 128)
        line = pltpu.roll(line, GSIZE, 1)
    x = x_ref[...].reshape(SLOTS, D)
    square = jnp.sum(x * x, axis=1, keepdims=True)
    table = square - 2.0 * scores(x, pieces_ref) + norms_ref[0:1, :]
    out_ref[...] = lookup(table, rows_ref[...].reshape(SLOTS, 128))


def loss_kernel(p_ref, x_ref, rows_ref, near_ref, pieces_ref, out_ref):
    x = x_ref[...].reshape(SLOTS, D)
    rows = rows_ref[...].reshape(SLOTS, 128)
    r = x - p_ref[...]
    hi = r.astype(BF16)
    mid = (r - hi.astype(F32)).astype(BF16)
    chi, cmid = pieces_ref[0], pieces_ref[1]
    table = dot(hi, chi, NT) + (dot(hi, cmid, NT) + dot(mid, chi, NT))
    rx = jnp.sum(r * x, axis=1, keepdims=True)
    rr = jnp.sum(r * r, axis=1, keepdims=True)
    gap = rx - lookup(table, rows)
    loss = (near_ref[...] + amplify * gap * gap / (rr + tiny)) / D
    loss = loss.reshape(COLS, 2, NZ, 128)
    second = pltpu.roll(loss[:, 1].reshape(COLS * NZ, 128), GSIZE, 1)
    first = loss[:, 0].reshape(COLS * NZ, 128)
    out_ref[...] = jnp.where(iota((COLS * NZ, 128), 1) < GSIZE, first, second)


def collect_kernel(owner_ref, in_ref, out_ref):
    lane = iota((V, 128), 1)
    hits = [owner_ref[:, g : g + 1] == lane for g in range(GROUPS)]
    rank = dot(before_same_block(V), bits(hits[0] | hits[1] | hits[2] | hits[3]).astype(BF16))
    a = in_ref[...]
    plain, rolled = split3(a), split3(pltpu.roll(a, GSIZE, 1))
    for h in range(2):
        halves = []
        for g in (2 * h, 2 * h + 1):
            first = bits(hits[g] & (rank == 0.0)).astype(BF16)
            second = bits(hits[g] & (rank == 1.0)).astype(BF16)
            if g % 2 == 0:
                halves.append(pick(first, plain) + pick(second, rolled))
            else:
                halves.append(pick(first, rolled) + pick(second, plain))
        out_ref[:, 128 * h : 128 * h + 128] = jnp.where(lane < GSIZE, halves[0], halves[1])


def swap(a, axes):
    return lax.all_to_all(a, axes, split_axis=0, concat_axis=0, tiled=True)


def shards(new_vectors, centroids, primary_owner, primary_row, cand_owner, cand_row):
    plane = ("y", "x")
    column = lax.axis_index(("y", "x")).astype(I32)
    me = jnp.stack([lax.axis_index("z").astype(I32), column])
    with jax.named_scope("requests_and_vectors"):
        [sent] = call(
            request_kernel,
            [shape((PER * SHARDS, 128))],
            primary_owner.T,
            primary_row.T,
            cand_owner.T,
            new_vectors,
            cand_row,
            far_in=(0, 1, 2, 3, 4),
            far_out=(0,),
            scratch=[
                pltpu.VMEM((1, V), I32),
                pltpu.VMEM((1, V), I32),
                pltpu.VMEM((GROUPS, V), I32),
                pltpu.VMEM((V, D), F32),
                pltpu.VMEM((V, GROUPS * GSIZE), I32),
                pltpu.VMEM((PER * SHARDS, 128), F32),
                copies_semaphores(6),
            ],
            name="request",
        )
        arrived = swap(sent.reshape(SHARDS, 1, PER * 128), ("y", "x", "z")).reshape(PER * SHARDS, 128)
    pieces, norms = call(
        prepare_kernel, [shape((3, ROWS, D), BF16), shape((8, ROWS))], centroids, name="prepare"
    )
    with jax.named_scope("primary_rows"):
        [found] = call(
            fetch_kernel,
            [shape((COLS, 16, D))],
            arrived,
            pieces,
            far_out=(0,),
            scratch=[pltpu.VMEM((2, COLS, 8, D), F32), copies_semaphores(2)],
            name="fetch",
        )
        fetched = swap(found, plane).reshape(SLOTS, D)
    info, slots, most = call(
        slots_kernel,
        [shape((COLV, 128), I32), shape((SLOTS, COLV)), shape((8, 128), I32)],
        me,
        arrived,
        found,
        smem=(0,),
        far_in=(2,),
        scratch=[pltpu.VMEM((2, SHARDS, 128), I32)],
        name="slots",
    )
    most = most[:1, :1]
    most = jnp.maximum(most, lax.ppermute(most, "rep", [(0, 1), (1, 0)]))[0, 0]

    def relay(turn):
        return call(
            relay_kernel,
            [shape((NZ * K, SLOTS), BF16), shape((SLOTS, NZ * K), BF16)],
            me,
            turn.reshape(1),
            info,
            slots,
            smem=(0, 1),
            name="relay",
        )

    def across(send, take):
        def move(onehot, source, name):
            [moved] = call(
                move_kernel,
                [shape((SLOTS, D))],
                onehot,
                source,
                far_out=(0,),
                scratch=[pltpu.VMEM((2, SLOTS // 2, D), F32), copies_semaphores(2)],
                name=name,
            )
            return moved

        leaving = move(send, fetched, "send")
        got = swap(leaving.reshape(NZ, K, D), "z").reshape(NZ * K, D)
        return move(take, got, "take")

    def more(state):
        turn, total = state
        return turn + 1, total + across(*relay(turn))

    with jax.named_scope("primary_across"):
        primaries = across(*relay(jnp.int32(0)))
        _, primaries = lax.while_loop(lambda s: s[0] * K < most, more, (jnp.int32(1), primaries))
    x, rows, near = call(
        near_kernel,
        [shape((COLS, 16, D)), shape((COLS, 16, 128), I32), shape((SLOTS, 128))],
        arrived,
        pieces,
        norms,
        name="near",
    )
    with jax.named_scope("primaries_out"):
        primaries = swap(primaries.reshape(COLS, 16, D), plane).reshape(SLOTS, D)
    [losses] = call(
        loss_kernel,
        [shape((SHARDS, 128))],
        primaries,
        x,
        rows,
        near,
        pieces,
        name="loss",
    )
    with jax.named_scope("losses_back"):
        back = swap(losses.reshape(SHARDS, 1, 128), ("y", "x", "z")).reshape(SHARDS, 128)
    [result] = call(
        collect_kernel, [shape((V, GROUPS * GSIZE))], cand_owner, back, name="collect"
    )
    return result


def solution(mesh):
    fine = Mesh(mesh.devices.reshape(NY, NX, NZ, 2), ("y", "x", "z", "rep"))
    rows = P(("y", "x", "z", "rep"), None)
    in_specs = (rows, P(("y", "x", "z"), None), rows, rows, rows, rows)
    return jax.shard_map(shards, mesh=fine, in_specs=in_specs, out_specs=rows, check_vma=False)
```

```python
import functools

import jax
import jax.numpy as jnp
from jax import lax
from jax.experimental import pallas as pl
from jax.experimental.pallas import tpu as pltpu
from jax.sharding import Mesh, PartitionSpec as P

D = 1024
V = 32
GROUPS = 4
GSIZE = 64
ROWS = 512
NY, NX, NZ = 4, 4, 8
COLS = NY * NX
COLV = NZ * V
SLOTS = COLS * NZ * 2
SHARDS = COLS * NZ
K = 32
LATER = 16
PER = 3
amplify = 1.0
tiny = 1e-06

F32, BF16, I32 = jnp.float32, jnp.bfloat16, jnp.int32
VMEM = pl.BlockSpec(memory_space=pltpu.VMEM)
SMEM = pl.BlockSpec(memory_space=pltpu.SMEM)
HBM = pl.BlockSpec(memory_space=pltpu.HBM)
NN = (((1,), (0,)), ((), ()))
NT = (((1,), (1,)), ((), ()))
TN = (((0,), (0,)), ((), ()))


def call(kernel, out_shape, *operands, smem=(), far_in=(), far_out=(), scratch=(), alias=None, name=None):
    specs = [SMEM if i in smem else HBM if i in far_in else VMEM for i in range(len(operands))]
    operands = [
        pltpu.with_memory_space_constraint(a, pltpu.HBM) if i in far_in else a
        for i, a in enumerate(operands)
    ]
    out_shape = [
        pltpu.HBM(o.shape, o.dtype) if i in far_out else o for i, o in enumerate(out_shape)
    ]
    return pl.pallas_call(
        kernel,
        out_shape=out_shape,
        in_specs=specs,
        out_specs=[HBM if i in far_out else VMEM for i in range(len(out_shape))],
        scratch_shapes=list(scratch),
        input_output_aliases=alias or {},
        compiler_params=pltpu.CompilerParams(vmem_limit_bytes=24 * 2**20),
        name=name,
    )(*operands)


def copies_semaphores(n):
    return pltpu.SemaphoreType.DMA((n,))


def start_all(copies):
    for copy in copies:
        copy.start()


def wait_all(copies):
    for copy in copies:
        copy.wait()


def shape(dims, dtype=F32):
    return jax.ShapeDtypeStruct(dims, dtype)


def split3(a):
    hi = a.astype(BF16)
    rest = a - hi.astype(F32)
    mid = rest.astype(BF16)
    lo = (rest - mid.astype(F32)).astype(BF16)
    return hi, mid, lo


def dot(a, b, dims=NN):
    return lax.dot_general(a, b, dims, preferred_element_type=F32)


def pick(onehot, pieces):
    hi, mid, lo = pieces
    return dot(onehot, hi) + dot(onehot, mid) + dot(onehot, lo)


def bits(mask):
    return jnp.where(mask, 1.0, 0.0)


def iota(dims, axis):
    return lax.broadcasted_iota(I32, dims, axis)


def before_same_block(rows):
    u, w = iota((rows, rows), 0), iota((rows, rows), 1)
    return bits((w < u) & ((u >> 5) == (w >> 5))).astype(BF16)


def before_all(rows):
    return bits(iota((rows, rows), 1) < iota((rows, rows), 0)).astype(BF16)


def prepare_kernel(c_ref, pieces_ref, norms_ref):
    c = c_ref[...]
    for i, piece in enumerate(split3(c)):
        pieces_ref[i] = piece
    squares = split3(c * c)
    ones = jnp.ones((8, D), BF16)
    norms_ref[...] = sum(dot(ones, s, NT) for s in squares)


def request_kernel(owner_ref, row_ref, cand_ref, rows_ref, out_ref, owner, row, cand, rows, hold, sems):
    copies = [
        pltpu.make_async_copy(a, b, sems.at[i])
        for i, (a, b) in enumerate(
            [(owner_ref, owner), (row_ref, row), (cand_ref, cand), (rows_ref, rows)]
        )
    ]
    start_all(copies)
    shard = iota((SHARDS, V), 0)
    earlier = bits(iota((V, V), 0) < iota((V, V), 1)).astype(BF16)
    lane = iota((SHARDS, 128), 1)
    wait_all(copies)
    hit = owner[...] == shard
    rank = dot(bits(hit).astype(BF16), earlier)
    asked = row[...].astype(F32)
    asks = [
        jnp.sum(jnp.where(hit & (rank == float(k)), asked, 0.0), axis=1, keepdims=True)
        for k in range(2)
    ]
    empty = jnp.zeros((1, V), I32)
    owners = jnp.concatenate([empty, owner[...], empty, empty], axis=1).astype(F32)
    line = jnp.where(lane == 0, asks[0], jnp.where(lane == 1, asks[1], 0.0)) + owners
    hold[pl.ds(0, SHARDS, stride=PER), :] = line
    line = jnp.concatenate([cand[g : g + 1, :] for g in range(GROUPS)], axis=1).astype(F32)
    hold[pl.ds(1, SHARDS, stride=PER), :] = jnp.broadcast_to(line, (SHARDS, 128))
    hits = [cand[g : g + 1, :] == shard for g in range(GROUPS)]
    any_hit = hits[0] | hits[1] | hits[2] | hits[3]
    rank = dot(bits(any_hit).astype(BF16), earlier)
    wide = [split3(rows[:, 128 * h : 128 * h + 128].astype(F32))[:2] for h in range(2)]
    lines = []
    for k in range(2):
        sides = [jnp.zeros((SHARDS, 128), F32)] * 2
        for g in range(GROUPS):
            onehot = bits(hits[g] & (rank == float(k))).astype(BF16)
            sides[g % 2] = sides[g % 2] + dot(onehot, wide[g // 2][0]) + dot(onehot, wide[g // 2][1])
        sides[1 - k] = pltpu.roll(sides[1 - k], GSIZE, 1)
        side = even_lanes if k == 0 else odd_lanes
        lines.append(side(sides[0]) + side(sides[1]))
    hold[pl.ds(2, SHARDS, stride=PER), :] = lines[0] + lines[1]
    copy = pltpu.make_async_copy(hold, out_ref, sems.at[4])
    copy.start()
    copy.wait()


def even_lanes(a):
    return jnp.where(iota(a.shape, 1) < GSIZE, a, 0.0)


def odd_lanes(a):
    return jnp.where(iota(a.shape, 1) < GSIZE, 0.0, a)


def slots_kernel(me_ref, got_ref, found_ref, info_ref, slots_ref, most_ref, hold):
    me, column = me_ref[0], me_ref[1]
    owners = got_ref[pl.ds(0, SHARDS, stride=PER), :].astype(I32)
    cands = got_ref[pl.ds(1, SHARDS, stride=PER), :].astype(I32)
    hold[0] = owners
    hold[1] = cands
    at = pl.multiple_of(column * NZ, NZ)
    tile = jnp.concatenate([hold[0, pl.ds(at, NZ), :], hold[1, pl.ds(at, NZ), :]], axis=0)
    turned = jnp.concatenate([tile, jnp.zeros((128 - NZ * 2, 128), I32)], axis=0).T
    block_lane = iota((V, 128), 1)
    for z in range(NZ):
        block = jnp.where(block_lane == 0, turned[V : 2 * V, z : z + 1], 0)
        for g in range(GROUPS):
            cand = turned[g * V : (g + 1) * V, NZ + z : NZ + z + 1]
            block = jnp.where(block_lane == 1 + g, cand, block)
        info_ref[z * V : (z + 1) * V, :] = block
    lane = iota((COLV, 128), 1)
    hit = lane < 0
    for g in range(GROUPS):
        hit = hit | (info_ref[:, 1 + g : 2 + g] == lane * NZ + me)
    hit = hit & (lane < COLS)
    rank = dot(before_same_block(COLV), bits(hit).astype(BF16))
    mine = (iota((NZ, COLV), 1) >> 5) == iota((NZ, COLV), 0)
    for k in range(2):
        turned = bits(hit & (rank == float(k))).T
        for b in range(COLS):
            part = jnp.where(mine, turned[b : b + 1, :], 0.0)
            slots_ref[b * 16 + k * 8 : b * 16 + k * 8 + 8, :] = part
    lane = iota((SHARDS, 128), 1)
    owners = jnp.where((lane >= V) & (lane < 2 * V), owners, 0)
    owners = owners + pltpu.roll(owners, 2 * V, 1)
    owners = (owners + pltpu.roll(owners, V, 1)) & 7
    parts = []
    for b in range(NZ):
        to_plane = bits((cands & 7) == b)
        to_plane = jnp.maximum(to_plane, pltpu.roll(to_plane, 2 * V, 1))
        to_plane = jnp.maximum(to_plane, pltpu.roll(to_plane, V, 1))
        for h in range(2):
            parts.append(jnp.where(owners == (lane >> 5) + 4 * h, to_plane, 0.0).astype(BF16))
    columns = bits((iota((COLS, SHARDS), 1) >> 3) == iota((COLS, SHARDS), 0)).astype(BF16)
    group = bits((iota((128, 128), 0) >> 5) == iota((128, 128), 1)).astype(BF16)
    most = 0.0
    for part in parts:
        most = jnp.maximum(most, jnp.max(dot(dot(columns, part).astype(BF16), group)))
    most_ref[...] = jnp.full((8, 128), most, F32).astype(I32)


def relay_kernel(me_ref, turn_ref, info_ref, slots_ref, send_ref, take_ref):
    me = me_ref[0]
    base = turn_ref[0].astype(F32)
    depth_of = send_ref.shape[0] // NZ
    lane = iota((COLV, 128), 1)
    u = iota((COLV, 1), 0)
    info = info_ref[...]
    owner = info[:, 0:1]
    hits = bits((owner == lane * NZ + me) & (lane < COLS))
    rank = dot(before_same_block(COLV), hits.astype(BF16))
    rank = jnp.sum(rank * hits, axis=1, keepdims=True)
    here = (owner & 7) == me
    wanted = lane < 0
    to_me = u < 0
    for g in range(GROUPS):
        plane = info[:, 1 + g : 2 + g] & 7
        wanted = wanted | (plane == lane)
        to_me = to_me | (plane == me)
    earlier = before_all(COLV)
    leaves = wanted & (lane < NZ) & here
    order = dot(earlier, bits(leaves).astype(BF16))
    place = jnp.where(leaves, order - base, -1.0).T
    depth = iota((depth_of, COLV), 0).astype(F32)
    rows = jnp.concatenate([bits(place[z : z + 1, :] == depth) for z in range(NZ)], axis=0)
    slot = (owner >> 3) * 16 + rank.astype(I32) * 8 + (u >> 5)
    held = bits((slot == iota((COLV, SLOTS), 1)) & here)
    send_ref[...] = dot(rows.astype(BF16), held.astype(BF16)).astype(BF16)
    comes = ((owner & 7) == lane) & (lane < NZ) & to_me
    order = dot(earlier, bits(comes).astype(BF16)) - base
    fits = comes & (order >= 0.0) & (order < float(depth_of))
    at = jnp.sum(jnp.where(fits, lane.astype(F32) * depth_of + order + 1.0, 0.0), axis=1, keepdims=True)
    found = bits(at == iota((COLV, NZ * depth_of), 1).astype(F32) + 1.0).astype(BF16)
    take_ref[...] = dot(slots_ref[...].astype(BF16), found).astype(BF16)


def fetch_kernel(got_ref, pieces_ref, out_ref, hold, sems):
    column = iota((SHARDS, ROWS), 1)
    asked = got_ref[pl.ds(0, SHARDS, stride=PER), :].astype(I32)
    pieces = [pieces_ref[i] for i in range(3)]
    copies = []
    for k in range(2):
        onehot = bits(asked[:, k : k + 1] == column).astype(BF16)
        hold[k] = pick(onehot, pieces).reshape(COLS, 8, D)
        copies.append(
            pltpu.make_async_copy(hold.at[k], out_ref.at[:, pl.ds(k * 8, 8), :], sems.at[k])
        )
        copies[-1].start()
    wait_all(copies)


def send_kernel(onehot_ref, in_ref, out_ref, hold, sems):
    pieces = split3(in_ref[...])
    half = onehot_ref.shape[0] // 2
    copies = []
    for c in range(2):
        hold[c] = pick(onehot_ref[c * half : (c + 1) * half, :], pieces)
        copies.append(
            pltpu.make_async_copy(hold.at[c], out_ref.at[pl.ds(c * half, half), :], sems.at[c])
        )
        copies[-1].start()
    wait_all(copies)


def put_kernel(first, onehot_ref, in_ref, both_ref, out_ref, hold, sems):
    pieces = split3(in_ref[...])
    half = SLOTS // 2
    at = [out_ref.at[pl.ds(c * half, half), pl.ds(first, D)] for c in range(2)]
    copies = []
    for c in range(2):
        hold[c] = pick(onehot_ref[c * half : (c + 1) * half, :], pieces)
        copies.append(pltpu.make_async_copy(hold.at[c], at[c], sems.at[c]))
        copies[-1].start()
    wait_all(copies)


def add_kernel(onehot_ref, in_ref, both_ref, out_ref, hold, sems):
    at = out_ref.at[:, pl.ds(D, D)]
    copy = pltpu.make_async_copy(at, hold, sems.at[0])
    copy.start()
    copy.wait()
    hold[...] += pick(onehot_ref[...], split3(in_ref[...]))
    copy = pltpu.make_async_copy(hold, at, sems.at[1])
    copy.start()
    copy.wait()


def vectors_kernel(slots_ref, in_ref, out_ref, hold, sems):
    onehot = slots_ref[...].astype(BF16)
    pieces = split3(in_ref[...])
    half = SLOTS // 2
    copies = []
    for c in range(2):
        hold[c] = pick(onehot[c * half : (c + 1) * half, :], pieces)
        target = out_ref.at[pl.ds(c * half, half), pl.ds(0, D)]
        copies.append(pltpu.make_async_copy(hold.at[c], target, sems.at[c]))
        copies[-1].start()
    wait_all(copies)


def lookup(table, rows):
    low, high = rows & 127, rows >> 7
    found = jnp.zeros(rows.shape, F32)
    for i in range(ROWS // 128):
        part = jnp.take_along_axis(table[:, 128 * i : 128 * i + 128], low, axis=1)
        found = jnp.where(high == i, part, found)
    return found


def scores(a, pieces_ref):
    hi, mid, lo = split3(a)
    chi, cmid, clo = (pieces_ref[i] for i in range(3))
    small = dot(mid, cmid, NT) + dot(lo, chi, NT) + dot(hi, clo, NT)
    return dot(hi, chi, NT) + (dot(hi, cmid, NT) + dot(mid, chi, NT) + small)


def loss_kernel(both_ref, got_ref, pieces_ref, norms_ref, out_ref):
    line = got_ref[pl.ds(2, SHARDS, stride=PER), :].astype(I32)
    rows = [line, pltpu.roll(line, GSIZE, 1)]
    rows = jnp.concatenate([a.reshape(COLS, 1, NZ, 128) for a in rows], axis=1).reshape(SLOTS, 128)
    rows = rows & (ROWS - 1)
    x = both_ref[:, :D]
    r = x - both_ref[:, D:]
    square = jnp.sum(x * x, axis=1, keepdims=True)
    near = square - 2.0 * scores(x, pieces_ref) + norms_ref[0:1, :]
    hi = r.astype(BF16)
    mid = (r - hi.astype(F32)).astype(BF16)
    chi, cmid = pieces_ref[0], pieces_ref[1]
    table = dot(hi, chi, NT) + (dot(hi, cmid, NT) + dot(mid, chi, NT))
    rx = jnp.sum(r * x, axis=1, keepdims=True)
    rr = jnp.sum(r * r, axis=1, keepdims=True)
    gap = rx - table
    loss = lookup((near + amplify * gap * gap / (rr + tiny)) / D, rows)
    loss = loss.reshape(COLS, 2, NZ, 128)
    second = pltpu.roll(loss[:, 1].reshape(COLS * NZ, 128), GSIZE, 1)
    first = loss[:, 0].reshape(COLS * NZ, 128)
    out_ref[...] = jnp.where(iota((COLS * NZ, 128), 1) < GSIZE, first, second)


def collect_kernel(owner_ref, in_ref, out_ref):
    lane = iota((V, 128), 1)
    hits = [owner_ref[:, g : g + 1] == lane for g in range(GROUPS)]
    rank = dot(before_same_block(V), bits(hits[0] | hits[1] | hits[2] | hits[3]).astype(BF16))
    a = in_ref[...]
    plain, rolled = split3(a), split3(pltpu.roll(a, GSIZE, 1))
    for h in range(2):
        halves = []
        for g in (2 * h, 2 * h + 1):
            first = bits(hits[g] & (rank == 0.0)).astype(BF16)
            second = bits(hits[g] & (rank == 1.0)).astype(BF16)
            if g % 2 == 0:
                halves.append(pick(first, plain) + pick(second, rolled))
            else:
                halves.append(pick(first, rolled) + pick(second, plain))
        out_ref[:, 128 * h : 128 * h + 128] = jnp.where(lane < GSIZE, halves[0], halves[1])


def swap(a, axes):
    return lax.all_to_all(a, axes, split_axis=0, concat_axis=0, tiled=True)


def shards(new_vectors, centroids, primary_owner, primary_row, cand_owner, cand_row):
    plane = ("y", "x")
    column = lax.axis_index(("y", "x")).astype(I32)
    me = jnp.stack([lax.axis_index("z").astype(I32), column])
    with jax.named_scope("column_vectors"):
        vectors = lax.all_gather(new_vectors, "z", axis=0, tiled=True)
    with jax.named_scope("requests"):
        [sent] = call(
            request_kernel,
            [shape((PER * SHARDS, 128))],
            primary_owner.T,
            primary_row.T,
            cand_owner.T,
            cand_row,
            far_in=(0, 1, 2, 3),
            far_out=(0,),
            scratch=[
                pltpu.VMEM((1, V), I32),
                pltpu.VMEM((1, V), I32),
                pltpu.VMEM((GROUPS, V), I32),
                pltpu.VMEM((V, GROUPS * GSIZE), I32),
                pltpu.VMEM((PER * SHARDS, 128), F32),
                copies_semaphores(5),
            ],
            name="request",
        )
        arrived = swap(sent.reshape(SHARDS, 1, PER * 128), ("y", "x", "z")).reshape(PER * SHARDS, 128)
    pieces, norms = call(
        prepare_kernel, [shape((3, ROWS, D), BF16), shape((8, ROWS))], centroids, name="prepare"
    )
    with jax.named_scope("primary_rows"):
        [found] = call(
            fetch_kernel,
            [shape((COLS, 16, D))],
            arrived,
            pieces,
            far_out=(0,),
            scratch=[pltpu.VMEM((2, COLS, 8, D), F32), copies_semaphores(2)],
            name="fetch",
        )
        fetched = swap(found, plane).reshape(SLOTS, D)
    info, slots, most = call(
        slots_kernel,
        [shape((COLV, 128), I32), shape((SLOTS, COLV)), shape((8, 128), I32)],
        me,
        arrived,
        found,
        smem=(0,),
        far_in=(2,),
        scratch=[pltpu.VMEM((2, SHARDS, 128), I32)],
        name="slots",
    )
    most = most[:1, :1]
    most = jnp.maximum(most, lax.ppermute(most, "rep", [(0, 1), (1, 0)]))[0, 0]

    halves = [pltpu.VMEM((2, SLOTS // 2, D), F32), copies_semaphores(2)]
    pair = [shape((SLOTS, 2 * D))]

    def across(base, depth):
        send, take = call(
            relay_kernel,
            [shape((NZ * depth, SLOTS), BF16), shape((SLOTS, NZ * depth), BF16)],
            me,
            base.reshape(1),
            info,
            slots,
            smem=(0, 1),
            name="relay",
        )
        [leaving] = call(
            send_kernel,
            [shape((NZ * depth, D))],
            send,
            fetched,
            far_out=(0,),
            scratch=[pltpu.VMEM((2, NZ * depth // 2, D), F32), copies_semaphores(2)],
            name="send",
        )
        return take, swap(leaving.reshape(NZ, depth, D), "z").reshape(NZ * depth, D)

    def more(state):
        base, both = state
        take, got = across(base, LATER)
        [both] = call(
            add_kernel,
            pair,
            take,
            got,
            both,
            far_in=(2,),
            far_out=(0,),
            alias={2: 0},
            scratch=[pltpu.VMEM((SLOTS, D), F32), copies_semaphores(2)],
            name="add",
        )
        return base + LATER, both

    with jax.named_scope("vectors_out"):
        [both] = call(
            vectors_kernel, pair, slots, vectors, far_out=(0,), scratch=halves, name="vectors"
        )
    with jax.named_scope("primary_across"):
        take, got = across(jnp.int32(0), K)
        [both] = call(
            functools.partial(put_kernel, D),
            pair,
            take,
            got,
            both,
            far_in=(2,),
            far_out=(0,),
            alias={2: 0},
            scratch=halves,
            name="put",
        )
        _, both = lax.while_loop(lambda s: s[0] < most, more, (jnp.int32(K), both))
    with jax.named_scope("out_to_owners"):
        both = swap(both.reshape(COLS, 16, 2 * D), plane).reshape(SLOTS, 2 * D)
    [losses] = call(
        loss_kernel, [shape((SHARDS, 128))], both, arrived, pieces, norms, name="loss"
    )
    with jax.named_scope("losses_back"):
        back = swap(losses.reshape(SHARDS, 1, 128), ("y", "x", "z")).reshape(SHARDS, 128)
    [result] = call(
        collect_kernel, [shape((V, GROUPS * GSIZE))], cand_owner, back, name="collect"
    )
    return result


def solution(mesh):
    fine = Mesh(mesh.devices.reshape(NY, NX, NZ, 2), ("y", "x", "z", "rep"))
    rows = P(("y", "x", "z", "rep"), None)
    in_specs = (rows, P(("y", "x", "z"), None), rows, rows, rows, rows)
    return jax.shard_map(shards, mesh=fine, in_specs=in_specs, out_specs=rows, check_vma=False)
```

```python
import functools

import jax
import jax.numpy as jnp
from jax import lax
from jax.experimental import pallas as pl
from jax.experimental.pallas import tpu as pltpu
from jax.sharding import Mesh, PartitionSpec as P

D = 1024
V = 32
GROUPS = 4
GSIZE = 64
ROWS = 512
NY, NX, NZ = 4, 4, 8
COLS = NY * NX
COLV = NZ * V
SLOTS = COLS * NZ * 2
SHARDS = COLS * NZ
K = 32
LATER = 16
PER = 3
FIRST = (2, -2, 1, -1)
amplify = 1.0
tiny = 1e-06

F32, BF16, I32 = jnp.float32, jnp.bfloat16, jnp.int32
VMEM = pl.BlockSpec(memory_space=pltpu.VMEM)
SMEM = pl.BlockSpec(memory_space=pltpu.SMEM)
HBM = pl.BlockSpec(memory_space=pltpu.HBM)
NN = (((1,), (0,)), ((), ()))
NT = (((1,), (1,)), ((), ()))
TN = (((0,), (0,)), ((), ()))


def call(kernel, out_shape, *operands, smem=(), far_in=(), far_out=(), scratch=(), alias=None, name=None):
    specs = [SMEM if i in smem else HBM if i in far_in else VMEM for i in range(len(operands))]
    operands = [
        pltpu.with_memory_space_constraint(a, pltpu.HBM) if i in far_in else a
        for i, a in enumerate(operands)
    ]
    out_shape = [
        pltpu.HBM(o.shape, o.dtype) if i in far_out else o for i, o in enumerate(out_shape)
    ]
    return pl.pallas_call(
        kernel,
        out_shape=out_shape,
        in_specs=specs,
        out_specs=[HBM if i in far_out else VMEM for i in range(len(out_shape))],
        scratch_shapes=list(scratch),
        input_output_aliases=alias or {},
        compiler_params=pltpu.CompilerParams(vmem_limit_bytes=24 * 2**20),
        name=name,
    )(*operands)


def copies_semaphores(n):
    return pltpu.SemaphoreType.DMA((n,))


def start_all(copies):
    for copy in copies:
        copy.start()


def wait_all(copies):
    for copy in copies:
        copy.wait()


def shape(dims, dtype=F32):
    return jax.ShapeDtypeStruct(dims, dtype)


def split3(a):
    hi = a.astype(BF16)
    rest = a - hi.astype(F32)
    mid = rest.astype(BF16)
    lo = (rest - mid.astype(F32)).astype(BF16)
    return hi, mid, lo


def dot(a, b, dims=NN):
    return lax.dot_general(a, b, dims, preferred_element_type=F32)


def pick(onehot, pieces):
    hi, mid, lo = pieces
    return dot(onehot, hi) + dot(onehot, mid) + dot(onehot, lo)


def bits(mask):
    return jnp.where(mask, 1.0, 0.0)


def iota(dims, axis):
    return lax.broadcasted_iota(I32, dims, axis)


def before_same_block(rows):
    u, w = iota((rows, rows), 0), iota((rows, rows), 1)
    return bits((w < u) & ((u >> 5) == (w >> 5))).astype(BF16)


def before_all(rows):
    return bits(iota((rows, rows), 1) < iota((rows, rows), 0)).astype(BF16)


def prepare_kernel(c_ref, pieces_ref, norms_ref):
    c = c_ref[...]
    for i, piece in enumerate(split3(c)):
        pieces_ref[i] = piece
    squares = split3(c * c)
    ones = jnp.ones((8, D), BF16)
    norms_ref[...] = sum(dot(ones, s, NT) for s in squares)


def request_kernel(owner_ref, row_ref, cand_ref, rows_ref, out_ref, owner, row, cand, rows, hold, sems):
    copies = [
        pltpu.make_async_copy(a, b, sems.at[i])
        for i, (a, b) in enumerate(
            [(owner_ref, owner), (row_ref, row), (cand_ref, cand), (rows_ref, rows)]
        )
    ]
    start_all(copies)
    shard = iota((SHARDS, V), 0)
    earlier = bits(iota((V, V), 0) < iota((V, V), 1)).astype(BF16)
    lane = iota((SHARDS, 128), 1)
    wait_all(copies)
    hit = owner[...] == shard
    rank = dot(bits(hit).astype(BF16), earlier)
    asked = row[...].astype(F32)
    asks = [
        jnp.sum(jnp.where(hit & (rank == float(k)), asked, 0.0), axis=1, keepdims=True)
        for k in range(2)
    ]
    empty = jnp.zeros((1, V), I32)
    owners = jnp.concatenate([empty, owner[...], empty, empty], axis=1).astype(F32)
    line = jnp.where(lane == 0, asks[0], jnp.where(lane == 1, asks[1], 0.0)) + owners
    hold[pl.ds(0, SHARDS, stride=PER), :] = line
    line = jnp.concatenate([cand[g : g + 1, :] for g in range(GROUPS)], axis=1).astype(F32)
    hold[pl.ds(1, SHARDS, stride=PER), :] = jnp.broadcast_to(line, (SHARDS, 128))
    hits = [cand[g : g + 1, :] == shard for g in range(GROUPS)]
    any_hit = hits[0] | hits[1] | hits[2] | hits[3]
    rank = dot(bits(any_hit).astype(BF16), earlier)
    wide = [split3(rows[:, 128 * h : 128 * h + 128].astype(F32))[:2] for h in range(2)]
    lines = []
    for k in range(2):
        sides = [jnp.zeros((SHARDS, 128), F32)] * 2
        for g in range(GROUPS):
            onehot = bits(hits[g] & (rank == float(k))).astype(BF16)
            sides[g % 2] = sides[g % 2] + dot(onehot, wide[g // 2][0]) + dot(onehot, wide[g // 2][1])
        sides[1 - k] = pltpu.roll(sides[1 - k], GSIZE, 1)
        side = even_lanes if k == 0 else odd_lanes
        lines.append(side(sides[0]) + side(sides[1]))
    hold[pl.ds(2, SHARDS, stride=PER), :] = lines[0] + lines[1]
    copy = pltpu.make_async_copy(hold, out_ref, sems.at[4])
    copy.start()
    copy.wait()


def even_lanes(a):
    return jnp.where(iota(a.shape, 1) < GSIZE, a, 0.0)


def odd_lanes(a):
    return jnp.where(iota(a.shape, 1) < GSIZE, 0.0, a)


def slots_kernel(me_ref, got_ref, found_ref, info_ref, slots_ref, most_ref, hold):
    me, column = me_ref[0], me_ref[1]
    owners = got_ref[pl.ds(0, SHARDS, stride=PER), :].astype(I32)
    cands = got_ref[pl.ds(1, SHARDS, stride=PER), :].astype(I32)
    hold[0] = owners
    hold[1] = cands
    at = pl.multiple_of(column * NZ, NZ)
    tile = jnp.concatenate([hold[0, pl.ds(at, NZ), :], hold[1, pl.ds(at, NZ), :]], axis=0)
    turned = jnp.concatenate([tile, jnp.zeros((128 - NZ * 2, 128), I32)], axis=0).T
    block_lane = iota((V, 128), 1)
    for z in range(NZ):
        block = jnp.where(block_lane == 0, turned[V : 2 * V, z : z + 1], 0)
        for g in range(GROUPS):
            cand = turned[g * V : (g + 1) * V, NZ + z : NZ + z + 1]
            block = jnp.where(block_lane == 1 + g, cand, block)
        info_ref[z * V : (z + 1) * V, :] = block
    lane = iota((COLV, 128), 1)
    hit = lane < 0
    for g in range(GROUPS):
        hit = hit | (info_ref[:, 1 + g : 2 + g] == lane * NZ + me)
    hit = hit & (lane < COLS)
    rank = dot(before_same_block(COLV), bits(hit).astype(BF16))
    mine = (iota((NZ, COLV), 1) >> 5) == iota((NZ, COLV), 0)
    for k in range(2):
        turned = bits(hit & (rank == float(k))).T
        for b in range(COLS):
            part = jnp.where(mine, turned[b : b + 1, :], 0.0)
            slots_ref[b * 16 + k * 8 : b * 16 + k * 8 + 8, :] = part
    lane = iota((SHARDS, 128), 1)
    owners = jnp.where((lane >= V) & (lane < 2 * V), owners, 0)
    owners = owners + pltpu.roll(owners, 2 * V, 1)
    owners = (owners + pltpu.roll(owners, V, 1)) & 7
    parts = []
    for b in range(NZ):
        to_plane = bits((cands & 7) == b)
        to_plane = jnp.maximum(to_plane, pltpu.roll(to_plane, 2 * V, 1))
        to_plane = jnp.maximum(to_plane, pltpu.roll(to_plane, V, 1))
        for h in range(2):
            parts.append(jnp.where(owners == (lane >> 5) + 4 * h, to_plane, 0.0).astype(BF16))
    columns = bits((iota((COLS, SHARDS), 1) >> 3) == iota((COLS, SHARDS), 0)).astype(BF16)
    group = bits((iota((128, 128), 0) >> 5) == iota((128, 128), 1)).astype(BF16)
    most = 0.0
    for part in parts:
        most = jnp.maximum(most, jnp.max(dot(dot(columns, part).astype(BF16), group)))
    most_ref[...] = jnp.full((8, 128), most, F32).astype(I32)


def relay_kernel(me_ref, turn_ref, info_ref, slots_ref, send_ref, take_ref):
    me = me_ref[0]
    base = turn_ref[0].astype(F32)
    depth_of = send_ref.shape[0] // NZ
    lane = iota((COLV, 128), 1)
    u = iota((COLV, 1), 0)
    info = info_ref[...]
    owner = info[:, 0:1]
    hits = bits((owner == lane * NZ + me) & (lane < COLS))
    rank = dot(before_same_block(COLV), hits.astype(BF16))
    rank = jnp.sum(rank * hits, axis=1, keepdims=True)
    here = (owner & 7) == me
    wanted = lane < 0
    to_me = u < 0
    for g in range(GROUPS):
        plane = info[:, 1 + g : 2 + g] & 7
        wanted = wanted | (plane == lane)
        to_me = to_me | (plane == me)
    earlier = before_all(COLV)
    leaves = wanted & (lane < NZ) & here
    order = dot(earlier, bits(leaves).astype(BF16))
    place = jnp.where(leaves, order - base, -1.0).T
    depth = iota((depth_of, COLV), 0).astype(F32)
    rows = jnp.concatenate([bits(place[z : z + 1, :] == depth) for z in range(NZ)], axis=0)
    slot = (owner >> 3) * 16 + rank.astype(I32) * 8 + (u >> 5)
    held = bits((slot == iota((COLV, SLOTS), 1)) & here)
    send_ref[...] = dot(rows.astype(BF16), held.astype(BF16)).astype(BF16)
    comes = ((owner & 7) == lane) & (lane < NZ) & to_me
    order = dot(earlier, bits(comes).astype(BF16)) - base
    fits = comes & (order >= 0.0) & (order < float(depth_of))
    at = jnp.sum(jnp.where(fits, lane.astype(F32) * depth_of + order + 1.0, 0.0), axis=1, keepdims=True)
    found = bits(at == iota((COLV, NZ * depth_of), 1).astype(F32) + 1.0).astype(BF16)
    take_ref[...] = dot(slots_ref[...].astype(BF16), found).astype(BF16)


def fetch_kernel(got_ref, pieces_ref, *rest):
    out_ref, hold, sems = rest[-3:]
    column = iota((SHARDS, ROWS), 1)
    asked = got_ref[pl.ds(0, SHARDS, stride=PER), :].astype(I32)
    pieces = [pieces_ref[i] for i in range(3)]
    copies = []
    for k in range(2):
        onehot = bits(asked[:, k : k + 1] == column).astype(BF16)
        hold[k] = pick(onehot, pieces).reshape(COLS, 8, D)
        copies.append(
            pltpu.make_async_copy(hold.at[k], out_ref.at[:, pl.ds(k * 8, 8), :], sems.at[k])
        )
        copies[-1].start()
    wait_all(copies)


def send_kernel(onehot_ref, in_ref, *rest):
    out_ref, hold, sems = rest[-3:]
    pieces = split3(in_ref[...])
    half = onehot_ref.shape[0] // 2
    copies = []
    for c in range(2):
        hold[c] = pick(onehot_ref[c * half : (c + 1) * half, :], pieces)
        copies.append(
            pltpu.make_async_copy(hold.at[c], out_ref.at[pl.ds(c * half, half), :], sems.at[c])
        )
        copies[-1].start()
    wait_all(copies)


def put_kernel(first, onehot_ref, in_ref, both_ref, out_ref, hold, sems):
    pieces = split3(in_ref[...])
    half = SLOTS // 2
    at = [out_ref.at[pl.ds(c * half, half), pl.ds(first, D)] for c in range(2)]
    copies = []
    for c in range(2):
        hold[c] = pick(onehot_ref[c * half : (c + 1) * half, :], pieces)
        copies.append(pltpu.make_async_copy(hold.at[c], at[c], sems.at[c]))
        copies[-1].start()
    wait_all(copies)


def add_kernel(onehot_ref, in_ref, both_ref, out_ref, hold, sems):
    at = out_ref.at[:, pl.ds(D, D)]
    copy = pltpu.make_async_copy(at, hold, sems.at[0])
    copy.start()
    copy.wait()
    hold[...] += pick(onehot_ref[...], split3(in_ref[...]))
    copy = pltpu.make_async_copy(hold, at, sems.at[1])
    copy.start()
    copy.wait()


def vectors_kernel(me_ref, slots_ref, *rest):
    parts, out_ref, column, hold, sems = rest[:NZ], rest[-4], rest[-3], rest[-2], rest[-1]
    me = me_ref[0]
    copies = []
    for i, part in enumerate(parts):
        at = pl.multiple_of(((me + i) & 7) * V, V)
        copies.append(pltpu.make_async_copy(part, column.at[pl.ds(at, V), :], sems.at[i]))
    start_all(copies)
    onehot = slots_ref[...].astype(BF16)
    wait_all(copies)
    pieces = split3(column[...])
    half = SLOTS // 2
    copies = []
    for c in range(2):
        hold[c] = pick(onehot[c * half : (c + 1) * half, :], pieces)
        target = out_ref.at[pl.ds(c * half, half), pl.ds(0, D)]
        copies.append(pltpu.make_async_copy(hold.at[c], target, sems.at[NZ + c]))
        copies[-1].start()
    wait_all(copies)


def lookup(table, rows):
    low, high = rows & 127, rows >> 7
    found = jnp.zeros(rows.shape, F32)
    for i in range(ROWS // 128):
        part = jnp.take_along_axis(table[:, 128 * i : 128 * i + 128], low, axis=1)
        found = jnp.where(high == i, part, found)
    return found


def scores(a, pieces_ref):
    hi, mid, lo = split3(a)
    chi, cmid, clo = (pieces_ref[i] for i in range(3))
    small = dot(mid, cmid, NT) + dot(lo, chi, NT) + dot(hi, clo, NT)
    return dot(hi, chi, NT) + (dot(hi, cmid, NT) + dot(mid, chi, NT) + small)


def loss_kernel(both_ref, got_ref, pieces_ref, norms_ref, out_ref):
    line = got_ref[pl.ds(2, SHARDS, stride=PER), :].astype(I32)
    rows = [line, pltpu.roll(line, GSIZE, 1)]
    rows = jnp.concatenate([a.reshape(COLS, 1, NZ, 128) for a in rows], axis=1).reshape(SLOTS, 128)
    rows = rows & (ROWS - 1)
    x = both_ref[:, :D]
    r = x - both_ref[:, D:]
    square = jnp.sum(x * x, axis=1, keepdims=True)
    near = square - 2.0 * scores(x, pieces_ref) + norms_ref[0:1, :]
    hi = r.astype(BF16)
    mid = (r - hi.astype(F32)).astype(BF16)
    chi, cmid = pieces_ref[0], pieces_ref[1]
    table = dot(hi, chi, NT) + (dot(hi, cmid, NT) + dot(mid, chi, NT))
    rx = jnp.sum(r * x, axis=1, keepdims=True)
    rr = jnp.sum(r * r, axis=1, keepdims=True)
    gap = rx - table
    loss = lookup((near + amplify * gap * gap / (rr + tiny)) / D, rows)
    loss = loss.reshape(COLS, 2, NZ, 128)
    second = pltpu.roll(loss[:, 1].reshape(COLS * NZ, 128), GSIZE, 1)
    first = loss[:, 0].reshape(COLS * NZ, 128)
    out_ref[...] = jnp.where(iota((COLS * NZ, 128), 1) < GSIZE, first, second)


def collect_kernel(owner_ref, in_ref, out_ref):
    lane = iota((V, 128), 1)
    hits = [owner_ref[:, g : g + 1] == lane for g in range(GROUPS)]
    rank = dot(before_same_block(V), bits(hits[0] | hits[1] | hits[2] | hits[3]).astype(BF16))
    a = in_ref[...]
    plain, rolled = split3(a), split3(pltpu.roll(a, GSIZE, 1))
    for h in range(2):
        halves = []
        for g in (2 * h, 2 * h + 1):
            first = bits(hits[g] & (rank == 0.0)).astype(BF16)
            second = bits(hits[g] & (rank == 1.0)).astype(BF16)
            if g % 2 == 0:
                halves.append(pick(first, plain) + pick(second, rolled))
            else:
                halves.append(pick(first, rolled) + pick(second, plain))
        out_ref[:, 128 * h : 128 * h + 128] = jnp.where(lane < GSIZE, halves[0], halves[1])


def swap(a, axes):
    return lax.all_to_all(a, axes, split_axis=0, concat_axis=0, tiled=True)


def shards(new_vectors, centroids, primary_owner, primary_row, cand_owner, cand_row):
    plane = ("y", "x")
    column = lax.axis_index(("y", "x")).astype(I32)
    me = jnp.stack([lax.axis_index("z").astype(I32), column])
    def along_z(block, step):
        return lax.ppermute(block, "z", [(z, (z - step) % NZ) for z in range(NZ)])

    with jax.named_scope("column_vectors"):
        blocks = {0: new_vectors}
        for step in (2, -2, 1, -1, 4):
            blocks[step] = along_z(new_vectors, step)
        blocks[3] = along_z(blocks[2], 1)
        blocks[-3] = along_z(blocks[-2], -1)
    with jax.named_scope("requests"):
        [sent] = call(
            request_kernel,
            [shape((PER * SHARDS, 128))],
            primary_owner.T,
            primary_row.T,
            cand_owner.T,
            cand_row,
            far_in=(0, 1, 2, 3),
            far_out=(0,),
            scratch=[
                pltpu.VMEM((1, V), I32),
                pltpu.VMEM((1, V), I32),
                pltpu.VMEM((GROUPS, V), I32),
                pltpu.VMEM((V, GROUPS * GSIZE), I32),
                pltpu.VMEM((PER * SHARDS, 128), F32),
                copies_semaphores(5),
            ],
            name="request",
        )
        arrived = swap(sent.reshape(SHARDS, 1, PER * 128), ("y", "x", "z")).reshape(PER * SHARDS, 128)
    pieces, norms = call(
        prepare_kernel, [shape((3, ROWS, D), BF16), shape((8, ROWS))], centroids, name="prepare"
    )
    with jax.named_scope("primary_rows"):
        [found] = call(
            fetch_kernel,
            [shape((COLS, 16, D))],
            arrived,
            pieces,
            *[blocks[o] for o in FIRST],
            far_in=tuple(range(2, 2 + len(FIRST))),
            far_out=(0,),
            scratch=[pltpu.VMEM((2, COLS, 8, D), F32), copies_semaphores(2)],
            name="fetch",
        )
        fetched = swap(found, plane).reshape(SLOTS, D)
    info, slots, most = call(
        slots_kernel,
        [shape((COLV, 128), I32), shape((SLOTS, COLV)), shape((8, 128), I32)],
        me,
        arrived,
        found,
        smem=(0,),
        far_in=(2,),
        scratch=[pltpu.VMEM((2, SHARDS, 128), I32)],
        name="slots",
    )
    most = most[:1, :1]
    most = jnp.maximum(most, lax.ppermute(most, "rep", [(0, 1), (1, 0)]))[0, 0]

    halves = [pltpu.VMEM((2, SLOTS // 2, D), F32), copies_semaphores(2)]
    pair = [shape((SLOTS, 2 * D))]

    def across(base, depth, *after):
        send, take = call(
            relay_kernel,
            [shape((NZ * depth, SLOTS), BF16), shape((SLOTS, NZ * depth), BF16)],
            me,
            base.reshape(1),
            info,
            slots,
            smem=(0, 1),
            name="relay",
        )
        [leaving] = call(
            send_kernel,
            [shape((NZ * depth, D))],
            send,
            fetched,
            *after,
            far_in=tuple(range(2, 2 + len(after))),
            far_out=(0,),
            scratch=[pltpu.VMEM((2, NZ * depth // 2, D), F32), copies_semaphores(2)],
            name="send",
        )
        return take, swap(leaving.reshape(NZ, depth, D), "z").reshape(NZ * depth, D)

    def more(state):
        base, both = state
        take, got = across(base, LATER)
        [both] = call(
            add_kernel,
            pair,
            take,
            got,
            both,
            far_in=(2,),
            far_out=(0,),
            alias={2: 0},
            scratch=[pltpu.VMEM((SLOTS, D), F32), copies_semaphores(2)],
            name="add",
        )
        return base + LATER, both

    with jax.named_scope("vectors_out"):
        [both] = call(
            vectors_kernel,
            pair,
            me,
            slots,
            *[blocks[o] for o in (0, 1, 2, 3, 4, -3, -2, -1)],
            smem=(0,),
            far_in=tuple(range(2, 2 + NZ)),
            far_out=(0,),
            scratch=[pltpu.VMEM((COLV, D), F32), halves[0], copies_semaphores(NZ + 2)],
            name="vectors",
        )
    with jax.named_scope("primary_across"):
        take, got = across(jnp.int32(0), K, blocks[4], blocks[3], blocks[-3])
        [both] = call(
            functools.partial(put_kernel, D),
            pair,
            take,
            got,
            both,
            far_in=(2,),
            far_out=(0,),
            alias={2: 0},
            scratch=halves,
            name="put",
        )
        _, both = lax.while_loop(lambda s: s[0] < most, more, (jnp.int32(K), both))
    with jax.named_scope("out_to_owners"):
        both = swap(both.reshape(COLS, 16, 2 * D), plane).reshape(SLOTS, 2 * D)
    [losses] = call(
        loss_kernel, [shape((SHARDS, 128))], both, arrived, pieces, norms, name="loss"
    )
    with jax.named_scope("losses_back"):
        back = swap(losses.reshape(SHARDS, 1, 128), ("y", "x", "z")).reshape(SHARDS, 128)
    [result] = call(
        collect_kernel, [shape((V, GROUPS * GSIZE))], cand_owner, back, name="collect"
    )
    return result


def solution(mesh):
    fine = Mesh(mesh.devices.reshape(NY, NX, NZ, 2), ("y", "x", "z", "rep"))
    rows = P(("y", "x", "z", "rep"), None)
    in_specs = (rows, P(("y", "x", "z"), None), rows, rows, rows, rows)
    return jax.shard_map(shards, mesh=fine, in_specs=in_specs, out_specs=rows, check_vma=False)
```

```python
import functools

import jax
import jax.numpy as jnp
from jax import lax
from jax.experimental import pallas as pl
from jax.experimental.pallas import tpu as pltpu
from jax.sharding import Mesh, PartitionSpec as P

D = 1024
V = 32
GROUPS = 4
GSIZE = 64
ROWS = 512
NY, NX, NZ = 4, 4, 8
COLS = NY * NX
COLV = NZ * V
SLOTS = COLS * NZ * 2
SHARDS = COLS * NZ
K = 32
NEXT = 8
PER = 3
FIRST = (2, -2, 1, -1)
amplify = 1.0
tiny = 1e-06

F32, BF16, I32 = jnp.float32, jnp.bfloat16, jnp.int32
VMEM = pl.BlockSpec(memory_space=pltpu.VMEM)
SMEM = pl.BlockSpec(memory_space=pltpu.SMEM)
HBM = pl.BlockSpec(memory_space=pltpu.HBM)
NN = (((1,), (0,)), ((), ()))
NT = (((1,), (1,)), ((), ()))
TN = (((0,), (0,)), ((), ()))


def call(kernel, out_shape, *operands, smem=(), far_in=(), far_out=(), scratch=(), alias=None, name=None):
    specs = [SMEM if i in smem else HBM if i in far_in else VMEM for i in range(len(operands))]
    operands = [
        pltpu.with_memory_space_constraint(a, pltpu.HBM) if i in far_in else a
        for i, a in enumerate(operands)
    ]
    out_shape = [
        pltpu.HBM(o.shape, o.dtype) if i in far_out else o for i, o in enumerate(out_shape)
    ]
    return pl.pallas_call(
        kernel,
        out_shape=out_shape,
        in_specs=specs,
        out_specs=[HBM if i in far_out else VMEM for i in range(len(out_shape))],
        scratch_shapes=list(scratch),
        input_output_aliases=alias or {},
        compiler_params=pltpu.CompilerParams(vmem_limit_bytes=24 * 2**20),
        name=name,
    )(*operands)


def copies_semaphores(n):
    return pltpu.SemaphoreType.DMA((n,))


def start_all(copies):
    for copy in copies:
        copy.start()


def wait_all(copies):
    for copy in copies:
        copy.wait()


def shape(dims, dtype=F32):
    return jax.ShapeDtypeStruct(dims, dtype)


def split3(a):
    hi = a.astype(BF16)
    rest = a - hi.astype(F32)
    mid = rest.astype(BF16)
    lo = (rest - mid.astype(F32)).astype(BF16)
    return hi, mid, lo


def dot(a, b, dims=NN):
    return lax.dot_general(a, b, dims, preferred_element_type=F32)


def pick(onehot, pieces):
    hi, mid, lo = pieces
    return dot(onehot, hi) + dot(onehot, mid) + dot(onehot, lo)


def bits(mask):
    return jnp.where(mask, 1.0, 0.0)


def iota(dims, axis):
    return lax.broadcasted_iota(I32, dims, axis)


def before_same_block(rows):
    u, w = iota((rows, rows), 0), iota((rows, rows), 1)
    return bits((w < u) & ((u >> 5) == (w >> 5))).astype(BF16)


def before_all(rows):
    return bits(iota((rows, rows), 1) < iota((rows, rows), 0)).astype(BF16)


def prepare_kernel(c_ref, pieces_ref, norms_ref):
    c = c_ref[...]
    for i, piece in enumerate(split3(c)):
        pieces_ref[i] = piece
    squares = split3(c * c)
    ones = jnp.ones((8, D), BF16)
    norms_ref[...] = sum(dot(ones, s, NT) for s in squares)


def request_kernel(owner_ref, row_ref, cand_ref, rows_ref, out_ref, owner, row, cand, rows, hold, sems):
    copies = [
        pltpu.make_async_copy(a, b, sems.at[i])
        for i, (a, b) in enumerate(
            [(owner_ref, owner), (row_ref, row), (cand_ref, cand), (rows_ref, rows)]
        )
    ]
    start_all(copies)
    shard = iota((SHARDS, V), 0)
    earlier = bits(iota((V, V), 0) < iota((V, V), 1)).astype(BF16)
    lane = iota((SHARDS, 128), 1)
    wait_all(copies)
    hit = owner[...] == shard
    rank = dot(bits(hit).astype(BF16), earlier)
    asked = row[...].astype(F32)
    asks = [
        jnp.sum(jnp.where(hit & (rank == float(k)), asked, 0.0), axis=1, keepdims=True)
        for k in range(2)
    ]
    empty = jnp.zeros((1, V), I32)
    owners = jnp.concatenate([empty, owner[...], empty, empty], axis=1).astype(F32)
    line = jnp.where(lane == 0, asks[0], jnp.where(lane == 1, asks[1], 0.0)) + owners
    hold[pl.ds(0, SHARDS, stride=PER), :] = line
    line = jnp.concatenate([cand[g : g + 1, :] for g in range(GROUPS)], axis=1).astype(F32)
    hold[pl.ds(1, SHARDS, stride=PER), :] = jnp.broadcast_to(line, (SHARDS, 128))
    hits = [cand[g : g + 1, :] == shard for g in range(GROUPS)]
    any_hit = hits[0] | hits[1] | hits[2] | hits[3]
    rank = dot(bits(any_hit).astype(BF16), earlier)
    wide = [split3(rows[:, 128 * h : 128 * h + 128].astype(F32))[:2] for h in range(2)]
    lines = []
    for k in range(2):
        sides = [jnp.zeros((SHARDS, 128), F32)] * 2
        for g in range(GROUPS):
            onehot = bits(hits[g] & (rank == float(k))).astype(BF16)
            sides[g % 2] = sides[g % 2] + dot(onehot, wide[g // 2][0]) + dot(onehot, wide[g // 2][1])
        sides[1 - k] = pltpu.roll(sides[1 - k], GSIZE, 1)
        side = even_lanes if k == 0 else odd_lanes
        lines.append(side(sides[0]) + side(sides[1]))
    hold[pl.ds(2, SHARDS, stride=PER), :] = lines[0] + lines[1]
    copy = pltpu.make_async_copy(hold, out_ref, sems.at[4])
    copy.start()
    copy.wait()


def even_lanes(a):
    return jnp.where(iota(a.shape, 1) < GSIZE, a, 0.0)


def odd_lanes(a):
    return jnp.where(iota(a.shape, 1) < GSIZE, 0.0, a)


def slots_kernel(me_ref, got_ref, found_ref, info_ref, slots_ref, most_ref, hold):
    me, column = me_ref[0], me_ref[1]
    owners = got_ref[pl.ds(0, SHARDS, stride=PER), :].astype(I32)
    cands = got_ref[pl.ds(1, SHARDS, stride=PER), :].astype(I32)
    hold[0] = owners
    hold[1] = cands
    at = pl.multiple_of(column * NZ, NZ)
    tile = jnp.concatenate([hold[0, pl.ds(at, NZ), :], hold[1, pl.ds(at, NZ), :]], axis=0)
    turned = jnp.concatenate([tile, jnp.zeros((128 - NZ * 2, 128), I32)], axis=0).T
    block_lane = iota((V, 128), 1)
    for z in range(NZ):
        block = jnp.where(block_lane == 0, turned[V : 2 * V, z : z + 1], 0)
        for g in range(GROUPS):
            cand = turned[g * V : (g + 1) * V, NZ + z : NZ + z + 1]
            block = jnp.where(block_lane == 1 + g, cand, block)
        info_ref[z * V : (z + 1) * V, :] = block
    lane = iota((COLV, 128), 1)
    hit = lane < 0
    for g in range(GROUPS):
        hit = hit | (info_ref[:, 1 + g : 2 + g] == lane * NZ + me)
    hit = hit & (lane < COLS)
    rank = dot(before_same_block(COLV), bits(hit).astype(BF16))
    mine = (iota((NZ, COLV), 1) >> 5) == iota((NZ, COLV), 0)
    for k in range(2):
        turned = bits(hit & (rank == float(k))).T
        for b in range(COLS):
            part = jnp.where(mine, turned[b : b + 1, :], 0.0)
            slots_ref[b * 16 + k * 8 : b * 16 + k * 8 + 8, :] = part
    lane = iota((SHARDS, 128), 1)
    owners = jnp.where((lane >= V) & (lane < 2 * V), owners, 0)
    owners = owners + pltpu.roll(owners, 2 * V, 1)
    owners = (owners + pltpu.roll(owners, V, 1)) & 7
    parts = []
    for b in range(NZ):
        to_plane = bits((cands & 7) == b)
        to_plane = jnp.maximum(to_plane, pltpu.roll(to_plane, 2 * V, 1))
        to_plane = jnp.maximum(to_plane, pltpu.roll(to_plane, V, 1))
        for h in range(2):
            parts.append(jnp.where(owners == (lane >> 5) + 4 * h, to_plane, 0.0).astype(BF16))
    columns = bits((iota((COLS, SHARDS), 1) >> 3) == iota((COLS, SHARDS), 0)).astype(BF16)
    group = bits((iota((128, 128), 0) >> 5) == iota((128, 128), 1)).astype(BF16)
    most = 0.0
    for part in parts:
        most = jnp.maximum(most, jnp.max(dot(dot(columns, part).astype(BF16), group)))
    most_ref[...] = jnp.full((8, 128), most, F32).astype(I32)


def relay_kernel(me_ref, turn_ref, info_ref, slots_ref, send_ref, take_ref):
    me = me_ref[0]
    base = turn_ref[0].astype(F32)
    depth_of = send_ref.shape[0] // NZ
    lane = iota((COLV, 128), 1)
    u = iota((COLV, 1), 0)
    info = info_ref[...]
    owner = info[:, 0:1]
    hits = bits((owner == lane * NZ + me) & (lane < COLS))
    rank = dot(before_same_block(COLV), hits.astype(BF16))
    rank = jnp.sum(rank * hits, axis=1, keepdims=True)
    here = (owner & 7) == me
    wanted = lane < 0
    to_me = u < 0
    for g in range(GROUPS):
        plane = info[:, 1 + g : 2 + g] & 7
        wanted = wanted | (plane == lane)
        to_me = to_me | (plane == me)
    earlier = before_all(COLV)
    leaves = wanted & (lane < NZ) & here
    order = dot(earlier, bits(leaves).astype(BF16))
    place = jnp.where(leaves, order - base, -1.0).T
    depth = iota((depth_of, COLV), 0).astype(F32)
    rows = jnp.concatenate([bits(place[z : z + 1, :] == depth) for z in range(NZ)], axis=0)
    slot = (owner >> 3) * 16 + rank.astype(I32) * 8 + (u >> 5)
    held = bits((slot == iota((COLV, SLOTS), 1)) & here)
    send_ref[...] = dot(rows.astype(BF16), held.astype(BF16)).astype(BF16)
    comes = ((owner & 7) == lane) & (lane < NZ) & to_me
    order = dot(earlier, bits(comes).astype(BF16)) - base
    fits = comes & (order >= 0.0) & (order < float(depth_of))
    at = jnp.sum(jnp.where(fits, lane.astype(F32) * depth_of + order + 1.0, 0.0), axis=1, keepdims=True)
    found = bits(at == iota((COLV, NZ * depth_of), 1).astype(F32) + 1.0).astype(BF16)
    take_ref[...] = dot(slots_ref[...].astype(BF16), found).astype(BF16)


def fetch_kernel(got_ref, pieces_ref, *rest):
    out_ref, hold, sems = rest[-3:]
    column = iota((SHARDS, ROWS), 1)
    asked = got_ref[pl.ds(0, SHARDS, stride=PER), :].astype(I32)
    pieces = [pieces_ref[i] for i in range(3)]
    copies = []
    for k in range(2):
        onehot = bits(asked[:, k : k + 1] == column).astype(BF16)
        hold[k] = pick(onehot, pieces).reshape(COLS, 8, D)
        copies.append(
            pltpu.make_async_copy(hold.at[k], out_ref.at[:, pl.ds(k * 8, 8), :], sems.at[k])
        )
        copies[-1].start()
    wait_all(copies)


def send_kernel(base_ref, onehot_ref, in_ref, *rest):
    out_ref, hold, sems = rest[-3:]
    pieces = split3(in_ref[...])
    half = onehot_ref.shape[0] // 2
    copies = []
    for c in range(2):
        hold[c] = pick(onehot_ref[c * half : (c + 1) * half, :], pieces)
        copies.append(
            pltpu.make_async_copy(hold.at[c], out_ref.at[pl.ds(c * half, half), :], sems.at[c])
        )
        copies[-1].start()
    wait_all(copies)


def put_kernel(first, onehot_ref, in_ref, both_ref, out_ref, hold, sems):
    pieces = split3(in_ref[...])
    half = SLOTS // 2
    at = [out_ref.at[pl.ds(c * half, half), pl.ds(first, D)] for c in range(2)]
    copies = []
    for c in range(2):
        hold[c] = pick(onehot_ref[c * half : (c + 1) * half, :], pieces)
        copies.append(pltpu.make_async_copy(hold.at[c], at[c], sems.at[c]))
        copies[-1].start()
    wait_all(copies)


def add_kernel(onehot_ref, in_ref, both_ref, out_ref, hold, sems):
    at = out_ref.at[:, pl.ds(D, D)]
    copy = pltpu.make_async_copy(at, hold, sems.at[0])
    copy.start()
    copy.wait()
    hold[...] += pick(onehot_ref[...], split3(in_ref[...]))
    copy = pltpu.make_async_copy(hold, at, sems.at[1])
    copy.start()
    copy.wait()


def vectors_kernel(me_ref, slots_ref, *rest):
    parts, out_ref, column, hold, sems = rest[:NZ], rest[-4], rest[-3], rest[-2], rest[-1]
    me = me_ref[0]
    copies = []
    for i, part in enumerate(parts):
        at = pl.multiple_of(((me + i) & 7) * V, V)
        copies.append(pltpu.make_async_copy(part, column.at[pl.ds(at, V), :], sems.at[i]))
    start_all(copies)
    onehot = slots_ref[...].astype(BF16)
    wait_all(copies)
    pieces = split3(column[...])
    half = SLOTS // 2
    copies = []
    for c in range(2):
        hold[c] = pick(onehot[c * half : (c + 1) * half, :], pieces)
        target = out_ref.at[pl.ds(c * half, half), pl.ds(0, D)]
        copies.append(pltpu.make_async_copy(hold.at[c], target, sems.at[NZ + c]))
        copies[-1].start()
    wait_all(copies)


def lookup(table, rows):
    low, high = rows & 127, rows >> 7
    found = jnp.zeros(rows.shape, F32)
    for i in range(ROWS // 128):
        part = jnp.take_along_axis(table[:, 128 * i : 128 * i + 128], low, axis=1)
        found = jnp.where(high == i, part, found)
    return found


def scores(a, pieces_ref):
    hi, mid, lo = split3(a)
    chi, cmid, clo = (pieces_ref[i] for i in range(3))
    small = dot(mid, cmid, NT) + dot(lo, chi, NT) + dot(hi, clo, NT)
    return dot(hi, chi, NT) + (dot(hi, cmid, NT) + dot(mid, chi, NT) + small)


def loss_kernel(both_ref, got_ref, pieces_ref, norms_ref, out_ref):
    line = got_ref[pl.ds(2, SHARDS, stride=PER), :].astype(I32)
    rows = [line, pltpu.roll(line, GSIZE, 1)]
    rows = jnp.concatenate([a.reshape(COLS, 1, NZ, 128) for a in rows], axis=1).reshape(SLOTS, 128)
    rows = rows & (ROWS - 1)
    x = both_ref[:, :D]
    r = x - both_ref[:, D:]
    square = jnp.sum(x * x, axis=1, keepdims=True)
    near = square - 2.0 * scores(x, pieces_ref) + norms_ref[0:1, :]
    hi = r.astype(BF16)
    mid = (r - hi.astype(F32)).astype(BF16)
    chi, cmid = pieces_ref[0], pieces_ref[1]
    table = dot(hi, chi, NT) + (dot(hi, cmid, NT) + dot(mid, chi, NT))
    rx = jnp.sum(r * x, axis=1, keepdims=True)
    rr = jnp.sum(r * r, axis=1, keepdims=True)
    gap = rx - table
    loss = lookup((near + amplify * gap * gap / (rr + tiny)) / D, rows)
    loss = loss.reshape(COLS, 2, NZ, 128)
    second = pltpu.roll(loss[:, 1].reshape(COLS * NZ, 128), GSIZE, 1)
    first = loss[:, 0].reshape(COLS * NZ, 128)
    out_ref[...] = jnp.where(iota((COLS * NZ, 128), 1) < GSIZE, first, second)


def collect_kernel(owner_ref, in_ref, out_ref):
    lane = iota((V, 128), 1)
    hits = [owner_ref[:, g : g + 1] == lane for g in range(GROUPS)]
    rank = dot(before_same_block(V), bits(hits[0] | hits[1] | hits[2] | hits[3]).astype(BF16))
    a = in_ref[...]
    plain, rolled = split3(a), split3(pltpu.roll(a, GSIZE, 1))
    for h in range(2):
        halves = []
        for g in (2 * h, 2 * h + 1):
            first = bits(hits[g] & (rank == 0.0)).astype(BF16)
            second = bits(hits[g] & (rank == 1.0)).astype(BF16)
            if g % 2 == 0:
                halves.append(pick(first, plain) + pick(second, rolled))
            else:
                halves.append(pick(first, rolled) + pick(second, plain))
        out_ref[:, 128 * h : 128 * h + 128] = jnp.where(lane < GSIZE, halves[0], halves[1])


def swap(a, axes):
    return lax.all_to_all(a, axes, split_axis=0, concat_axis=0, tiled=True)


def shards(new_vectors, centroids, primary_owner, primary_row, cand_owner, cand_row):
    plane = ("y", "x")
    column = lax.axis_index(("y", "x")).astype(I32)
    me = jnp.stack([lax.axis_index("z").astype(I32), column])
    def along_z(block, step):
        return lax.ppermute(block, "z", [(z, (z - step) % NZ) for z in range(NZ)])

    with jax.named_scope("column_vectors"):
        blocks = {0: new_vectors}
        for step in (2, -2, 1, -1, 4):
            blocks[step] = along_z(new_vectors, step)
        blocks[3] = along_z(blocks[2], 1)
        blocks[-3] = along_z(blocks[-2], -1)
    with jax.named_scope("requests"):
        [sent] = call(
            request_kernel,
            [shape((PER * SHARDS, 128))],
            primary_owner.T,
            primary_row.T,
            cand_owner.T,
            cand_row,
            far_in=(0, 1, 2, 3),
            far_out=(0,),
            scratch=[
                pltpu.VMEM((1, V), I32),
                pltpu.VMEM((1, V), I32),
                pltpu.VMEM((GROUPS, V), I32),
                pltpu.VMEM((V, GROUPS * GSIZE), I32),
                pltpu.VMEM((PER * SHARDS, 128), F32),
                copies_semaphores(5),
            ],
            name="request",
        )
        arrived = swap(sent.reshape(SHARDS, 1, PER * 128), ("y", "x", "z")).reshape(PER * SHARDS, 128)
    pieces, norms = call(
        prepare_kernel, [shape((3, ROWS, D), BF16), shape((8, ROWS))], centroids, name="prepare"
    )
    with jax.named_scope("primary_rows"):
        [found] = call(
            fetch_kernel,
            [shape((COLS, 16, D))],
            arrived,
            pieces,
            *[blocks[o] for o in FIRST],
            far_in=tuple(range(2, 2 + len(FIRST))),
            far_out=(0,),
            scratch=[pltpu.VMEM((2, COLS, 8, D), F32), copies_semaphores(2)],
            name="fetch",
        )
        fetched = swap(found, plane).reshape(SLOTS, D)
    info, slots, most = call(
        slots_kernel,
        [shape((COLV, 128), I32), shape((SLOTS, COLV)), shape((8, 128), I32)],
        me,
        arrived,
        found,
        smem=(0,),
        far_in=(2,),
        scratch=[pltpu.VMEM((2, SHARDS, 128), I32)],
        name="slots",
    )
    most = most[:1, :1]
    most = jnp.maximum(most, lax.ppermute(most, "rep", [(0, 1), (1, 0)]))[0, 0]

    halves = [pltpu.VMEM((2, SLOTS // 2, D), F32), copies_semaphores(2)]
    pair = [shape((SLOTS, 2 * D))]

    def relay(base, depth):
        return call(
            relay_kernel,
            [shape((NZ * depth, SLOTS), BF16), shape((SLOTS, NZ * depth), BF16)],
            me,
            base.reshape(1),
            info,
            slots,
            smem=(0, 1),
            name="relay",
        )

    def across(base, send, *after):
        depth = send.shape[0] // NZ
        [leaving] = call(
            send_kernel,
            [shape((NZ * depth, D))],
            base.reshape(1),
            send,
            fetched,
            *after,
            smem=(0,),
            far_in=tuple(range(3, 3 + len(after))),
            far_out=(0,),
            scratch=[pltpu.VMEM((2, NZ * depth // 2, D), F32), copies_semaphores(2)],
            name="send",
        )
        return swap(leaving.reshape(NZ, depth, D), "z").reshape(NZ * depth, D)

    def add(take, got, both):
        [both] = call(
            add_kernel,
            pair,
            take,
            got,
            both,
            far_in=(2,),
            far_out=(0,),
            alias={2: 0},
            scratch=[pltpu.VMEM((SLOTS, D), F32), copies_semaphores(2)],
            name="add",
        )
        return both

    def second(state):
        base, both = state
        return base + NEXT, add(next_take, across(base, next_send), both)

    def more(state):
        base, both = state
        send, take = relay(base, K)
        return base + K, add(take, across(base, send), both)

    with jax.named_scope("vectors_out"):
        [both] = call(
            vectors_kernel,
            pair,
            me,
            slots,
            *[blocks[o] for o in (0, 1, 2, 3, 4, -3, -2, -1)],
            smem=(0,),
            far_in=tuple(range(2, 2 + NZ)),
            far_out=(0,),
            scratch=[pltpu.VMEM((COLV, D), F32), halves[0], copies_semaphores(NZ + 2)],
            name="vectors",
        )
    with jax.named_scope("primary_across"):
        send, take = relay(jnp.int32(0), K)
        got = across(jnp.int32(0), send, blocks[4], blocks[3], blocks[-3])
        next_send, next_take = relay(jnp.int32(K), NEXT)
        [both] = call(
            functools.partial(put_kernel, D),
            pair,
            take,
            got,
            both,
            far_in=(2,),
            far_out=(0,),
            alias={2: 0},
            scratch=halves,
            name="put",
        )
        state = (jnp.int32(K), both)
        state = lax.while_loop(lambda s: (s[0] == K) & (K < most), second, state)
        _, both = lax.while_loop(lambda s: s[0] < most, more, state)
    with jax.named_scope("out_to_owners"):
        both = swap(both.reshape(COLS, 16, 2 * D), plane).reshape(SLOTS, 2 * D)
    [losses] = call(
        loss_kernel, [shape((SHARDS, 128))], both, arrived, pieces, norms, name="loss"
    )
    with jax.named_scope("losses_back"):
        back = swap(losses.reshape(SHARDS, 1, 128), ("y", "x", "z")).reshape(SHARDS, 128)
    [result] = call(
        collect_kernel, [shape((V, GROUPS * GSIZE))], cand_owner, back, name="collect"
    )
    return result


def solution(mesh):
    fine = Mesh(mesh.devices.reshape(NY, NX, NZ, 2), ("y", "x", "z", "rep"))
    rows = P(("y", "x", "z", "rep"), None)
    in_specs = (rows, P(("y", "x", "z"), None), rows, rows, rows, rows)
    return jax.shard_map(shards, mesh=fine, in_specs=in_specs, out_specs=rows, check_vma=False)
```

```python
import jax
import jax.numpy as jnp
from jax import lax
from jax.experimental import pallas as pl
from jax.experimental.pallas import tpu as pltpu
from jax.sharding import Mesh, PartitionSpec as P

D = 1024
V = 32
GROUPS = 4
GSIZE = 64
ROWS = 512
NY, NX, NZ = 4, 4, 8
COLS = NY * NX
COLV = NZ * V
SLOTS = COLS * NZ * 2
SHARDS = COLS * NZ
QUARTER = SLOTS // 4
K = 32
NEXT = 8
PER = 3
FIRST = (2, -2, 1, -1)
amplify = 1.0
tiny = 1e-06

F32, BF16, I32 = jnp.float32, jnp.bfloat16, jnp.int32
VMEM = pl.BlockSpec(memory_space=pltpu.VMEM)
SMEM = pl.BlockSpec(memory_space=pltpu.SMEM)
HBM = pl.BlockSpec(memory_space=pltpu.HBM)
NN = (((1,), (0,)), ((), ()))
NT = (((1,), (1,)), ((), ()))
TN = (((0,), (0,)), ((), ()))


def call(kernel, out_shape, *operands, smem=(), far_in=(), far_out=(), scratch=(), alias=None, name=None):
    specs = [SMEM if i in smem else HBM if i in far_in else VMEM for i in range(len(operands))]
    operands = [
        pltpu.with_memory_space_constraint(a, pltpu.HBM) if i in far_in else a
        for i, a in enumerate(operands)
    ]
    out_shape = [
        pltpu.HBM(o.shape, o.dtype) if i in far_out else o for i, o in enumerate(out_shape)
    ]
    return pl.pallas_call(
        kernel,
        out_shape=out_shape,
        in_specs=specs,
        out_specs=[HBM if i in far_out else VMEM for i in range(len(out_shape))],
        scratch_shapes=list(scratch),
        input_output_aliases=alias or {},
        compiler_params=pltpu.CompilerParams(vmem_limit_bytes=24 * 2**20),
        name=name,
    )(*operands)


def copies_semaphores(n):
    return pltpu.SemaphoreType.DMA((n,))


def start_all(copies):
    for copy in copies:
        copy.start()


def wait_all(copies):
    for copy in copies:
        copy.wait()


def shape(dims, dtype=F32):
    return jax.ShapeDtypeStruct(dims, dtype)


def split3(a):
    hi = a.astype(BF16)
    rest = a - hi.astype(F32)
    mid = rest.astype(BF16)
    lo = (rest - mid.astype(F32)).astype(BF16)
    return hi, mid, lo


def dot(a, b, dims=NN):
    return lax.dot_general(a, b, dims, preferred_element_type=F32)


def pick(onehot, pieces):
    hi, mid, lo = pieces
    return dot(onehot, hi) + dot(onehot, mid) + dot(onehot, lo)


def bits(mask):
    return jnp.where(mask, 1.0, 0.0)


def iota(dims, axis):
    return lax.broadcasted_iota(I32, dims, axis)


def before_same_block(rows):
    u, w = iota((rows, rows), 0), iota((rows, rows), 1)
    return bits((w < u) & ((u >> 5) == (w >> 5))).astype(BF16)


def before_all(rows):
    return bits(iota((rows, rows), 1) < iota((rows, rows), 0)).astype(BF16)


def prepare_kernel(c_ref, pieces_ref, norms_ref):
    c = c_ref[...]
    for i, piece in enumerate(split3(c)):
        pieces_ref[i] = piece
    squares = split3(c * c)
    ones = jnp.ones((8, D), BF16)
    norms_ref[...] = sum(dot(ones, s, NT) for s in squares)


def request_kernel(owner_ref, row_ref, cand_ref, rows_ref, out_ref, owner, row, cand, rows, hold, sems):
    copies = [
        pltpu.make_async_copy(a, b, sems.at[i])
        for i, (a, b) in enumerate(
            [(owner_ref, owner), (row_ref, row), (cand_ref, cand), (rows_ref, rows)]
        )
    ]
    start_all(copies)
    shard = iota((SHARDS, V), 0)
    earlier = bits(iota((V, V), 0) < iota((V, V), 1)).astype(BF16)
    lane = iota((SHARDS, 128), 1)
    wait_all(copies)
    hit = owner[...] == shard
    rank = dot(bits(hit).astype(BF16), earlier)
    asked = row[...].astype(F32)
    asks = [
        jnp.sum(jnp.where(hit & (rank == float(k)), asked, 0.0), axis=1, keepdims=True)
        for k in range(2)
    ]
    empty = jnp.zeros((1, V), I32)
    owners = jnp.concatenate([empty, owner[...], empty, empty], axis=1).astype(F32)
    line = jnp.where(lane == 0, asks[0], jnp.where(lane == 1, asks[1], 0.0)) + owners
    hold[pl.ds(0, SHARDS, stride=PER), :] = line
    line = jnp.concatenate([cand[g : g + 1, :] for g in range(GROUPS)], axis=1).astype(F32)
    hold[pl.ds(1, SHARDS, stride=PER), :] = jnp.broadcast_to(line, (SHARDS, 128))
    hits = [cand[g : g + 1, :] == shard for g in range(GROUPS)]
    any_hit = hits[0] | hits[1] | hits[2] | hits[3]
    rank = dot(bits(any_hit).astype(BF16), earlier)
    wide = [split3(rows[:, 128 * h : 128 * h + 128].astype(F32))[:2] for h in range(2)]
    lines = []
    for k in range(2):
        sides = [jnp.zeros((SHARDS, 128), F32)] * 2
        for g in range(GROUPS):
            onehot = bits(hits[g] & (rank == float(k))).astype(BF16)
            sides[g % 2] = sides[g % 2] + dot(onehot, wide[g // 2][0]) + dot(onehot, wide[g // 2][1])
        sides[1 - k] = pltpu.roll(sides[1 - k], GSIZE, 1)
        side = even_lanes if k == 0 else odd_lanes
        lines.append(side(sides[0]) + side(sides[1]))
    hold[pl.ds(2, SHARDS, stride=PER), :] = lines[0] + lines[1]
    copy = pltpu.make_async_copy(hold, out_ref, sems.at[4])
    copy.start()
    copy.wait()


def even_lanes(a):
    return jnp.where(iota(a.shape, 1) < GSIZE, a, 0.0)


def odd_lanes(a):
    return jnp.where(iota(a.shape, 1) < GSIZE, 0.0, a)


def slots_kernel(me_ref, got_ref, found_ref, info_ref, slots_ref, most_ref, hold):
    me, column = me_ref[0], me_ref[1]
    owners = got_ref[pl.ds(0, SHARDS, stride=PER), :].astype(I32)
    cands = got_ref[pl.ds(1, SHARDS, stride=PER), :].astype(I32)
    hold[0] = owners
    hold[1] = cands
    at = pl.multiple_of(column * NZ, NZ)
    tile = jnp.concatenate([hold[0, pl.ds(at, NZ), :], hold[1, pl.ds(at, NZ), :]], axis=0)
    turned = jnp.concatenate([tile, jnp.zeros((128 - NZ * 2, 128), I32)], axis=0).T
    block_lane = iota((V, 128), 1)
    for z in range(NZ):
        block = jnp.where(block_lane == 0, turned[V : 2 * V, z : z + 1], 0)
        for g in range(GROUPS):
            cand = turned[g * V : (g + 1) * V, NZ + z : NZ + z + 1]
            block = jnp.where(block_lane == 1 + g, cand, block)
        info_ref[z * V : (z + 1) * V, :] = block
    lane = iota((COLV, 128), 1)
    hit = lane < 0
    for g in range(GROUPS):
        hit = hit | (info_ref[:, 1 + g : 2 + g] == lane * NZ + me)
    hit = hit & (lane < COLS)
    rank = dot(before_same_block(COLV), bits(hit).astype(BF16))
    mine = (iota((NZ, COLV), 1) >> 5) == iota((NZ, COLV), 0)
    for k in range(2):
        turned = bits(hit & (rank == float(k))).T
        for b in range(COLS):
            part = jnp.where(mine, turned[b : b + 1, :], 0.0)
            slots_ref[b * 16 + k * 8 : b * 16 + k * 8 + 8, :] = part
    lane = iota((SHARDS, 128), 1)
    owners = jnp.where((lane >= V) & (lane < 2 * V), owners, 0)
    owners = owners + pltpu.roll(owners, 2 * V, 1)
    owners = (owners + pltpu.roll(owners, V, 1)) & 7
    parts = []
    for b in range(NZ):
        to_plane = bits((cands & 7) == b)
        to_plane = jnp.maximum(to_plane, pltpu.roll(to_plane, 2 * V, 1))
        to_plane = jnp.maximum(to_plane, pltpu.roll(to_plane, V, 1))
        for h in range(2):
            parts.append(jnp.where(owners == (lane >> 5) + 4 * h, to_plane, 0.0).astype(BF16))
    columns = bits((iota((COLS, SHARDS), 1) >> 3) == iota((COLS, SHARDS), 0)).astype(BF16)
    group = bits((iota((128, 128), 0) >> 5) == iota((128, 128), 1)).astype(BF16)
    most = 0.0
    for part in parts:
        most = jnp.maximum(most, jnp.max(dot(dot(columns, part).astype(BF16), group)))
    most_ref[...] = jnp.full((8, 128), most, F32).astype(I32)


def relay_kernel(me_ref, turn_ref, info_ref, slots_ref, *rest):
    send_ref, take_ref = rest[-2:]
    me = me_ref[0]
    base = turn_ref[0].astype(F32)
    depth_of = send_ref.shape[0] // NZ
    lane = iota((COLV, 128), 1)
    u = iota((COLV, 1), 0)
    info = info_ref[...]
    owner = info[:, 0:1]
    hits = bits((owner == lane * NZ + me) & (lane < COLS))
    rank = dot(before_same_block(COLV), hits.astype(BF16))
    rank = jnp.sum(rank * hits, axis=1, keepdims=True)
    here = (owner & 7) == me
    wanted = lane < 0
    to_me = u < 0
    for g in range(GROUPS):
        plane = info[:, 1 + g : 2 + g] & 7
        wanted = wanted | (plane == lane)
        to_me = to_me | (plane == me)
    earlier = before_all(COLV)
    leaves = wanted & (lane < NZ) & here
    order = dot(earlier, bits(leaves).astype(BF16))
    place = jnp.where(leaves, order - base, -1.0).T
    depth = iota((depth_of, COLV), 0).astype(F32)
    rows = jnp.concatenate([bits(place[z : z + 1, :] == depth) for z in range(NZ)], axis=0)
    slot = (owner >> 3) * 16 + rank.astype(I32) * 8 + (u >> 5)
    held = bits((slot == iota((COLV, SLOTS), 1)) & here)
    send_ref[...] = dot(rows.astype(BF16), held.astype(BF16)).astype(BF16)
    comes = ((owner & 7) == lane) & (lane < NZ) & to_me
    order = dot(earlier, bits(comes).astype(BF16)) - base
    fits = comes & (order >= 0.0) & (order < float(depth_of))
    at = jnp.sum(jnp.where(fits, lane.astype(F32) * depth_of + order + 1.0, 0.0), axis=1, keepdims=True)
    found = bits(at == iota((COLV, NZ * depth_of), 1).astype(F32) + 1.0).astype(BF16)
    take_ref[...] = dot(slots_ref[...].astype(BF16), found).astype(BF16)


def fetch_kernel(got_ref, pieces_ref, *rest):
    out_ref, hold, sems = rest[-3:]
    column = iota((SHARDS, ROWS), 1)
    asked = got_ref[pl.ds(0, SHARDS, stride=PER), :].astype(I32)
    pieces = [pieces_ref[i] for i in range(3)]
    copies = []
    for k in range(2):
        onehot = bits(asked[:, k : k + 1] == column).astype(BF16)
        hold[k] = pick(onehot, pieces).reshape(COLS, 8, D)
        copies.append(
            pltpu.make_async_copy(hold.at[k], out_ref.at[:, pl.ds(k * 8, 8), :], sems.at[k])
        )
        copies[-1].start()
    wait_all(copies)


def send_kernel(base_ref, onehot_ref, in_ref, *rest):
    out_ref, hold, sems = rest[-3:]
    pieces = split3(in_ref[...])
    half = onehot_ref.shape[0] // 2
    copies = []
    for c in range(2):
        hold[c] = pick(onehot_ref[c * half : (c + 1) * half, :], pieces)
        copies.append(
            pltpu.make_async_copy(hold.at[c], out_ref.at[pl.ds(c * half, half), :], sems.at[c])
        )
        copies[-1].start()
    wait_all(copies)


def add_kernel(onehot_ref, in_ref, total_ref, out_ref, hold, sems):
    copy = pltpu.make_async_copy(out_ref, hold, sems.at[0])
    copy.start()
    copy.wait()
    hold[...] += pick(onehot_ref[...], split3(in_ref[...]))
    copy = pltpu.make_async_copy(hold, out_ref, sems.at[1])
    copy.start()
    copy.wait()


def vectors_kernel(here_ref, slots_ref, *rest):
    parts, outs, column, hold, sems = rest[:NZ], rest[-NY - 3 : -3], rest[-3], rest[-2], rest[-1]
    me, y = here_ref[0], here_ref[1]
    copies = []
    for i, part in enumerate(parts):
        at = pl.multiple_of(((me + i) & 7) * V, V)
        copies.append(pltpu.make_async_copy(part, column.at[pl.ds(at, V), :], sems.at[i]))
    start_all(copies)
    onehot = slots_ref[...].astype(BF16)
    wait_all(copies)
    hold[...] = pick(onehot, split3(column[...]))
    copies = []
    for d in range(NY):
        at = pl.multiple_of(((y + d) & 3) * QUARTER, QUARTER)
        copies.append(
            pltpu.make_async_copy(hold.at[pl.ds(at, QUARTER), :], outs[d], sems.at[NZ + d])
        )
    start_all(copies)
    wait_all(copies)


def regroup_kernel(here_ref, *rest):
    parts, outs, hold, sems = rest[:NY], rest[NY : NY + NX], rest[-2], rest[-1]
    y, x = here_ref[1], here_ref[2]
    copies = [pltpu.make_async_copy(parts[d], hold.at[d], sems.at[d]) for d in range(NY)]
    start_all(copies)
    wait_all(copies)
    copies = []
    for e in range(NX):
        source = pl.multiple_of(((x + e) & 3) * 16, 16)
        for d in range(NY):
            target = pl.multiple_of(((y - d) & 3) * 16, 16)
            copies.append(
                pltpu.make_async_copy(
                    hold.at[d, pl.ds(source, 16), :],
                    outs[e].at[pl.ds(target, 16), :],
                    sems.at[NY + e * NY + d],
                )
            )
    start_all(copies)
    wait_all(copies)


def lookup(table, rows):
    low, high = rows & 127, rows >> 7
    found = jnp.zeros(rows.shape, F32)
    for i in range(ROWS // 128):
        part = jnp.take_along_axis(table[:, 128 * i : 128 * i + 128], low, axis=1)
        found = jnp.where(high == i, part, found)
    return found


def scores(a, pieces_ref):
    hi, mid, lo = split3(a)
    chi, cmid, clo = (pieces_ref[i] for i in range(3))
    small = dot(mid, cmid, NT) + dot(lo, chi, NT) + dot(hi, clo, NT)
    return dot(hi, chi, NT) + (dot(hi, cmid, NT) + dot(mid, chi, NT) + small)


def near_kernel(here_ref, got_ref, pieces_ref, norms_ref, *rest):
    parts, x_ref, rows_ref, out_ref, sems = rest[:NX], rest[-4], rest[-3], rest[-2], rest[-1]
    x = here_ref[2]
    copies = []
    for e in range(NX):
        for y in range(NY):
            target = pl.multiple_of(y * QUARTER + ((x - e) & 3) * 16, 16)
            copies.append(
                pltpu.make_async_copy(
                    parts[e].at[pl.ds(y * 16, 16), :],
                    x_ref.at[pl.ds(target, 16), :],
                    sems.at[e * NY + y],
                )
            )
    start_all(copies)
    line = got_ref[pl.ds(2, SHARDS, stride=PER), :].astype(I32)
    rows = [line, pltpu.roll(line, GSIZE, 1)]
    rows = jnp.concatenate([a.reshape(COLS, 1, NZ, 128) for a in rows], axis=1).reshape(SLOTS, 128)
    rows = rows & (ROWS - 1)
    rows_ref[...] = rows
    wait_all(copies)
    x = x_ref[...]
    square = jnp.sum(x * x, axis=1, keepdims=True)
    out_ref[...] = lookup(square - 2.0 * scores(x, pieces_ref) + norms_ref[0:1, :], rows)


def loss_kernel(p_ref, x_ref, rows_ref, near_ref, pieces_ref, out_ref):
    x = x_ref[...]
    r = x - p_ref[...]
    hi = r.astype(BF16)
    mid = (r - hi.astype(F32)).astype(BF16)
    chi, cmid = pieces_ref[0], pieces_ref[1]
    table = dot(hi, chi, NT) + (dot(hi, cmid, NT) + dot(mid, chi, NT))
    rx = jnp.sum(r * x, axis=1, keepdims=True)
    rr = jnp.sum(r * r, axis=1, keepdims=True)
    gap = rx - lookup(table, rows_ref[...])
    loss = (near_ref[...] + amplify * gap * gap / (rr + tiny)) / D
    loss = loss.reshape(COLS, 2, NZ, 128)
    second = pltpu.roll(loss[:, 1].reshape(COLS * NZ, 128), GSIZE, 1)
    first = loss[:, 0].reshape(COLS * NZ, 128)
    out_ref[...] = jnp.where(iota((COLS * NZ, 128), 1) < GSIZE, first, second)


def collect_kernel(owner_ref, in_ref, out_ref):
    lane = iota((V, 128), 1)
    hits = [owner_ref[:, g : g + 1] == lane for g in range(GROUPS)]
    rank = dot(before_same_block(V), bits(hits[0] | hits[1] | hits[2] | hits[3]).astype(BF16))
    a = in_ref[...]
    plain, rolled = split3(a), split3(pltpu.roll(a, GSIZE, 1))
    for h in range(2):
        halves = []
        for g in (2 * h, 2 * h + 1):
            first = bits(hits[g] & (rank == 0.0)).astype(BF16)
            second = bits(hits[g] & (rank == 1.0)).astype(BF16)
            if g % 2 == 0:
                halves.append(pick(first, plain) + pick(second, rolled))
            else:
                halves.append(pick(first, rolled) + pick(second, plain))
        out_ref[:, 128 * h : 128 * h + 128] = jnp.where(lane < GSIZE, halves[0], halves[1])


def swap(a, axes):
    return lax.all_to_all(a, axes, split_axis=0, concat_axis=0, tiled=True)


def shards(new_vectors, centroids, primary_owner, primary_row, cand_owner, cand_row):
    plane = ("y", "x")
    column = lax.axis_index(("y", "x")).astype(I32)
    me = jnp.stack([lax.axis_index("z").astype(I32), column])
    here = jnp.stack([lax.axis_index(n).astype(I32) for n in ("z", "y", "x")])
    def along_z(block, step):
        return lax.ppermute(block, "z", [(z, (z - step) % NZ) for z in range(NZ)])

    with jax.named_scope("column_vectors"):
        blocks = {0: new_vectors}
        for step in (2, -2, 1, -1, 4):
            blocks[step] = along_z(new_vectors, step)
        blocks[3] = along_z(blocks[2], 1)
        blocks[-3] = along_z(blocks[-2], -1)
    with jax.named_scope("requests"):
        [sent] = call(
            request_kernel,
            [shape((PER * SHARDS, 128))],
            primary_owner.T,
            primary_row.T,
            cand_owner.T,
            cand_row,
            far_in=(0, 1, 2, 3),
            far_out=(0,),
            scratch=[
                pltpu.VMEM((1, V), I32),
                pltpu.VMEM((1, V), I32),
                pltpu.VMEM((GROUPS, V), I32),
                pltpu.VMEM((V, GROUPS * GSIZE), I32),
                pltpu.VMEM((PER * SHARDS, 128), F32),
                copies_semaphores(5),
            ],
            name="request",
        )
        arrived = swap(sent.reshape(SHARDS, 1, PER * 128), ("y", "x", "z")).reshape(PER * SHARDS, 128)
    pieces, norms = call(
        prepare_kernel, [shape((3, ROWS, D), BF16), shape((8, ROWS))], centroids, name="prepare"
    )
    with jax.named_scope("primary_rows"):
        [found] = call(
            fetch_kernel,
            [shape((COLS, 16, D))],
            arrived,
            pieces,
            *[blocks[o] for o in FIRST],
            far_in=tuple(range(2, 2 + len(FIRST))),
            far_out=(0,),
            scratch=[pltpu.VMEM((2, COLS, 8, D), F32), copies_semaphores(2)],
            name="fetch",
        )
        fetched = swap(found, plane).reshape(SLOTS, D)
    info, slots, most = call(
        slots_kernel,
        [shape((COLV, 128), I32), shape((SLOTS, COLV)), shape((8, 128), I32)],
        me,
        arrived,
        found,
        smem=(0,),
        far_in=(2,),
        scratch=[pltpu.VMEM((2, SHARDS, 128), I32)],
        name="slots",
    )
    most = most[:1, :1]
    most = jnp.maximum(most, lax.ppermute(most, "rep", [(0, 1), (1, 0)]))[0, 0]

    def relay(base, depth, *after):
        return call(
            relay_kernel,
            [shape((NZ * depth, SLOTS), BF16), shape((SLOTS, NZ * depth), BF16)],
            me,
            base.reshape(1),
            info,
            slots,
            *after,
            smem=(0, 1),
            far_in=tuple(range(4, 4 + len(after))),
            name="relay",
        )

    def move(base, onehot, source, name, *after):
        count = onehot.shape[0]
        [moved] = call(
            send_kernel,
            [shape((count, D))],
            base.reshape(1),
            onehot,
            source,
            *after,
            smem=(0,),
            far_in=tuple(range(3, 3 + len(after))),
            far_out=(0,),
            scratch=[pltpu.VMEM((2, count // 2, D), F32), copies_semaphores(2)],
            name=name,
        )
        return moved

    def across(leaving):
        return swap(leaving.reshape(NZ, -1, D), "z").reshape(-1, D)

    def add(take, got, total):
        [total] = call(
            add_kernel,
            [shape((SLOTS, D))],
            take,
            got,
            total,
            far_in=(2,),
            far_out=(0,),
            alias={2: 0},
            scratch=[pltpu.VMEM((SLOTS, D), F32), copies_semaphores(2)],
            name="add",
        )
        return total

    def second(state):
        base, total = state
        return base + NEXT, add(next_take, across(move(base, next_send, fetched, "send")), total)

    def more(state):
        base, total = state
        send, take = relay(base, K)
        return base + K, add(take, across(move(base, send, fetched, "send")), total)

    def around(block, axis, step, size):
        return lax.ppermute(block, axis, [(i, (i + step) % size) for i in range(size)])

    zero = jnp.int32(0)
    with jax.named_scope("primary_across"):
        send, take = relay(zero, K)
        leaving = move(zero, send, fetched, "send", blocks[4], blocks[3], blocks[-3])
        got = across(leaving)
    with jax.named_scope("vectors_out"):
        quarters = call(
            vectors_kernel,
            [shape((QUARTER, D))] * NY,
            here,
            slots,
            *[blocks[o] for o in (0, 1, 2, 3, 4, -3, -2, -1)],
            leaving,
            smem=(0,),
            far_in=tuple(range(2, 3 + NZ)),
            far_out=tuple(range(NY)),
            scratch=[pltpu.VMEM((COLV, D), F32), pltpu.VMEM((SLOTS, D), F32), copies_semaphores(NZ + NY)],
            name="vectors",
        )
        quarters = [quarters[0]] + [around(quarters[d], "y", d, NY) for d in range(1, NY)]
        quarters = call(
            regroup_kernel,
            [shape((QUARTER, D))] * NX,
            here,
            *quarters,
            smem=(0,),
            far_in=tuple(range(1, 1 + NY)),
            far_out=tuple(range(NX)),
            scratch=[pltpu.VMEM((NY, QUARTER, D), F32), copies_semaphores(NY + NY * NX)],
            name="regroup",
        )
        mine = quarters[0]
        quarters = [mine] + [around(quarters[e], "x", e, NX) for e in range(1, NX)]
    with jax.named_scope("primary_across"):
        next_send, next_take = relay(jnp.int32(K), NEXT, mine)
        total = move(zero, take, got, "take", mine)
        state = (jnp.int32(K), total)
        state = lax.while_loop(lambda s: (s[0] == K) & (K < most), second, state)
        _, total = lax.while_loop(lambda s: s[0] < most, more, state)
    x, rows, near = call(
        near_kernel,
        [shape((SLOTS, D)), shape((SLOTS, 128), I32), shape((SLOTS, 128))],
        here,
        arrived,
        pieces,
        norms,
        *quarters,
        smem=(0,),
        far_in=tuple(range(4, 4 + NX)),
        scratch=[copies_semaphores(NX * NY)],
        name="near",
    )
    with jax.named_scope("primaries_out"):
        primaries = swap(total.reshape(COLS, 16, D), plane).reshape(SLOTS, D)
    [losses] = call(
        loss_kernel, [shape((SHARDS, 128))], primaries, x, rows, near, pieces, name="loss"
    )
    with jax.named_scope("losses_back"):
        back = swap(losses.reshape(SHARDS, 1, 128), ("y", "x", "z")).reshape(SHARDS, 128)
    [result] = call(
        collect_kernel, [shape((V, GROUPS * GSIZE))], cand_owner, back, name="collect"
    )
    return result


def solution(mesh):
    fine = Mesh(mesh.devices.reshape(NY, NX, NZ, 2), ("y", "x", "z", "rep"))
    rows = P(("y", "x", "z", "rep"), None)
    in_specs = (rows, P(("y", "x", "z"), None), rows, rows, rows, rows)
    return jax.shard_map(shards, mesh=fine, in_specs=in_specs, out_specs=rows, check_vma=False)
```

```python
import jax
import jax.numpy as jnp
from jax import lax
from jax.experimental import pallas as pl
from jax.experimental.pallas import tpu as pltpu
from jax.sharding import Mesh, PartitionSpec as P

D = 1024
V = 32
GROUPS = 4
GSIZE = 64
ROWS = 512
NY, NX, NZ = 4, 4, 8
COLS = NY * NX
COLV = NZ * V
SLOTS = COLS * NZ * 2
SHARDS = COLS * NZ
QUARTER = SLOTS // 4
K = 32
NEXT = 8
PER = 3
FIRST = (2, -2, 1, -1)
amplify = 1.0
tiny = 1e-06

F32, BF16, I32 = jnp.float32, jnp.bfloat16, jnp.int32
VMEM = pl.BlockSpec(memory_space=pltpu.VMEM)
SMEM = pl.BlockSpec(memory_space=pltpu.SMEM)
HBM = pl.BlockSpec(memory_space=pltpu.HBM)
ANY = pl.BlockSpec(memory_space=pl.ANY)
NN = (((1,), (0,)), ((), ()))
NT = (((1,), (1,)), ((), ()))
TN = (((0,), (0,)), ((), ()))


def call(kernel, out_shape, *operands, smem=(), any_in=(), far_in=(), far_out=(), scratch=(), alias=None, name=None):
    specs = [
        SMEM if i in smem else ANY if i in any_in else HBM if i in far_in else VMEM
        for i in range(len(operands))
    ]
    operands = [
        pltpu.with_memory_space_constraint(a, pltpu.HBM) if i in far_in else a
        for i, a in enumerate(operands)
    ]
    out_shape = [
        pltpu.HBM(o.shape, o.dtype) if i in far_out else o for i, o in enumerate(out_shape)
    ]
    return pl.pallas_call(
        kernel,
        out_shape=out_shape,
        in_specs=specs,
        out_specs=[HBM if i in far_out else VMEM for i in range(len(out_shape))],
        scratch_shapes=list(scratch),
        input_output_aliases=alias or {},
        compiler_params=pltpu.CompilerParams(vmem_limit_bytes=24 * 2**20),
        name=name,
    )(*operands)


def copies_semaphores(n):
    return pltpu.SemaphoreType.DMA((n,))


def start_all(copies):
    for copy in copies:
        copy.start()


def wait_all(copies):
    for copy in copies:
        copy.wait()


def shape(dims, dtype=F32):
    return jax.ShapeDtypeStruct(dims, dtype)


def split3(a):
    hi = a.astype(BF16)
    rest = a - hi.astype(F32)
    mid = rest.astype(BF16)
    lo = (rest - mid.astype(F32)).astype(BF16)
    return hi, mid, lo


def dot(a, b, dims=NN):
    return lax.dot_general(a, b, dims, preferred_element_type=F32)


def pick(onehot, pieces):
    hi, mid, lo = pieces
    return dot(onehot, hi) + dot(onehot, mid) + dot(onehot, lo)


def bits(mask):
    return jnp.where(mask, 1.0, 0.0)


def iota(dims, axis):
    return lax.broadcasted_iota(I32, dims, axis)


def before_same_block(rows):
    u, w = iota((rows, rows), 0), iota((rows, rows), 1)
    return bits((w < u) & ((u >> 5) == (w >> 5))).astype(BF16)


def before_all(rows):
    return bits(iota((rows, rows), 1) < iota((rows, rows), 0)).astype(BF16)


def prepare_kernel(c_ref, pieces_ref, norms_ref):
    c = c_ref[...]
    for i, piece in enumerate(split3(c)):
        pieces_ref[i] = piece
    squares = split3(c * c)
    ones = jnp.ones((8, D), BF16)
    norms_ref[...] = sum(dot(ones, s, NT) for s in squares)


def request_kernel(owner_ref, row_ref, cand_ref, rows_ref, out_ref, owner, row, cand, rows, hold, sems):
    copies = [
        pltpu.make_async_copy(a, b, sems.at[i])
        for i, (a, b) in enumerate(
            [(owner_ref, owner), (row_ref, row), (cand_ref, cand), (rows_ref, rows)]
        )
    ]
    start_all(copies)
    shard = iota((SHARDS, V), 0)
    earlier = bits(iota((V, V), 0) < iota((V, V), 1)).astype(BF16)
    lane = iota((SHARDS, 128), 1)
    wait_all(copies)
    hit = owner[...] == shard
    rank = dot(bits(hit).astype(BF16), earlier)
    asked = row[...].astype(F32)
    asks = [
        jnp.sum(jnp.where(hit & (rank == float(k)), asked, 0.0), axis=1, keepdims=True)
        for k in range(2)
    ]
    empty = jnp.zeros((1, V), I32)
    owners = jnp.concatenate([empty, owner[...], empty, empty], axis=1).astype(F32)
    line = jnp.where(lane == 0, asks[0], jnp.where(lane == 1, asks[1], 0.0)) + owners
    hold[pl.ds(0, SHARDS, stride=PER), :] = line
    line = jnp.concatenate([cand[g : g + 1, :] for g in range(GROUPS)], axis=1).astype(F32)
    hold[pl.ds(1, SHARDS, stride=PER), :] = jnp.broadcast_to(line, (SHARDS, 128))
    hits = [cand[g : g + 1, :] == shard for g in range(GROUPS)]
    any_hit = hits[0] | hits[1] | hits[2] | hits[3]
    rank = dot(bits(any_hit).astype(BF16), earlier)
    wide = [split3(rows[:, 128 * h : 128 * h + 128].astype(F32))[:2] for h in range(2)]
    lines = []
    for k in range(2):
        sides = [jnp.zeros((SHARDS, 128), F32)] * 2
        for g in range(GROUPS):
            onehot = bits(hits[g] & (rank == float(k))).astype(BF16)
            sides[g % 2] = sides[g % 2] + dot(onehot, wide[g // 2][0]) + dot(onehot, wide[g // 2][1])
        sides[1 - k] = pltpu.roll(sides[1 - k], GSIZE, 1)
        side = even_lanes if k == 0 else odd_lanes
        lines.append(side(sides[0]) + side(sides[1]))
    hold[pl.ds(2, SHARDS, stride=PER), :] = lines[0] + lines[1]
    copy = pltpu.make_async_copy(hold, out_ref, sems.at[4])
    copy.start()
    copy.wait()


def even_lanes(a):
    return jnp.where(iota(a.shape, 1) < GSIZE, a, 0.0)


def odd_lanes(a):
    return jnp.where(iota(a.shape, 1) < GSIZE, 0.0, a)


def slots_kernel(me_ref, got_ref, found_ref, info_ref, slots_ref, most_ref, hold):
    me, column = me_ref[0], me_ref[1]
    owners = got_ref[pl.ds(0, SHARDS, stride=PER), :].astype(I32)
    cands = got_ref[pl.ds(1, SHARDS, stride=PER), :].astype(I32)
    hold[0] = owners
    hold[1] = cands
    at = pl.multiple_of(column * NZ, NZ)
    tile = jnp.concatenate([hold[0, pl.ds(at, NZ), :], hold[1, pl.ds(at, NZ), :]], axis=0)
    turned = jnp.concatenate([tile, jnp.zeros((128 - NZ * 2, 128), I32)], axis=0).T
    block_lane = iota((V, 128), 1)
    for z in range(NZ):
        block = jnp.where(block_lane == 0, turned[V : 2 * V, z : z + 1], 0)
        for g in range(GROUPS):
            cand = turned[g * V : (g + 1) * V, NZ + z : NZ + z + 1]
            block = jnp.where(block_lane == 1 + g, cand, block)
        info_ref[z * V : (z + 1) * V, :] = block
    lane = iota((COLV, 128), 1)
    hit = lane < 0
    for g in range(GROUPS):
        hit = hit | (info_ref[:, 1 + g : 2 + g] == lane * NZ + me)
    hit = hit & (lane < COLS)
    rank = dot(before_same_block(COLV), bits(hit).astype(BF16))
    mine = (iota((NZ, COLV), 1) >> 5) == iota((NZ, COLV), 0)
    for k in range(2):
        turned = bits(hit & (rank == float(k))).T
        for b in range(COLS):
            part = jnp.where(mine, turned[b : b + 1, :], 0.0)
            slots_ref[b * 16 + k * 8 : b * 16 + k * 8 + 8, :] = part
    lane = iota((SHARDS, 128), 1)
    owners = jnp.where((lane >= V) & (lane < 2 * V), owners, 0)
    owners = owners + pltpu.roll(owners, 2 * V, 1)
    owners = (owners + pltpu.roll(owners, V, 1)) & 7
    parts = []
    for b in range(NZ):
        to_plane = bits((cands & 7) == b)
        to_plane = jnp.maximum(to_plane, pltpu.roll(to_plane, 2 * V, 1))
        to_plane = jnp.maximum(to_plane, pltpu.roll(to_plane, V, 1))
        for h in range(2):
            parts.append(jnp.where(owners == (lane >> 5) + 4 * h, to_plane, 0.0).astype(BF16))
    columns = bits((iota((COLS, SHARDS), 1) >> 3) == iota((COLS, SHARDS), 0)).astype(BF16)
    group = bits((iota((128, 128), 0) >> 5) == iota((128, 128), 1)).astype(BF16)
    most = 0.0
    for part in parts:
        most = jnp.maximum(most, jnp.max(dot(dot(columns, part).astype(BF16), group)))
    most_ref[...] = jnp.full((8, 128), most, F32).astype(I32)


def relay_kernel(me_ref, turn_ref, info_ref, slots_ref, *rest):
    send_ref, take_ref = rest[-2:]
    me = me_ref[0]
    base = turn_ref[0].astype(F32)
    depth_of = send_ref.shape[0] // NZ
    lane = iota((COLV, 128), 1)
    u = iota((COLV, 1), 0)
    info = info_ref[...]
    owner = info[:, 0:1]
    hits = bits((owner == lane * NZ + me) & (lane < COLS))
    rank = dot(before_same_block(COLV), hits.astype(BF16))
    rank = jnp.sum(rank * hits, axis=1, keepdims=True)
    here = (owner & 7) == me
    wanted = lane < 0
    to_me = u < 0
    for g in range(GROUPS):
        plane = info[:, 1 + g : 2 + g] & 7
        wanted = wanted | (plane == lane)
        to_me = to_me | (plane == me)
    earlier = before_all(COLV)
    leaves = wanted & (lane < NZ) & here
    order = dot(earlier, bits(leaves).astype(BF16))
    place = jnp.where(leaves, order - base, -1.0).T
    depth = iota((depth_of, COLV), 0).astype(F32)
    rows = jnp.concatenate([bits(place[z : z + 1, :] == depth) for z in range(NZ)], axis=0)
    slot = (owner >> 3) * 16 + rank.astype(I32) * 8 + (u >> 5)
    held = bits((slot == iota((COLV, SLOTS), 1)) & here)
    send_ref[...] = dot(rows.astype(BF16), held.astype(BF16)).astype(BF16)
    comes = ((owner & 7) == lane) & (lane < NZ) & to_me
    order = dot(earlier, bits(comes).astype(BF16)) - base
    fits = comes & (order >= 0.0) & (order < float(depth_of))
    at = jnp.sum(jnp.where(fits, lane.astype(F32) * depth_of + order + 1.0, 0.0), axis=1, keepdims=True)
    found = bits(at == iota((COLV, NZ * depth_of), 1).astype(F32) + 1.0).astype(BF16)
    take_ref[...] = dot(slots_ref[...].astype(BF16), found).astype(BF16)


def fetch_kernel(got_ref, pieces_ref, *rest):
    out_ref, hold, sems = rest[-3:]
    column = iota((SHARDS, ROWS), 1)
    asked = got_ref[pl.ds(0, SHARDS, stride=PER), :].astype(I32)
    pieces = [pieces_ref[i] for i in range(3)]
    copies = []
    for k in range(2):
        onehot = bits(asked[:, k : k + 1] == column).astype(BF16)
        hold[k] = pick(onehot, pieces).reshape(COLS, 8, D)
        copies.append(
            pltpu.make_async_copy(hold.at[k], out_ref.at[:, pl.ds(k * 8, 8), :], sems.at[k])
        )
        copies[-1].start()
    wait_all(copies)


def send_kernel(base_ref, onehot_ref, in_ref, *rest):
    out_ref, hold, sems = rest[-3:]
    pieces = split3(in_ref[...])
    half = onehot_ref.shape[0] // 2
    copies = []
    for c in range(2):
        hold[c] = pick(onehot_ref[c * half : (c + 1) * half, :], pieces)
        copies.append(
            pltpu.make_async_copy(hold.at[c], out_ref.at[pl.ds(c * half, half), :], sems.at[c])
        )
        copies[-1].start()
    wait_all(copies)


def add_kernel(onehot_ref, in_ref, total_ref, out_ref, hold, sems):
    copy = pltpu.make_async_copy(out_ref, hold, sems.at[0])
    copy.start()
    copy.wait()
    hold[...] += pick(onehot_ref[...], split3(in_ref[...]))
    copy = pltpu.make_async_copy(hold, out_ref, sems.at[1])
    copy.start()
    copy.wait()


def vectors_kernel(here_ref, slots_ref, *rest):
    parts, outs, column, hold, sems = rest[:NZ], rest[-NY - 3 : -3], rest[-3], rest[-2], rest[-1]
    me, y = here_ref[0], here_ref[1]
    copies = []
    for i, part in enumerate(parts):
        at = pl.multiple_of(((me + i) & 7) * V, V)
        copies.append(pltpu.make_async_copy(part, column.at[pl.ds(at, V), :], sems.at[i]))
    start_all(copies)
    onehot = slots_ref[...].astype(BF16)
    wait_all(copies)
    hold[...] = pick(onehot, split3(column[...]))
    copies = []
    for d in range(NY):
        at = pl.multiple_of(((y + d) & 3) * QUARTER, QUARTER)
        copies.append(
            pltpu.make_async_copy(hold.at[pl.ds(at, QUARTER), :], outs[d], sems.at[NZ + d])
        )
    start_all(copies)
    wait_all(copies)


def regroup_kernel(here_ref, *rest):
    parts, outs, hold, sems = rest[:NY], rest[NY : NY + NX], rest[-2], rest[-1]
    y, x = here_ref[1], here_ref[2]
    copies = [pltpu.make_async_copy(parts[d], hold.at[d], sems.at[d]) for d in range(NY)]
    start_all(copies)
    wait_all(copies)
    copies = []
    for e in range(NX):
        source = pl.multiple_of(((x + e) & 3) * 16, 16)
        for d in range(NY):
            target = pl.multiple_of(((y - d) & 3) * 16, 16)
            copies.append(
                pltpu.make_async_copy(
                    hold.at[d, pl.ds(source, 16), :],
                    outs[e].at[pl.ds(target, 16), :],
                    sems.at[NY + e * NY + d],
                )
            )
    start_all(copies)
    wait_all(copies)


def lookup(table, rows):
    low, high = rows & 127, rows >> 7
    found = jnp.zeros(rows.shape, F32)
    for i in range(ROWS // 128):
        part = jnp.take_along_axis(table[:, 128 * i : 128 * i + 128], low, axis=1)
        found = jnp.where(high == i, part, found)
    return found


def scores(a, pieces_ref):
    hi, mid, lo = split3(a)
    chi, cmid, clo = (pieces_ref[i] for i in range(3))
    small = dot(mid, cmid, NT) + dot(lo, chi, NT) + dot(hi, clo, NT)
    return dot(hi, chi, NT) + (dot(hi, cmid, NT) + dot(mid, chi, NT) + small)


def near_kernel(here_ref, got_ref, pieces_ref, norms_ref, *rest):
    parts, out_ref, near_ref, x_all, near, sems = rest[:NX], *rest[-5:]
    x = here_ref[2]
    copies = []
    for e in range(NX):
        for y in range(NY):
            target = pl.multiple_of(y * QUARTER + ((x - e) & 3) * 16, 16)
            copies.append(
                pltpu.make_async_copy(
                    parts[e].at[pl.ds(y * 16, 16), :],
                    x_all.at[pl.ds(target, 16), :],
                    sems.at[e * NY + y],
                )
            )
    start_all(copies)
    line = got_ref[pl.ds(2, SHARDS, stride=PER), :].astype(I32)
    rows = [line, pltpu.roll(line, GSIZE, 1)]
    rows = jnp.concatenate([a.reshape(COLS, 1, NZ, 128) for a in rows], axis=1).reshape(SLOTS, 128)
    rows = rows & (ROWS - 1)
    near[:, 128:] = rows.astype(F32)
    wait_all(copies)
    ends = [pltpu.make_async_copy(x_all, out_ref, sems.at[NX * NY])]
    ends[0].start()
    x = x_all[...]
    square = jnp.sum(x * x, axis=1, keepdims=True)
    near[:, :128] = lookup(square - 2.0 * scores(x, pieces_ref) + norms_ref[0:1, :], rows)
    ends.append(pltpu.make_async_copy(near, near_ref, sems.at[NX * NY + 1]))
    ends[1].start()
    wait_all(ends)


def loss_kernel(p_ref, x_ref, near_ref, pieces_ref, out_ref, p_half, x_half, near, sems):
    copies = []
    for c in range(2):
        cut = pl.ds(c * D // 2, D // 2)
        copies.append(pltpu.make_async_copy(p_ref.at[:, cut], p_half.at[c], sems.at[2 * c]))
        copies.append(pltpu.make_async_copy(x_ref.at[:, cut], x_half.at[c], sems.at[2 * c + 1]))
    copies.append(pltpu.make_async_copy(near_ref, near, sems.at[4]))
    start_all(copies)
    table, rx, rr = 0.0, 0.0, 0.0
    for c in range(2):
        wait_all(copies[2 * c : 2 * c + 2])
        x = x_half[c]
        r = x - p_half[c]
        hi = r.astype(BF16)
        mid = (r - hi.astype(F32)).astype(BF16)
        cut = slice(c * D // 2, (c + 1) * D // 2)
        chi, cmid = pieces_ref[0, :, cut], pieces_ref[1, :, cut]
        table = table + (dot(hi, chi, NT) + (dot(hi, cmid, NT) + dot(mid, chi, NT)))
        rx = rx + jnp.sum(r * x, axis=1, keepdims=True)
        rr = rr + jnp.sum(r * r, axis=1, keepdims=True)
    copies[4].wait()
    gap = rx - lookup(table, near[:, 128:].astype(I32))
    loss = (near[:, :128] + amplify * gap * gap / (rr + tiny)) / D
    loss = loss.reshape(COLS, 2, NZ, 128)
    second = pltpu.roll(loss[:, 1].reshape(COLS * NZ, 128), GSIZE, 1)
    first = loss[:, 0].reshape(COLS * NZ, 128)
    out_ref[...] = jnp.where(iota((COLS * NZ, 128), 1) < GSIZE, first, second)


def collect_kernel(owner_ref, in_ref, out_ref):
    lane = iota((V, 128), 1)
    hits = [owner_ref[:, g : g + 1] == lane for g in range(GROUPS)]
    rank = dot(before_same_block(V), bits(hits[0] | hits[1] | hits[2] | hits[3]).astype(BF16))
    a = in_ref[...]
    plain, rolled = split3(a), split3(pltpu.roll(a, GSIZE, 1))
    for h in range(2):
        halves = []
        for g in (2 * h, 2 * h + 1):
            first = bits(hits[g] & (rank == 0.0)).astype(BF16)
            second = bits(hits[g] & (rank == 1.0)).astype(BF16)
            if g % 2 == 0:
                halves.append(pick(first, plain) + pick(second, rolled))
            else:
                halves.append(pick(first, rolled) + pick(second, plain))
        out_ref[:, 128 * h : 128 * h + 128] = jnp.where(lane < GSIZE, halves[0], halves[1])


def swap(a, axes):
    return lax.all_to_all(a, axes, split_axis=0, concat_axis=0, tiled=True)


def shards(new_vectors, centroids, primary_owner, primary_row, cand_owner, cand_row):
    plane = ("y", "x")
    column = lax.axis_index(("y", "x")).astype(I32)
    me = jnp.stack([lax.axis_index("z").astype(I32), column])
    here = jnp.stack([lax.axis_index(n).astype(I32) for n in ("z", "y", "x")])
    def along_z(block, step):
        return lax.ppermute(block, "z", [(z, (z - step) % NZ) for z in range(NZ)])

    with jax.named_scope("column_vectors"):
        blocks = {0: new_vectors}
        for step in (2, -2, 1, -1, 4):
            blocks[step] = along_z(new_vectors, step)
        blocks[3] = along_z(blocks[2], 1)
        blocks[-3] = along_z(blocks[-2], -1)
    with jax.named_scope("requests"):
        [sent] = call(
            request_kernel,
            [shape((PER * SHARDS, 128))],
            primary_owner.T,
            primary_row.T,
            cand_owner.T,
            cand_row,
            far_in=(0, 1, 2, 3),
            far_out=(0,),
            scratch=[
                pltpu.VMEM((1, V), I32),
                pltpu.VMEM((1, V), I32),
                pltpu.VMEM((GROUPS, V), I32),
                pltpu.VMEM((V, GROUPS * GSIZE), I32),
                pltpu.VMEM((PER * SHARDS, 128), F32),
                copies_semaphores(5),
            ],
            name="request",
        )
        arrived = swap(sent.reshape(SHARDS, 1, PER * 128), ("y", "x", "z")).reshape(PER * SHARDS, 128)
    pieces, norms = call(
        prepare_kernel, [shape((3, ROWS, D), BF16), shape((8, ROWS))], centroids, name="prepare"
    )
    with jax.named_scope("primary_rows"):
        [found] = call(
            fetch_kernel,
            [shape((COLS, 16, D))],
            arrived,
            pieces,
            *[blocks[o] for o in FIRST],
            any_in=tuple(range(2, 2 + len(FIRST))),
            far_out=(0,),
            scratch=[pltpu.VMEM((2, COLS, 8, D), F32), copies_semaphores(2)],
            name="fetch",
        )
        fetched = swap(found, plane).reshape(SLOTS, D)
    info, slots, most = call(
        slots_kernel,
        [shape((COLV, 128), I32), shape((SLOTS, COLV)), shape((8, 128), I32)],
        me,
        arrived,
        found,
        smem=(0,),
        far_in=(2,),
        scratch=[pltpu.VMEM((2, SHARDS, 128), I32)],
        name="slots",
    )
    most = most[:1, :1]
    most = jnp.maximum(most, lax.ppermute(most, "rep", [(0, 1), (1, 0)]))[0, 0]

    def relay(base, depth, *after):
        return call(
            relay_kernel,
            [shape((NZ * depth, SLOTS), BF16), shape((SLOTS, NZ * depth), BF16)],
            me,
            base.reshape(1),
            info,
            slots,
            *after,
            smem=(0, 1),
            any_in=tuple(range(4, 4 + len(after))),
            name="relay",
        )

    def move(base, onehot, source, name, *after):
        count = onehot.shape[0]
        [moved] = call(
            send_kernel,
            [shape((count, D))],
            base.reshape(1),
            onehot,
            source,
            *after,
            smem=(0,),
            any_in=tuple(range(3, 3 + len(after))),
            far_out=(0,),
            scratch=[pltpu.VMEM((2, count // 2, D), F32), copies_semaphores(2)],
            name=name,
        )
        return moved

    def across(leaving):
        return swap(leaving.reshape(NZ, -1, D), "z").reshape(-1, D)

    def add(take, got, total):
        [total] = call(
            add_kernel,
            [shape((SLOTS, D))],
            take,
            got,
            total,
            far_in=(2,),
            far_out=(0,),
            alias={2: 0},
            scratch=[pltpu.VMEM((SLOTS, D), F32), copies_semaphores(2)],
            name="add",
        )
        return total

    def second(state):
        base, total = state
        send, take = relay(base, NEXT)
        return base + NEXT, add(take, across(move(base, send, fetched, "send")), total)

    def more(state):
        base, total = state
        send, take = relay(base, K)
        return base + K, add(take, across(move(base, send, fetched, "send")), total)

    def around(block, axis, step, size):
        return lax.ppermute(block, axis, [(i, (i + step) % size) for i in range(size)])

    zero = jnp.int32(0)
    with jax.named_scope("primary_across"):
        send, take = relay(zero, K)
        leaving = move(zero, send, fetched, "send", blocks[4], blocks[3], blocks[-3])
        got = across(leaving)
    with jax.named_scope("vectors_out"):
        quarters = call(
            vectors_kernel,
            [shape((QUARTER, D))] * NY,
            here,
            slots,
            *[blocks[o] for o in (0, 1, 2, 3, 4, -3, -2, -1)],
            leaving,
            smem=(0,),
            any_in=tuple(range(2, 3 + NZ)),
            far_out=tuple(range(NY)),
            scratch=[pltpu.VMEM((COLV, D), F32), pltpu.VMEM((SLOTS, D), F32), copies_semaphores(NZ + NY)],
            name="vectors",
        )
        quarters = [quarters[0]] + [around(quarters[d], "y", d, NY) for d in range(1, NY)]
        quarters = call(
            regroup_kernel,
            [shape((QUARTER, D))] * NX,
            here,
            *quarters,
            smem=(0,),
            any_in=tuple(range(1, 1 + NY)),
            far_out=tuple(range(NX)),
            scratch=[pltpu.VMEM((NY, QUARTER, D), F32), copies_semaphores(NY + NY * NX)],
            name="regroup",
        )
        quarters = [quarters[0]] + [around(quarters[e], "x", e, NX) for e in range(1, NX)]
    with jax.named_scope("primary_across"):
        total = move(zero, take, got, "take", *quarters)
        state = (jnp.int32(K), total)
        state = lax.while_loop(lambda s: (s[0] == K) & (K < most), second, state)
        _, total = lax.while_loop(lambda s: s[0] < most, more, state)
    x, near = call(
        near_kernel,
        [shape((SLOTS, D)), shape((SLOTS, 256))],
        here,
        arrived,
        pieces,
        norms,
        *quarters,
        smem=(0,),
        any_in=tuple(range(4, 4 + NX)),
        far_out=(0, 1),
        scratch=[
            pltpu.VMEM((SLOTS, D), F32),
            pltpu.VMEM((SLOTS, 256), F32),
            copies_semaphores(NX * NY + 2),
        ],
        name="near",
    )
    with jax.named_scope("primaries_out"):
        primaries = swap(total.reshape(COLS, 16, D), plane).reshape(SLOTS, D)
    [losses] = call(
        loss_kernel,
        [shape((SHARDS, 128))],
        primaries,
        x,
        near,
        pieces,
        any_in=(0,),
        far_in=(1, 2),
        scratch=[
            pltpu.VMEM((2, SLOTS, D // 2), F32),
            pltpu.VMEM((2, SLOTS, D // 2), F32),
            pltpu.VMEM((SLOTS, 256), F32),
            copies_semaphores(5),
        ],
        name="loss",
    )
    with jax.named_scope("losses_back"):
        back = swap(losses.reshape(SHARDS, 1, 128), ("y", "x", "z")).reshape(SHARDS, 128)
    [result] = call(
        collect_kernel, [shape((V, GROUPS * GSIZE))], cand_owner, back, name="collect"
    )
    return result


def solution(mesh):
    fine = Mesh(mesh.devices.reshape(NY, NX, NZ, 2), ("y", "x", "z", "rep"))
    rows = P(("y", "x", "z", "rep"), None)
    in_specs = (rows, P(("y", "x", "z"), None), rows, rows, rows, rows)
    return jax.shard_map(shards, mesh=fine, in_specs=in_specs, out_specs=rows, check_vma=False)
```

```python
import functools

import jax
import jax.numpy as jnp
from jax import lax
from jax.experimental import pallas as pl
from jax.experimental.pallas import tpu as pltpu
from jax.sharding import Mesh, PartitionSpec as P

D = 1024
V = 32
GROUPS = 4
GSIZE = 64
ROWS = 512
NY, NX, NZ = 4, 4, 8
COLS = NY * NX
COLV = NZ * V
SLOTS = COLS * NZ * 2
SHARDS = COLS * NZ
K = 32
NEXT = 8
PER = 3
FIRST = (2, -2)
amplify = 1.0
tiny = 1e-06

F32, BF16, I32 = jnp.float32, jnp.bfloat16, jnp.int32
VMEM = pl.BlockSpec(memory_space=pltpu.VMEM)
SMEM = pl.BlockSpec(memory_space=pltpu.SMEM)
HBM = pl.BlockSpec(memory_space=pltpu.HBM)
NN = (((1,), (0,)), ((), ()))
NT = (((1,), (1,)), ((), ()))
TN = (((0,), (0,)), ((), ()))


def call(kernel, out_shape, *operands, smem=(), far_in=(), far_out=(), scratch=(), alias=None, name=None):
    specs = [SMEM if i in smem else HBM if i in far_in else VMEM for i in range(len(operands))]
    operands = [
        pltpu.with_memory_space_constraint(a, pltpu.HBM) if i in far_in else a
        for i, a in enumerate(operands)
    ]
    out_shape = [
        pltpu.HBM(o.shape, o.dtype) if i in far_out else o for i, o in enumerate(out_shape)
    ]
    return pl.pallas_call(
        kernel,
        out_shape=out_shape,
        in_specs=specs,
        out_specs=[HBM if i in far_out else VMEM for i in range(len(out_shape))],
        scratch_shapes=list(scratch),
        input_output_aliases=alias or {},
        compiler_params=pltpu.CompilerParams(vmem_limit_bytes=24 * 2**20),
        name=name,
    )(*operands)


def copies_semaphores(n):
    return pltpu.SemaphoreType.DMA((n,))


def start_all(copies):
    for copy in copies:
        copy.start()


def wait_all(copies):
    for copy in copies:
        copy.wait()


def shape(dims, dtype=F32):
    return jax.ShapeDtypeStruct(dims, dtype)


def split3(a):
    hi = a.astype(BF16)
    rest = a - hi.astype(F32)
    mid = rest.astype(BF16)
    lo = (rest - mid.astype(F32)).astype(BF16)
    return hi, mid, lo


def dot(a, b, dims=NN):
    return lax.dot_general(a, b, dims, preferred_element_type=F32)


def pick(onehot, pieces):
    hi, mid, lo = pieces
    return dot(onehot, hi) + dot(onehot, mid) + dot(onehot, lo)


def bits(mask):
    return jnp.where(mask, 1.0, 0.0)


def iota(dims, axis):
    return lax.broadcasted_iota(I32, dims, axis)


def before_same_block(rows):
    u, w = iota((rows, rows), 0), iota((rows, rows), 1)
    return bits((w < u) & ((u >> 5) == (w >> 5))).astype(BF16)


def before_all(rows):
    return bits(iota((rows, rows), 1) < iota((rows, rows), 0)).astype(BF16)


def prepare_kernel(c_ref, pieces_ref, norms_ref):
    c = c_ref[...]
    for i, piece in enumerate(split3(c)):
        pieces_ref[i] = piece
    squares = split3(c * c)
    ones = jnp.ones((8, D), BF16)
    norms_ref[...] = sum(dot(ones, s, NT) for s in squares)


def request_kernel(owner_ref, row_ref, cand_ref, rows_ref, out_ref, owner, row, cand, rows, hold, sems):
    copies = [
        pltpu.make_async_copy(a, b, sems.at[i])
        for i, (a, b) in enumerate(
            [(owner_ref, owner), (row_ref, row), (cand_ref, cand), (rows_ref, rows)]
        )
    ]
    start_all(copies)
    shard = iota((SHARDS, V), 0)
    earlier = bits(iota((V, V), 0) < iota((V, V), 1)).astype(BF16)
    lane = iota((SHARDS, 128), 1)
    wait_all(copies)
    hit = owner[...] == shard
    rank = dot(bits(hit).astype(BF16), earlier)
    asked = row[...].astype(F32)
    asks = [
        jnp.sum(jnp.where(hit & (rank == float(k)), asked, 0.0), axis=1, keepdims=True)
        for k in range(2)
    ]
    empty = jnp.zeros((1, V), I32)
    owners = jnp.concatenate([empty, owner[...], empty, empty], axis=1).astype(F32)
    line = jnp.where(lane == 0, asks[0], jnp.where(lane == 1, asks[1], 0.0)) + owners
    hold[pl.ds(0, SHARDS, stride=PER), :] = line
    line = jnp.concatenate([cand[g : g + 1, :] for g in range(GROUPS)], axis=1).astype(F32)
    hold[pl.ds(1, SHARDS, stride=PER), :] = jnp.broadcast_to(line, (SHARDS, 128))
    hits = [cand[g : g + 1, :] == shard for g in range(GROUPS)]
    any_hit = hits[0] | hits[1] | hits[2] | hits[3]
    rank = dot(bits(any_hit).astype(BF16), earlier)
    wide = [split3(rows[:, 128 * h : 128 * h + 128].astype(F32))[:2] for h in range(2)]
    lines = []
    for k in range(2):
        sides = [jnp.zeros((SHARDS, 128), F32)] * 2
        for g in range(GROUPS):
            onehot = bits(hits[g] & (rank == float(k))).astype(BF16)
            sides[g % 2] = sides[g % 2] + dot(onehot, wide[g // 2][0]) + dot(onehot, wide[g // 2][1])
        sides[1 - k] = pltpu.roll(sides[1 - k], GSIZE, 1)
        side = even_lanes if k == 0 else odd_lanes
        lines.append(side(sides[0]) + side(sides[1]))
    hold[pl.ds(2, SHARDS, stride=PER), :] = lines[0] + lines[1]
    copy = pltpu.make_async_copy(hold, out_ref, sems.at[4])
    copy.start()
    copy.wait()


def even_lanes(a):
    return jnp.where(iota(a.shape, 1) < GSIZE, a, 0.0)


def odd_lanes(a):
    return jnp.where(iota(a.shape, 1) < GSIZE, 0.0, a)


def slots_kernel(me_ref, got_ref, found_ref, info_ref, slots_ref, most_ref, hold):
    me, column = me_ref[0], me_ref[1]
    owners = got_ref[pl.ds(0, SHARDS, stride=PER), :].astype(I32)
    cands = got_ref[pl.ds(1, SHARDS, stride=PER), :].astype(I32)
    hold[0] = owners
    hold[1] = cands
    at = pl.multiple_of(column * NZ, NZ)
    tile = jnp.concatenate([hold[0, pl.ds(at, NZ), :], hold[1, pl.ds(at, NZ), :]], axis=0)
    turned = jnp.concatenate([tile, jnp.zeros((128 - NZ * 2, 128), I32)], axis=0).T
    block_lane = iota((V, 128), 1)
    for z in range(NZ):
        block = jnp.where(block_lane == 0, turned[V : 2 * V, z : z + 1], 0)
        for g in range(GROUPS):
            cand = turned[g * V : (g + 1) * V, NZ + z : NZ + z + 1]
            block = jnp.where(block_lane == 1 + g, cand, block)
        info_ref[z * V : (z + 1) * V, :] = block
    lane = iota((COLV, 128), 1)
    hit = lane < 0
    for g in range(GROUPS):
        hit = hit | (info_ref[:, 1 + g : 2 + g] == lane * NZ + me)
    hit = hit & (lane < COLS)
    rank = dot(before_same_block(COLV), bits(hit).astype(BF16))
    mine = (iota((NZ, COLV), 1) >> 5) == iota((NZ, COLV), 0)
    for k in range(2):
        turned = bits(hit & (rank == float(k))).T
        for b in range(COLS):
            part = jnp.where(mine, turned[b : b + 1, :], 0.0)
            slots_ref[b * 16 + k * 8 : b * 16 + k * 8 + 8, :] = part
    lane = iota((SHARDS, 128), 1)
    owners = jnp.where((lane >= V) & (lane < 2 * V), owners, 0)
    owners = owners + pltpu.roll(owners, 2 * V, 1)
    owners = (owners + pltpu.roll(owners, V, 1)) & 7
    parts = []
    for b in range(NZ):
        to_plane = bits((cands & 7) == b)
        to_plane = jnp.maximum(to_plane, pltpu.roll(to_plane, 2 * V, 1))
        to_plane = jnp.maximum(to_plane, pltpu.roll(to_plane, V, 1))
        for h in range(2):
            parts.append(jnp.where(owners == (lane >> 5) + 4 * h, to_plane, 0.0).astype(BF16))
    columns = bits((iota((COLS, SHARDS), 1) >> 3) == iota((COLS, SHARDS), 0)).astype(BF16)
    group = bits((iota((128, 128), 0) >> 5) == iota((128, 128), 1)).astype(BF16)
    most = 0.0
    for part in parts:
        most = jnp.maximum(most, jnp.max(dot(dot(columns, part).astype(BF16), group)))
    most_ref[...] = jnp.full((8, 128), most, F32).astype(I32)


def relay_kernel(me_ref, turn_ref, info_ref, slots_ref, send_ref, take_ref):
    me = me_ref[0]
    base = turn_ref[0].astype(F32)
    depth_of = send_ref.shape[0] // NZ
    lane = iota((COLV, 128), 1)
    u = iota((COLV, 1), 0)
    info = info_ref[...]
    owner = info[:, 0:1]
    hits = bits((owner == lane * NZ + me) & (lane < COLS))
    rank = dot(before_same_block(COLV), hits.astype(BF16))
    rank = jnp.sum(rank * hits, axis=1, keepdims=True)
    here = (owner & 7) == me
    wanted = lane < 0
    to_me = u < 0
    for g in range(GROUPS):
        plane = info[:, 1 + g : 2 + g] & 7
        wanted = wanted | (plane == lane)
        to_me = to_me | (plane == me)
    earlier = before_all(COLV)
    leaves = wanted & (lane < NZ) & here
    order = dot(earlier, bits(leaves).astype(BF16))
    place = jnp.where(leaves, order - base, -1.0).T
    depth = iota((depth_of, COLV), 0).astype(F32)
    rows = jnp.concatenate([bits(place[z : z + 1, :] == depth) for z in range(NZ)], axis=0)
    slot = (owner >> 3) * 16 + rank.astype(I32) * 8 + (u >> 5)
    held = bits((slot == iota((COLV, SLOTS), 1)) & here)
    send_ref[...] = dot(rows.astype(BF16), held.astype(BF16)).astype(BF16)
    comes = ((owner & 7) == lane) & (lane < NZ) & to_me
    order = dot(earlier, bits(comes).astype(BF16)) - base
    fits = comes & (order >= 0.0) & (order < float(depth_of))
    at = jnp.sum(jnp.where(fits, lane.astype(F32) * depth_of + order + 1.0, 0.0), axis=1, keepdims=True)
    found = bits(at == iota((COLV, NZ * depth_of), 1).astype(F32) + 1.0).astype(BF16)
    take_ref[...] = dot(slots_ref[...].astype(BF16), found).astype(BF16)


def fetch_kernel(got_ref, pieces_ref, *rest):
    out_ref, hold, sems = rest[-3:]
    column = iota((SHARDS, ROWS), 1)
    asked = got_ref[pl.ds(0, SHARDS, stride=PER), :].astype(I32)
    pieces = [pieces_ref[i] for i in range(3)]
    copies = []
    for k in range(2):
        onehot = bits(asked[:, k : k + 1] == column).astype(BF16)
        hold[k] = pick(onehot, pieces).reshape(COLS, 8, D)
        copies.append(
            pltpu.make_async_copy(hold.at[k], out_ref.at[:, pl.ds(k * 8, 8), :], sems.at[k])
        )
        copies[-1].start()
    wait_all(copies)


def send_kernel(base_ref, onehot_ref, in_ref, *rest):
    out_ref, hold, sems = rest[-3:]
    pieces = split3(in_ref[...])
    half = onehot_ref.shape[0] // 2
    copies = []
    for c in range(2):
        hold[c] = pick(onehot_ref[c * half : (c + 1) * half, :], pieces)
        copies.append(
            pltpu.make_async_copy(hold.at[c], out_ref.at[pl.ds(c * half, half), :], sems.at[c])
        )
        copies[-1].start()
    wait_all(copies)


def put_kernel(first, onehot_ref, in_ref, both_ref, out_ref, hold, sems):
    pieces = split3(in_ref[...])
    half = SLOTS // 2
    at = [out_ref.at[pl.ds(c * half, half), pl.ds(first, D)] for c in range(2)]
    copies = []
    for c in range(2):
        hold[c] = pick(onehot_ref[c * half : (c + 1) * half, :], pieces)
        copies.append(pltpu.make_async_copy(hold.at[c], at[c], sems.at[c]))
        copies[-1].start()
    wait_all(copies)


def add_kernel(onehot_ref, in_ref, both_ref, out_ref, hold, sems):
    at = out_ref.at[:, pl.ds(D, D)]
    copy = pltpu.make_async_copy(at, hold, sems.at[0])
    copy.start()
    copy.wait()
    hold[...] += pick(onehot_ref[...], split3(in_ref[...]))
    copy = pltpu.make_async_copy(hold, at, sems.at[1])
    copy.start()
    copy.wait()


def vectors_kernel(me_ref, slots_ref, *rest):
    parts, out_ref, column, hold, sems = rest[:NZ], rest[-4], rest[-3], rest[-2], rest[-1]
    me = me_ref[0]
    copies = []
    for i, part in enumerate(parts):
        at = pl.multiple_of(((me + i) & 7) * V, V)
        copies.append(pltpu.make_async_copy(part, column.at[pl.ds(at, V), :], sems.at[i]))
    start_all(copies)
    onehot = slots_ref[...].astype(BF16)
    wait_all(copies)
    pieces = split3(column[...])
    half = SLOTS // 2
    copies = []
    for c in range(2):
        hold[c] = pick(onehot[c * half : (c + 1) * half, :], pieces)
        target = out_ref.at[pl.ds(c * half, half), pl.ds(0, D)]
        copies.append(pltpu.make_async_copy(hold.at[c], target, sems.at[NZ + c]))
        copies[-1].start()
    wait_all(copies)


def lookup(table, rows):
    low, high = rows & 127, rows >> 7
    found = jnp.zeros(rows.shape, F32)
    for i in range(ROWS // 128):
        part = jnp.take_along_axis(table[:, 128 * i : 128 * i + 128], low, axis=1)
        found = jnp.where(high == i, part, found)
    return found


def scores(a, pieces_ref):
    hi, mid, lo = split3(a)
    chi, cmid, clo = (pieces_ref[i] for i in range(3))
    small = dot(mid, cmid, NT) + dot(lo, chi, NT) + dot(hi, clo, NT)
    return dot(hi, chi, NT) + (dot(hi, cmid, NT) + dot(mid, chi, NT) + small)


def loss_kernel(both_ref, got_ref, pieces_ref, norms_ref, out_ref):
    line = got_ref[pl.ds(2, SHARDS, stride=PER), :].astype(I32)
    rows = [line, pltpu.roll(line, GSIZE, 1)]
    rows = jnp.concatenate([a.reshape(COLS, 1, NZ, 128) for a in rows], axis=1).reshape(SLOTS, 128)
    rows = rows & (ROWS - 1)
    x = both_ref[:, :D]
    r = x - both_ref[:, D:]
    square = jnp.sum(x * x, axis=1, keepdims=True)
    near = square - 2.0 * scores(x, pieces_ref) + norms_ref[0:1, :]
    hi = r.astype(BF16)
    mid = (r - hi.astype(F32)).astype(BF16)
    chi, cmid = pieces_ref[0], pieces_ref[1]
    table = dot(hi, chi, NT) + (dot(hi, cmid, NT) + dot(mid, chi, NT))
    rx = jnp.sum(r * x, axis=1, keepdims=True)
    rr = jnp.sum(r * r, axis=1, keepdims=True)
    gap = rx - table
    loss = lookup((near + amplify * gap * gap / (rr + tiny)) / D, rows)
    loss = loss.reshape(COLS, 2, NZ, 128)
    second = pltpu.roll(loss[:, 1].reshape(COLS * NZ, 128), GSIZE, 1)
    first = loss[:, 0].reshape(COLS * NZ, 128)
    out_ref[...] = jnp.where(iota((COLS * NZ, 128), 1) < GSIZE, first, second)


def collect_kernel(owner_ref, in_ref, out_ref):
    lane = iota((V, 128), 1)
    hits = [owner_ref[:, g : g + 1] == lane for g in range(GROUPS)]
    rank = dot(before_same_block(V), bits(hits[0] | hits[1] | hits[2] | hits[3]).astype(BF16))
    a = in_ref[...]
    plain, rolled = split3(a), split3(pltpu.roll(a, GSIZE, 1))
    for h in range(2):
        halves = []
        for g in (2 * h, 2 * h + 1):
            first = bits(hits[g] & (rank == 0.0)).astype(BF16)
            second = bits(hits[g] & (rank == 1.0)).astype(BF16)
            if g % 2 == 0:
                halves.append(pick(first, plain) + pick(second, rolled))
            else:
                halves.append(pick(first, rolled) + pick(second, plain))
        out_ref[:, 128 * h : 128 * h + 128] = jnp.where(lane < GSIZE, halves[0], halves[1])


def swap(a, axes):
    return lax.all_to_all(a, axes, split_axis=0, concat_axis=0, tiled=True)


def shards(new_vectors, centroids, primary_owner, primary_row, cand_owner, cand_row):
    plane = ("y", "x")
    column = lax.axis_index(("y", "x")).astype(I32)
    me = jnp.stack([lax.axis_index("z").astype(I32), column])
    def along_z(block, step):
        return lax.ppermute(block, "z", [(z, (z - step) % NZ) for z in range(NZ)])

    with jax.named_scope("column_vectors"):
        blocks = {0: new_vectors}
        for step in (2, -2, 1, -1, 4):
            blocks[step] = along_z(new_vectors, step)
        blocks[3] = along_z(blocks[2], 1)
        blocks[-3] = along_z(blocks[-2], -1)
    with jax.named_scope("requests"):
        [sent] = call(
            request_kernel,
            [shape((PER * SHARDS, 128))],
            primary_owner.T,
            primary_row.T,
            cand_owner.T,
            cand_row,
            far_in=(0, 1, 2, 3),
            far_out=(0,),
            scratch=[
                pltpu.VMEM((1, V), I32),
                pltpu.VMEM((1, V), I32),
                pltpu.VMEM((GROUPS, V), I32),
                pltpu.VMEM((V, GROUPS * GSIZE), I32),
                pltpu.VMEM((PER * SHARDS, 128), F32),
                copies_semaphores(5),
            ],
            name="request",
        )
        arrived = swap(sent.reshape(SHARDS, 1, PER * 128), ("y", "x", "z")).reshape(PER * SHARDS, 128)
    pieces, norms = call(
        prepare_kernel, [shape((3, ROWS, D), BF16), shape((8, ROWS))], centroids, name="prepare"
    )
    with jax.named_scope("primary_rows"):
        [found] = call(
            fetch_kernel,
            [shape((COLS, 16, D))],
            arrived,
            pieces,
            *[blocks[o] for o in FIRST],
            far_in=tuple(range(2, 2 + len(FIRST))),
            far_out=(0,),
            scratch=[pltpu.VMEM((2, COLS, 8, D), F32), copies_semaphores(2)],
            name="fetch",
        )
        fetched = swap(found, plane).reshape(SLOTS, D)
    info, slots, most = call(
        slots_kernel,
        [shape((COLV, 128), I32), shape((SLOTS, COLV)), shape((8, 128), I32)],
        me,
        arrived,
        found,
        smem=(0,),
        far_in=(2,),
        scratch=[pltpu.VMEM((2, SHARDS, 128), I32)],
        name="slots",
    )
    most = most[:1, :1]
    most = jnp.maximum(most, lax.ppermute(most, "rep", [(0, 1), (1, 0)]))[0, 0]

    halves = [pltpu.VMEM((2, SLOTS // 2, D), F32), copies_semaphores(2)]
    pair = [shape((SLOTS, 2 * D))]

    def relay(base, depth):
        return call(
            relay_kernel,
            [shape((NZ * depth, SLOTS), BF16), shape((SLOTS, NZ * depth), BF16)],
            me,
            base.reshape(1),
            info,
            slots,
            smem=(0, 1),
            name="relay",
        )

    def across(base, send, *after):
        depth = send.shape[0] // NZ
        [leaving] = call(
            send_kernel,
            [shape((NZ * depth, D))],
            base.reshape(1),
            send,
            fetched,
            *after,
            smem=(0,),
            far_in=tuple(range(3, 3 + len(after))),
            far_out=(0,),
            scratch=[pltpu.VMEM((2, NZ * depth // 2, D), F32), copies_semaphores(2)],
            name="send",
        )
        return swap(leaving.reshape(NZ, depth, D), "z").reshape(NZ * depth, D)

    def add(take, got, both):
        [both] = call(
            add_kernel,
            pair,
            take,
            got,
            both,
            far_in=(2,),
            far_out=(0,),
            alias={2: 0},
            scratch=[pltpu.VMEM((SLOTS, D), F32), copies_semaphores(2)],
            name="add",
        )
        return both

    def second(state):
        base, both = state
        return base + NEXT, add(next_take, across(base, next_send), both)

    def more(state):
        base, both = state
        send, take = relay(base, K)
        return base + K, add(take, across(base, send), both)

    with jax.named_scope("vectors_out"):
        [both] = call(
            vectors_kernel,
            pair,
            me,
            slots,
            *[blocks[o] for o in (0, 1, 2, 3, 4, -3, -2, -1)],
            smem=(0,),
            far_in=tuple(range(2, 2 + NZ)),
            far_out=(0,),
            scratch=[pltpu.VMEM((COLV, D), F32), halves[0], copies_semaphores(NZ + 2)],
            name="vectors",
        )
    with jax.named_scope("primary_across"):
        send, take = relay(jnp.int32(0), K)
        got = across(jnp.int32(0), send, *[blocks[o] for o in (4, 3, -3, 1, -1)])
        next_send, next_take = relay(jnp.int32(K), NEXT)
        [both] = call(
            functools.partial(put_kernel, D),
            pair,
            take,
            got,
            both,
            far_in=(2,),
            far_out=(0,),
            alias={2: 0},
            scratch=halves,
            name="put",
        )
        state = (jnp.int32(K), both)
        state = lax.while_loop(lambda s: (s[0] == K) & (K < most), second, state)
        _, both = lax.while_loop(lambda s: s[0] < most, more, state)
    with jax.named_scope("out_to_owners"):
        both = swap(both.reshape(COLS, 16, 2 * D), plane).reshape(SLOTS, 2 * D)
    [losses] = call(
        loss_kernel, [shape((SHARDS, 128))], both, arrived, pieces, norms, name="loss"
    )
    with jax.named_scope("losses_back"):
        back = swap(losses.reshape(SHARDS, 1, 128), ("y", "x", "z")).reshape(SHARDS, 128)
    [result] = call(
        collect_kernel, [shape((V, GROUPS * GSIZE))], cand_owner, back, name="collect"
    )
    return result


def solution(mesh):
    fine = Mesh(mesh.devices.reshape(NY, NX, NZ, 2), ("y", "x", "z", "rep"))
    rows = P(("y", "x", "z", "rep"), None)
    in_specs = (rows, P(("y", "x", "z"), None), rows, rows, rows, rows)
    return jax.shard_map(shards, mesh=fine, in_specs=in_specs, out_specs=rows, check_vma=False)
```

```python
import jax
import jax.numpy as jnp
from jax import lax
from jax.experimental import pallas as pl
from jax.experimental.pallas import tpu as pltpu
from jax.sharding import Mesh, PartitionSpec as P

D = 1024
V = 32
GROUPS = 4
GSIZE = 64
ROWS = 512
NY, NX, NZ = 4, 4, 8
COLS = NY * NX
COLV = NZ * V
SLOTS = COLS * NZ * 2
SHARDS = COLS * NZ
K = 32
WIDER = 40
PER = 3
FIRST = (2, -2)
amplify = 1.0
tiny = 1e-06

F32, BF16, I32 = jnp.float32, jnp.bfloat16, jnp.int32
VMEM = pl.BlockSpec(memory_space=pltpu.VMEM)
SMEM = pl.BlockSpec(memory_space=pltpu.SMEM)
HBM = pl.BlockSpec(memory_space=pltpu.HBM)
NN = (((1,), (0,)), ((), ()))
NT = (((1,), (1,)), ((), ()))
TN = (((0,), (0,)), ((), ()))


def call(kernel, out_shape, *operands, smem=(), far_in=(), far_out=(), scratch=(), alias=None, name=None):
    specs = [SMEM if i in smem else HBM if i in far_in else VMEM for i in range(len(operands))]
    operands = [
        pltpu.with_memory_space_constraint(a, pltpu.HBM) if i in far_in else a
        for i, a in enumerate(operands)
    ]
    out_shape = [
        pltpu.HBM(o.shape, o.dtype) if i in far_out else o for i, o in enumerate(out_shape)
    ]
    return pl.pallas_call(
        kernel,
        out_shape=out_shape,
        in_specs=specs,
        out_specs=[HBM if i in far_out else VMEM for i in range(len(out_shape))],
        scratch_shapes=list(scratch),
        input_output_aliases=alias or {},
        compiler_params=pltpu.CompilerParams(vmem_limit_bytes=24 * 2**20),
        name=name,
    )(*operands)


def copies_semaphores(n):
    return pltpu.SemaphoreType.DMA((n,))


def start_all(copies):
    for copy in copies:
        copy.start()


def wait_all(copies):
    for copy in copies:
        copy.wait()


def shape(dims, dtype=F32):
    return jax.ShapeDtypeStruct(dims, dtype)


def split3(a):
    hi = a.astype(BF16)
    rest = a - hi.astype(F32)
    mid = rest.astype(BF16)
    lo = (rest - mid.astype(F32)).astype(BF16)
    return hi, mid, lo


def dot(a, b, dims=NN):
    return lax.dot_general(a, b, dims, preferred_element_type=F32)


def pick(onehot, pieces):
    hi, mid, lo = pieces
    return dot(onehot, hi) + dot(onehot, mid) + dot(onehot, lo)


def bits(mask):
    return jnp.where(mask, 1.0, 0.0)


def iota(dims, axis):
    return lax.broadcasted_iota(I32, dims, axis)


def before_same_block(rows):
    u, w = iota((rows, rows), 0), iota((rows, rows), 1)
    return bits((w < u) & ((u >> 5) == (w >> 5))).astype(BF16)


def before_all(rows):
    return bits(iota((rows, rows), 1) < iota((rows, rows), 0)).astype(BF16)


def prepare_kernel(c_ref, pieces_ref, norms_ref):
    c = c_ref[...]
    for i, piece in enumerate(split3(c)):
        pieces_ref[i] = piece
    squares = split3(c * c)
    ones = jnp.ones((8, D), BF16)
    norms_ref[...] = sum(dot(ones, s, NT) for s in squares)


def request_kernel(owner_ref, row_ref, cand_ref, rows_ref, out_ref, owner, row, cand, rows, hold, sems):
    copies = [
        pltpu.make_async_copy(a, b, sems.at[i])
        for i, (a, b) in enumerate(
            [(owner_ref, owner), (row_ref, row), (cand_ref, cand), (rows_ref, rows)]
        )
    ]
    start_all(copies)
    shard = iota((SHARDS, V), 0)
    earlier = bits(iota((V, V), 0) < iota((V, V), 1)).astype(BF16)
    lane = iota((SHARDS, 128), 1)
    wait_all(copies)
    hit = owner[...] == shard
    rank = dot(bits(hit).astype(BF16), earlier)
    asked = row[...].astype(F32)
    asks = [
        jnp.sum(jnp.where(hit & (rank == float(k)), asked, 0.0), axis=1, keepdims=True)
        for k in range(2)
    ]
    empty = jnp.zeros((1, V), I32)
    owners = jnp.concatenate([empty, owner[...], empty, empty], axis=1).astype(F32)
    line = jnp.where(lane == 0, asks[0], jnp.where(lane == 1, asks[1], 0.0)) + owners
    hold[pl.ds(0, SHARDS, stride=PER), :] = line
    line = jnp.concatenate([cand[g : g + 1, :] for g in range(GROUPS)], axis=1).astype(F32)
    hold[pl.ds(1, SHARDS, stride=PER), :] = jnp.broadcast_to(line, (SHARDS, 128))
    hits = [cand[g : g + 1, :] == shard for g in range(GROUPS)]
    any_hit = hits[0] | hits[1] | hits[2] | hits[3]
    rank = dot(bits(any_hit).astype(BF16), earlier)
    wide = [split3(rows[:, 128 * h : 128 * h + 128].astype(F32))[:2] for h in range(2)]
    lines = []
    for k in range(2):
        sides = [jnp.zeros((SHARDS, 128), F32)] * 2
        for g in range(GROUPS):
            onehot = bits(hits[g] & (rank == float(k))).astype(BF16)
            sides[g % 2] = sides[g % 2] + dot(onehot, wide[g // 2][0]) + dot(onehot, wide[g // 2][1])
        sides[1 - k] = pltpu.roll(sides[1 - k], GSIZE, 1)
        side = even_lanes if k == 0 else odd_lanes
        lines.append(side(sides[0]) + side(sides[1]))
    hold[pl.ds(2, SHARDS, stride=PER), :] = lines[0] + lines[1]
    copy = pltpu.make_async_copy(hold, out_ref, sems.at[4])
    copy.start()
    copy.wait()


def even_lanes(a):
    return jnp.where(iota(a.shape, 1) < GSIZE, a, 0.0)


def odd_lanes(a):
    return jnp.where(iota(a.shape, 1) < GSIZE, 0.0, a)


def slots_kernel(me_ref, got_ref, found_ref, info_ref, slots_ref, most_ref, hold):
    me, column = me_ref[0], me_ref[1]
    owners = got_ref[pl.ds(0, SHARDS, stride=PER), :].astype(I32)
    cands = got_ref[pl.ds(1, SHARDS, stride=PER), :].astype(I32)
    hold[0] = owners
    hold[1] = cands
    at = pl.multiple_of(column * NZ, NZ)
    tile = jnp.concatenate([hold[0, pl.ds(at, NZ), :], hold[1, pl.ds(at, NZ), :]], axis=0)
    turned = jnp.concatenate([tile, jnp.zeros((128 - NZ * 2, 128), I32)], axis=0).T
    block_lane = iota((V, 128), 1)
    for z in range(NZ):
        block = jnp.where(block_lane == 0, turned[V : 2 * V, z : z + 1], 0)
        for g in range(GROUPS):
            cand = turned[g * V : (g + 1) * V, NZ + z : NZ + z + 1]
            block = jnp.where(block_lane == 1 + g, cand, block)
        info_ref[z * V : (z + 1) * V, :] = block
    lane = iota((COLV, 128), 1)
    hit = lane < 0
    for g in range(GROUPS):
        hit = hit | (info_ref[:, 1 + g : 2 + g] == lane * NZ + me)
    hit = hit & (lane < COLS)
    rank = dot(before_same_block(COLV), bits(hit).astype(BF16))
    mine = (iota((NZ, COLV), 1) >> 5) == iota((NZ, COLV), 0)
    for k in range(2):
        turned = bits(hit & (rank == float(k))).T
        for b in range(COLS):
            part = jnp.where(mine, turned[b : b + 1, :], 0.0)
            slots_ref[b * 16 + k * 8 : b * 16 + k * 8 + 8, :] = part
    lane = iota((SHARDS, 128), 1)
    owners = jnp.where((lane >= V) & (lane < 2 * V), owners, 0)
    owners = owners + pltpu.roll(owners, 2 * V, 1)
    owners = (owners + pltpu.roll(owners, V, 1)) & 7
    parts = []
    for b in range(NZ):
        to_plane = bits((cands & 7) == b)
        to_plane = jnp.maximum(to_plane, pltpu.roll(to_plane, 2 * V, 1))
        to_plane = jnp.maximum(to_plane, pltpu.roll(to_plane, V, 1))
        for h in range(2):
            parts.append(jnp.where(owners == (lane >> 5) + 4 * h, to_plane, 0.0).astype(BF16))
    columns = bits((iota((COLS, SHARDS), 1) >> 3) == iota((COLS, SHARDS), 0)).astype(BF16)
    group = bits((iota((128, 128), 0) >> 5) == iota((128, 128), 1)).astype(BF16)
    most = 0.0
    for part in parts:
        most = jnp.maximum(most, jnp.max(dot(dot(columns, part).astype(BF16), group)))
    most_ref[...] = jnp.full((8, 128), most, F32).astype(I32)


def relay_kernel(me_ref, turn_ref, info_ref, slots_ref, send_ref, take_ref):
    me = me_ref[0]
    base = turn_ref[0].astype(F32)
    depth_of = send_ref.shape[0] // NZ
    lane = iota((COLV, 128), 1)
    u = iota((COLV, 1), 0)
    info = info_ref[...]
    owner = info[:, 0:1]
    hits = bits((owner == lane * NZ + me) & (lane < COLS))
    rank = dot(before_same_block(COLV), hits.astype(BF16))
    rank = jnp.sum(rank * hits, axis=1, keepdims=True)
    here = (owner & 7) == me
    wanted = lane < 0
    to_me = u < 0
    for g in range(GROUPS):
        plane = info[:, 1 + g : 2 + g] & 7
        wanted = wanted | (plane == lane)
        to_me = to_me | (plane == me)
    earlier = before_all(COLV)
    leaves = wanted & (lane < NZ) & here
    order = dot(earlier, bits(leaves).astype(BF16))
    place = jnp.where(leaves, order - base, -1.0).T
    depth = iota((depth_of, COLV), 0).astype(F32)
    rows = jnp.concatenate([bits(place[z : z + 1, :] == depth) for z in range(NZ)], axis=0)
    slot = (owner >> 3) * 16 + rank.astype(I32) * 8 + (u >> 5)
    held = bits((slot == iota((COLV, SLOTS), 1)) & here)
    send_ref[...] = dot(rows.astype(BF16), held.astype(BF16)).astype(BF16)
    comes = ((owner & 7) == lane) & (lane < NZ) & to_me
    order = dot(earlier, bits(comes).astype(BF16)) - base
    fits = comes & (order >= 0.0) & (order < float(depth_of))
    at = jnp.sum(jnp.where(fits, lane.astype(F32) * depth_of + order + 1.0, 0.0), axis=1, keepdims=True)
    found = bits(at == iota((COLV, NZ * depth_of), 1).astype(F32) + 1.0).astype(BF16)
    take_ref[...] = dot(slots_ref[...].astype(BF16), found).astype(BF16)


def fetch_kernel(got_ref, pieces_ref, *rest):
    out_ref, hold, sems = rest[-3:]
    column = iota((SHARDS, ROWS), 1)
    asked = got_ref[pl.ds(0, SHARDS, stride=PER), :].astype(I32)
    pieces = [pieces_ref[i] for i in range(3)]
    copies = []
    for k in range(2):
        onehot = bits(asked[:, k : k + 1] == column).astype(BF16)
        hold[k] = pick(onehot, pieces).reshape(COLS, 8, D)
        copies.append(
            pltpu.make_async_copy(hold.at[k], out_ref.at[:, pl.ds(k * 8, 8), :], sems.at[k])
        )
        copies[-1].start()
    wait_all(copies)


def send_kernel(base_ref, onehot_ref, in_ref, *rest):
    out_ref, hold, sems = rest[-3:]
    pieces = split3(in_ref[...])
    half = onehot_ref.shape[0] // 2
    copies = []
    for c in range(2):
        hold[c] = pick(onehot_ref[c * half : (c + 1) * half, :], pieces)
        copies.append(
            pltpu.make_async_copy(hold.at[c], out_ref.at[pl.ds(c * half, half), :], sems.at[c])
        )
        copies[-1].start()
    wait_all(copies)


def put_kernel(onehot_ref, in_ref, both_ref, out_ref, hold, sems):
    pieces = split3(in_ref[...])
    half = SLOTS // 2
    at = [out_ref.at[pl.ds(c * half, half), pl.ds(D, D)] for c in range(2)]
    copies = []
    for c in range(2):
        hold[c] = pick(onehot_ref[c * half : (c + 1) * half, :], pieces)
        copies.append(pltpu.make_async_copy(hold.at[c], at[c], sems.at[c]))
        copies[-1].start()
    wait_all(copies)


def add_kernel(onehot_ref, in_ref, both_ref, out_ref, hold, sems):
    at = out_ref.at[:, pl.ds(D, D)]
    copy = pltpu.make_async_copy(at, hold, sems.at[0])
    copy.start()
    copy.wait()
    hold[...] += pick(onehot_ref[...], split3(in_ref[...]))
    copy = pltpu.make_async_copy(hold, at, sems.at[1])
    copy.start()
    copy.wait()


def vectors_kernel(me_ref, slots_ref, *rest):
    parts, out_ref, column, hold, sems = rest[:NZ], rest[-4], rest[-3], rest[-2], rest[-1]
    me = me_ref[0]
    copies = []
    for i, part in enumerate(parts):
        at = pl.multiple_of(((me + i) & 7) * V, V)
        copies.append(pltpu.make_async_copy(part, column.at[pl.ds(at, V), :], sems.at[i]))
    start_all(copies)
    onehot = slots_ref[...].astype(BF16)
    wait_all(copies)
    pieces = split3(column[...])
    half = SLOTS // 2
    copies = []
    for c in range(2):
        hold[c] = pick(onehot[c * half : (c + 1) * half, :], pieces)
        target = out_ref.at[pl.ds(c * half, half), pl.ds(0, D)]
        copies.append(pltpu.make_async_copy(hold.at[c], target, sems.at[NZ + c]))
        copies[-1].start()
    wait_all(copies)


def lookup(table, rows):
    low, high = rows & 127, rows >> 7
    found = jnp.zeros(rows.shape, F32)
    for i in range(ROWS // 128):
        part = jnp.take_along_axis(table[:, 128 * i : 128 * i + 128], low, axis=1)
        found = jnp.where(high == i, part, found)
    return found


def scores(a, pieces_ref):
    hi, mid, lo = split3(a)
    chi, cmid, clo = (pieces_ref[i] for i in range(3))
    small = dot(mid, cmid, NT) + dot(lo, chi, NT) + dot(hi, clo, NT)
    return dot(hi, chi, NT) + (dot(hi, cmid, NT) + dot(mid, chi, NT) + small)


def loss_kernel(both_ref, got_ref, pieces_ref, norms_ref, out_ref):
    line = got_ref[pl.ds(2, SHARDS, stride=PER), :].astype(I32)
    rows = [line, pltpu.roll(line, GSIZE, 1)]
    rows = jnp.concatenate([a.reshape(COLS, 1, NZ, 128) for a in rows], axis=1).reshape(SLOTS, 128)
    rows = rows & (ROWS - 1)
    x = both_ref[:, :D]
    r = x - both_ref[:, D:]
    square = jnp.sum(x * x, axis=1, keepdims=True)
    near = square - 2.0 * scores(x, pieces_ref) + norms_ref[0:1, :]
    hi = r.astype(BF16)
    mid = (r - hi.astype(F32)).astype(BF16)
    chi, cmid = pieces_ref[0], pieces_ref[1]
    table = dot(hi, chi, NT) + (dot(hi, cmid, NT) + dot(mid, chi, NT))
    rx = jnp.sum(r * x, axis=1, keepdims=True)
    rr = jnp.sum(r * r, axis=1, keepdims=True)
    gap = rx - table
    loss = lookup((near + amplify * gap * gap / (rr + tiny)) / D, rows)
    loss = loss.reshape(COLS, 2, NZ, 128)
    second = pltpu.roll(loss[:, 1].reshape(COLS * NZ, 128), GSIZE, 1)
    first = loss[:, 0].reshape(COLS * NZ, 128)
    out_ref[...] = jnp.where(iota((COLS * NZ, 128), 1) < GSIZE, first, second)


def collect_kernel(owner_ref, in_ref, out_ref):
    lane = iota((V, 128), 1)
    hits = [owner_ref[:, g : g + 1] == lane for g in range(GROUPS)]
    rank = dot(before_same_block(V), bits(hits[0] | hits[1] | hits[2] | hits[3]).astype(BF16))
    a = in_ref[...]
    plain, rolled = split3(a), split3(pltpu.roll(a, GSIZE, 1))
    for h in range(2):
        halves = []
        for g in (2 * h, 2 * h + 1):
            first = bits(hits[g] & (rank == 0.0)).astype(BF16)
            second = bits(hits[g] & (rank == 1.0)).astype(BF16)
            if g % 2 == 0:
                halves.append(pick(first, plain) + pick(second, rolled))
            else:
                halves.append(pick(first, rolled) + pick(second, plain))
        out_ref[:, 128 * h : 128 * h + 128] = jnp.where(lane < GSIZE, halves[0], halves[1])


def swap(a, axes):
    return lax.all_to_all(a, axes, split_axis=0, concat_axis=0, tiled=True)


def shards(new_vectors, centroids, primary_owner, primary_row, cand_owner, cand_row):
    plane = ("y", "x")
    column = lax.axis_index(("y", "x")).astype(I32)
    me = jnp.stack([lax.axis_index("z").astype(I32), column])
    def along_z(block, step):
        return lax.ppermute(block, "z", [(z, (z - step) % NZ) for z in range(NZ)])

    with jax.named_scope("column_vectors"):
        blocks = {0: new_vectors}
        for step in (2, -2, 1, -1, 4):
            blocks[step] = along_z(new_vectors, step)
        blocks[3] = along_z(blocks[2], 1)
        blocks[-3] = along_z(blocks[-2], -1)
    with jax.named_scope("requests"):
        [sent] = call(
            request_kernel,
            [shape((PER * SHARDS, 128))],
            primary_owner.T,
            primary_row.T,
            cand_owner.T,
            cand_row,
            far_in=(0, 1, 2, 3),
            far_out=(0,),
            scratch=[
                pltpu.VMEM((1, V), I32),
                pltpu.VMEM((1, V), I32),
                pltpu.VMEM((GROUPS, V), I32),
                pltpu.VMEM((V, GROUPS * GSIZE), I32),
                pltpu.VMEM((PER * SHARDS, 128), F32),
                copies_semaphores(5),
            ],
            name="request",
        )
        arrived = swap(sent.reshape(SHARDS, 1, PER * 128), ("y", "x", "z")).reshape(PER * SHARDS, 128)
    pieces, norms = call(
        prepare_kernel, [shape((3, ROWS, D), BF16), shape((8, ROWS))], centroids, name="prepare"
    )
    with jax.named_scope("primary_rows"):
        [found] = call(
            fetch_kernel,
            [shape((COLS, 16, D))],
            arrived,
            pieces,
            *[blocks[o] for o in FIRST],
            far_in=tuple(range(2, 2 + len(FIRST))),
            far_out=(0,),
            scratch=[pltpu.VMEM((2, COLS, 8, D), F32), copies_semaphores(2)],
            name="fetch",
        )
        fetched = swap(found, plane).reshape(SLOTS, D)
    info, slots, most = call(
        slots_kernel,
        [shape((COLV, 128), I32), shape((SLOTS, COLV)), shape((8, 128), I32)],
        me,
        arrived,
        found,
        smem=(0,),
        far_in=(2,),
        scratch=[pltpu.VMEM((2, SHARDS, 128), I32)],
        name="slots",
    )
    most = most[:1, :1]
    most = jnp.maximum(most, lax.ppermute(most, "rep", [(0, 1), (1, 0)]))[0, 0]

    halves = [pltpu.VMEM((2, SLOTS // 2, D), F32), copies_semaphores(2)]
    pair = [shape((SLOTS, 2 * D))]

    def relay(base, depth):
        return call(
            relay_kernel,
            [shape((NZ * depth, SLOTS), BF16), shape((SLOTS, NZ * depth), BF16)],
            me,
            base.reshape(1),
            info,
            slots,
            smem=(0, 1),
            name="relay",
        )

    def across(base, send, *after):
        depth = send.shape[0] // NZ
        [leaving] = call(
            send_kernel,
            [shape((NZ * depth, D))],
            base.reshape(1),
            send,
            fetched,
            *after,
            smem=(0,),
            far_in=tuple(range(3, 3 + len(after))),
            far_out=(0,),
            scratch=[pltpu.VMEM((2, NZ * depth // 2, D), F32), copies_semaphores(2)],
            name="send",
        )
        return swap(leaving.reshape(NZ, depth, D), "z").reshape(NZ * depth, D)

    def add(take, got, both):
        [both] = call(
            add_kernel,
            pair,
            take,
            got,
            both,
            far_in=(2,),
            far_out=(0,),
            alias={2: 0},
            scratch=[pltpu.VMEM((SLOTS, D), F32), copies_semaphores(2)],
            name="add",
        )
        return both

    def more(state):
        base, both = state
        send, take = relay(base, K)
        return base + K, add(take, across(base, send), both)

    def first(send, take):
        got = across(jnp.int32(0), send, *[blocks[o] for o in (4, 3, -3, 1, -1)])
        [both] = call(
            vectors_kernel,
            pair,
            me,
            slots,
            *[blocks[o] for o in (0, 1, 2, 3, 4, -3, -2, -1)],
            smem=(0,),
            far_in=tuple(range(2, 2 + NZ)),
            far_out=(0,),
            scratch=[pltpu.VMEM((COLV, D), F32), halves[0], copies_semaphores(NZ + 2)],
            name="vectors",
        )
        [both] = call(
            put_kernel,
            pair,
            take,
            got,
            both,
            far_in=(2,),
            far_out=(0,),
            alias={2: 0},
            scratch=halves,
            name="put",
        )
        return both

    with jax.named_scope("primary_across"):
        zero = jnp.int32(0)
        tables = relay(zero, K)
        calm = most <= K
        both = lax.cond(calm, lambda: first(*tables), lambda: first(*relay(zero, WIDER)))
        state = (jnp.where(calm, K, WIDER).astype(I32), both)
        _, both = lax.while_loop(lambda s: s[0] < most, more, state)
    with jax.named_scope("out_to_owners"):
        both = swap(both.reshape(COLS, 16, 2 * D), plane).reshape(SLOTS, 2 * D)
    [losses] = call(
        loss_kernel, [shape((SHARDS, 128))], both, arrived, pieces, norms, name="loss"
    )
    with jax.named_scope("losses_back"):
        back = swap(losses.reshape(SHARDS, 1, 128), ("y", "x", "z")).reshape(SHARDS, 128)
    [result] = call(
        collect_kernel, [shape((V, GROUPS * GSIZE))], cand_owner, back, name="collect"
    )
    return result


def solution(mesh):
    fine = Mesh(mesh.devices.reshape(NY, NX, NZ, 2), ("y", "x", "z", "rep"))
    rows = P(("y", "x", "z", "rep"), None)
    in_specs = (rows, P(("y", "x", "z"), None), rows, rows, rows, rows)
    return jax.shard_map(shards, mesh=fine, in_specs=in_specs, out_specs=rows, check_vma=False)
```

```python
import jax
import jax.numpy as jnp
from jax import lax
from jax.experimental import pallas as pl
from jax.experimental.pallas import tpu as pltpu
from jax.sharding import Mesh, PartitionSpec as P

D = 1024
V = 32
GROUPS = 4
GSIZE = 64
ROWS = 512
NY, NX, NZ = 4, 4, 8
COLS = NY * NX
COLV = NZ * V
SLOTS = COLS * NZ * 2
SHARDS = COLS * NZ
K = 32
NEXT = 8
PER = 3
FIRST = (2, -2)
amplify = 1.0
tiny = 1e-06

F32, BF16, I32 = jnp.float32, jnp.bfloat16, jnp.int32
VMEM = pl.BlockSpec(memory_space=pltpu.VMEM)
SMEM = pl.BlockSpec(memory_space=pltpu.SMEM)
HBM = pl.BlockSpec(memory_space=pltpu.HBM)
NN = (((1,), (0,)), ((), ()))
NT = (((1,), (1,)), ((), ()))
TN = (((0,), (0,)), ((), ()))


def call(kernel, out_shape, *operands, smem=(), far_in=(), far_out=(), scratch=(), alias=None, name=None):
    specs = [SMEM if i in smem else HBM if i in far_in else VMEM for i in range(len(operands))]
    operands = [
        pltpu.with_memory_space_constraint(a, pltpu.HBM) if i in far_in else a
        for i, a in enumerate(operands)
    ]
    out_shape = [
        pltpu.HBM(o.shape, o.dtype) if i in far_out else o for i, o in enumerate(out_shape)
    ]
    return pl.pallas_call(
        kernel,
        out_shape=out_shape,
        in_specs=specs,
        out_specs=[HBM if i in far_out else VMEM for i in range(len(out_shape))],
        scratch_shapes=list(scratch),
        input_output_aliases=alias or {},
        compiler_params=pltpu.CompilerParams(vmem_limit_bytes=24 * 2**20),
        name=name,
    )(*operands)


def copies_semaphores(n):
    return pltpu.SemaphoreType.DMA((n,))


def start_all(copies):
    for copy in copies:
        copy.start()


def wait_all(copies):
    for copy in copies:
        copy.wait()


def shape(dims, dtype=F32):
    return jax.ShapeDtypeStruct(dims, dtype)


def split3(a):
    hi = a.astype(BF16)
    rest = a - hi.astype(F32)
    mid = rest.astype(BF16)
    lo = (rest - mid.astype(F32)).astype(BF16)
    return hi, mid, lo


def dot(a, b, dims=NN):
    return lax.dot_general(a, b, dims, preferred_element_type=F32)


def pick(onehot, pieces):
    hi, mid, lo = pieces
    return dot(onehot, hi) + dot(onehot, mid) + dot(onehot, lo)


def bits(mask):
    return jnp.where(mask, 1.0, 0.0)


def iota(dims, axis):
    return lax.broadcasted_iota(I32, dims, axis)


def before_same_block(rows):
    u, w = iota((rows, rows), 0), iota((rows, rows), 1)
    return bits((w < u) & ((u >> 5) == (w >> 5))).astype(BF16)


def before_all(rows):
    return bits(iota((rows, rows), 1) < iota((rows, rows), 0)).astype(BF16)


def prepare_kernel(c_ref, pieces_ref, norms_ref):
    c = c_ref[...]
    for i, piece in enumerate(split3(c)):
        pieces_ref[i] = piece
    squares = split3(c * c)
    ones = jnp.ones((8, D), BF16)
    norms_ref[...] = sum(dot(ones, s, NT) for s in squares)


def request_kernel(owner_ref, row_ref, cand_ref, rows_ref, out_ref, owner, row, cand, rows, hold, sems):
    copies = [
        pltpu.make_async_copy(a, b, sems.at[i])
        for i, (a, b) in enumerate(
            [(owner_ref, owner), (row_ref, row), (cand_ref, cand), (rows_ref, rows)]
        )
    ]
    start_all(copies)
    shard = iota((SHARDS, V), 0)
    earlier = bits(iota((V, V), 0) < iota((V, V), 1)).astype(BF16)
    lane = iota((SHARDS, 128), 1)
    wait_all(copies)
    hit = owner[...] == shard
    rank = dot(bits(hit).astype(BF16), earlier)
    asked = row[...].astype(F32)
    asks = [
        jnp.sum(jnp.where(hit & (rank == float(k)), asked, 0.0), axis=1, keepdims=True)
        for k in range(2)
    ]
    empty = jnp.zeros((1, V), I32)
    owners = jnp.concatenate([empty, owner[...], empty, empty], axis=1).astype(F32)
    line = jnp.where(lane == 0, asks[0], jnp.where(lane == 1, asks[1], 0.0)) + owners
    hold[pl.ds(0, SHARDS, stride=PER), :] = line
    line = jnp.concatenate([cand[g : g + 1, :] for g in range(GROUPS)], axis=1).astype(F32)
    hold[pl.ds(1, SHARDS, stride=PER), :] = jnp.broadcast_to(line, (SHARDS, 128))
    hits = [cand[g : g + 1, :] == shard for g in range(GROUPS)]
    any_hit = hits[0] | hits[1] | hits[2] | hits[3]
    rank = dot(bits(any_hit).astype(BF16), earlier)
    wide = [split3(rows[:, 128 * h : 128 * h + 128].astype(F32))[:2] for h in range(2)]
    lines = []
    for k in range(2):
        sides = [jnp.zeros((SHARDS, 128), F32)] * 2
        for g in range(GROUPS):
            onehot = bits(hits[g] & (rank == float(k))).astype(BF16)
            sides[g % 2] = sides[g % 2] + dot(onehot, wide[g // 2][0]) + dot(onehot, wide[g // 2][1])
        sides[1 - k] = pltpu.roll(sides[1 - k], GSIZE, 1)
        side = even_lanes if k == 0 else odd_lanes
        lines.append(side(sides[0]) + side(sides[1]))
    hold[pl.ds(2, SHARDS, stride=PER), :] = lines[0] + lines[1]
    copy = pltpu.make_async_copy(hold, out_ref, sems.at[4])
    copy.start()
    copy.wait()


def even_lanes(a):
    return jnp.where(iota(a.shape, 1) < GSIZE, a, 0.0)


def odd_lanes(a):
    return jnp.where(iota(a.shape, 1) < GSIZE, 0.0, a)


def slots_kernel(me_ref, got_ref, found_ref, info_ref, slots_ref, most_ref, hold):
    me, column = me_ref[0], me_ref[1]
    owners = got_ref[pl.ds(0, SHARDS, stride=PER), :].astype(I32)
    cands = got_ref[pl.ds(1, SHARDS, stride=PER), :].astype(I32)
    hold[0] = owners
    hold[1] = cands
    at = pl.multiple_of(column * NZ, NZ)
    tile = jnp.concatenate([hold[0, pl.ds(at, NZ), :], hold[1, pl.ds(at, NZ), :]], axis=0)
    turned = jnp.concatenate([tile, jnp.zeros((128 - NZ * 2, 128), I32)], axis=0).T
    block_lane = iota((V, 128), 1)
    for z in range(NZ):
        block = jnp.where(block_lane == 0, turned[V : 2 * V, z : z + 1], 0)
        for g in range(GROUPS):
            cand = turned[g * V : (g + 1) * V, NZ + z : NZ + z + 1]
            block = jnp.where(block_lane == 1 + g, cand, block)
        info_ref[z * V : (z + 1) * V, :] = block
    lane = iota((COLV, 128), 1)
    hit = lane < 0
    for g in range(GROUPS):
        hit = hit | (info_ref[:, 1 + g : 2 + g] == lane * NZ + me)
    hit = hit & (lane < COLS)
    rank = dot(before_same_block(COLV), bits(hit).astype(BF16))
    mine = (iota((NZ, COLV), 1) >> 5) == iota((NZ, COLV), 0)
    for k in range(2):
        turned = bits(hit & (rank == float(k))).T
        for b in range(COLS):
            part = jnp.where(mine, turned[b : b + 1, :], 0.0)
            slots_ref[b * 16 + k * 8 : b * 16 + k * 8 + 8, :] = part
    lane = iota((SHARDS, 128), 1)
    owners = jnp.where((lane >= V) & (lane < 2 * V), owners, 0)
    owners = owners + pltpu.roll(owners, 2 * V, 1)
    owners = (owners + pltpu.roll(owners, V, 1)) & 7
    parts = []
    for b in range(NZ):
        to_plane = bits((cands & 7) == b)
        to_plane = jnp.maximum(to_plane, pltpu.roll(to_plane, 2 * V, 1))
        to_plane = jnp.maximum(to_plane, pltpu.roll(to_plane, V, 1))
        for h in range(2):
            parts.append(jnp.where(owners == (lane >> 5) + 4 * h, to_plane, 0.0).astype(BF16))
    columns = bits((iota((COLS, SHARDS), 1) >> 3) == iota((COLS, SHARDS), 0)).astype(BF16)
    group = bits((iota((128, 128), 0) >> 5) == iota((128, 128), 1)).astype(BF16)
    most = 0.0
    for part in parts:
        most = jnp.maximum(most, jnp.max(dot(dot(columns, part).astype(BF16), group)))
    most_ref[...] = jnp.full((8, 128), most, F32).astype(I32)


def relay_kernel(me_ref, turn_ref, info_ref, slots_ref, send_ref, take_ref):
    me = me_ref[0]
    base = turn_ref[0].astype(F32)
    depth_of = send_ref.shape[0] // NZ
    lane = iota((COLV, 128), 1)
    u = iota((COLV, 1), 0)
    info = info_ref[...]
    owner = info[:, 0:1]
    hits = bits((owner == lane * NZ + me) & (lane < COLS))
    rank = dot(before_same_block(COLV), hits.astype(BF16))
    rank = jnp.sum(rank * hits, axis=1, keepdims=True)
    here = (owner & 7) == me
    wanted = lane < 0
    to_me = u < 0
    for g in range(GROUPS):
        plane = info[:, 1 + g : 2 + g] & 7
        wanted = wanted | (plane == lane)
        to_me = to_me | (plane == me)
    earlier = before_all(COLV)
    leaves = wanted & (lane < NZ) & here
    order = dot(earlier, bits(leaves).astype(BF16))
    place = jnp.where(leaves, order - base, -1.0).T
    depth = iota((depth_of, COLV), 0).astype(F32)
    rows = jnp.concatenate([bits(place[z : z + 1, :] == depth) for z in range(NZ)], axis=0)
    slot = (owner >> 3) * 16 + rank.astype(I32) * 8 + (u >> 5)
    held = bits((slot == iota((COLV, SLOTS), 1)) & here)
    send_ref[...] = dot(rows.astype(BF16), held.astype(BF16)).astype(BF16)
    comes = ((owner & 7) == lane) & (lane < NZ) & to_me
    order = dot(earlier, bits(comes).astype(BF16)) - base
    fits = comes & (order >= 0.0) & (order < float(depth_of))
    at = jnp.sum(jnp.where(fits, lane.astype(F32) * depth_of + order + 1.0, 0.0), axis=1, keepdims=True)
    found = bits(at == iota((COLV, NZ * depth_of), 1).astype(F32) + 1.0).astype(BF16)
    take_ref[...] = dot(slots_ref[...].astype(BF16), found).astype(BF16)


def fetch_kernel(got_ref, pieces_ref, *rest):
    out_ref, hold, sems = rest[-3:]
    column = iota((SHARDS, ROWS), 1)
    asked = got_ref[pl.ds(0, SHARDS, stride=PER), :].astype(I32)
    pieces = [pieces_ref[i] for i in range(3)]
    copies = []
    for k in range(2):
        onehot = bits(asked[:, k : k + 1] == column).astype(BF16)
        hold[k] = pick(onehot, pieces).reshape(COLS, 8, D)
        copies.append(
            pltpu.make_async_copy(hold.at[k], out_ref.at[:, pl.ds(k * 8, 8), :], sems.at[k])
        )
        copies[-1].start()
    wait_all(copies)


def send_kernel(base_ref, onehot_ref, in_ref, *rest):
    out_ref, hold, sems = rest[-3:]
    pieces = split3(in_ref[...])
    half = onehot_ref.shape[0] // 2
    copies = []
    for c in range(2):
        hold[c] = pick(onehot_ref[c * half : (c + 1) * half, :], pieces)
        copies.append(
            pltpu.make_async_copy(hold.at[c], out_ref.at[pl.ds(c * half, half), :], sems.at[c])
        )
        copies[-1].start()
    wait_all(copies)


def put_kernel(onehot_ref, in_ref, next_onehot_ref, next_ref, both_ref, out_ref, hold, sems):
    pieces, next_pieces = split3(in_ref[...]), split3(next_ref[...])
    half = SLOTS // 2
    copies = []
    for c in range(2):
        cut = slice(c * half, (c + 1) * half)
        hold[c] = pick(onehot_ref[cut, :], pieces) + pick(next_onehot_ref[cut, :], next_pieces)
        target = out_ref.at[pl.ds(c * half, half), pl.ds(D, D)]
        copies.append(pltpu.make_async_copy(hold.at[c], target, sems.at[c]))
        copies[-1].start()
    wait_all(copies)


def add_kernel(onehot_ref, in_ref, both_ref, out_ref, hold, sems):
    at = out_ref.at[:, pl.ds(D, D)]
    copy = pltpu.make_async_copy(at, hold, sems.at[0])
    copy.start()
    copy.wait()
    hold[...] += pick(onehot_ref[...], split3(in_ref[...]))
    copy = pltpu.make_async_copy(hold, at, sems.at[1])
    copy.start()
    copy.wait()


def vectors_kernel(me_ref, slots_ref, *rest):
    parts, out_ref, column, hold, sems = rest[:NZ], rest[-4], rest[-3], rest[-2], rest[-1]
    me = me_ref[0]
    copies = []
    for i, part in enumerate(parts):
        at = pl.multiple_of(((me + i) & 7) * V, V)
        copies.append(pltpu.make_async_copy(part, column.at[pl.ds(at, V), :], sems.at[i]))
    start_all(copies)
    onehot = slots_ref[...].astype(BF16)
    wait_all(copies)
    pieces = split3(column[...])
    half = SLOTS // 2
    copies = []
    for c in range(2):
        hold[c] = pick(onehot[c * half : (c + 1) * half, :], pieces)
        target = out_ref.at[pl.ds(c * half, half), pl.ds(0, D)]
        copies.append(pltpu.make_async_copy(hold.at[c], target, sems.at[NZ + c]))
        copies[-1].start()
    wait_all(copies)


def lookup(table, rows):
    low, high = rows & 127, rows >> 7
    found = jnp.zeros(rows.shape, F32)
    for i in range(ROWS // 128):
        part = jnp.take_along_axis(table[:, 128 * i : 128 * i + 128], low, axis=1)
        found = jnp.where(high == i, part, found)
    return found


def scores(a, pieces_ref):
    hi, mid, lo = split3(a)
    chi, cmid, clo = (pieces_ref[i] for i in range(3))
    small = dot(mid, cmid, NT) + dot(lo, chi, NT) + dot(hi, clo, NT)
    return dot(hi, chi, NT) + (dot(hi, cmid, NT) + dot(mid, chi, NT) + small)


def loss_kernel(both_ref, got_ref, pieces_ref, norms_ref, out_ref):
    line = got_ref[pl.ds(2, SHARDS, stride=PER), :].astype(I32)
    rows = [line, pltpu.roll(line, GSIZE, 1)]
    rows = jnp.concatenate([a.reshape(COLS, 1, NZ, 128) for a in rows], axis=1).reshape(SLOTS, 128)
    rows = rows & (ROWS - 1)
    x = both_ref[:, :D]
    r = x - both_ref[:, D:]
    square = jnp.sum(x * x, axis=1, keepdims=True)
    near = square - 2.0 * scores(x, pieces_ref) + norms_ref[0:1, :]
    hi = r.astype(BF16)
    mid = (r - hi.astype(F32)).astype(BF16)
    chi, cmid = pieces_ref[0], pieces_ref[1]
    table = dot(hi, chi, NT) + (dot(hi, cmid, NT) + dot(mid, chi, NT))
    rx = jnp.sum(r * x, axis=1, keepdims=True)
    rr = jnp.sum(r * r, axis=1, keepdims=True)
    gap = rx - table
    loss = lookup((near + amplify * gap * gap / (rr + tiny)) / D, rows)
    loss = loss.reshape(COLS, 2, NZ, 128)
    second = pltpu.roll(loss[:, 1].reshape(COLS * NZ, 128), GSIZE, 1)
    first = loss[:, 0].reshape(COLS * NZ, 128)
    out_ref[...] = jnp.where(iota((COLS * NZ, 128), 1) < GSIZE, first, second)


def collect_kernel(owner_ref, in_ref, out_ref):
    lane = iota((V, 128), 1)
    hits = [owner_ref[:, g : g + 1] == lane for g in range(GROUPS)]
    rank = dot(before_same_block(V), bits(hits[0] | hits[1] | hits[2] | hits[3]).astype(BF16))
    a = in_ref[...]
    plain, rolled = split3(a), split3(pltpu.roll(a, GSIZE, 1))
    for h in range(2):
        halves = []
        for g in (2 * h, 2 * h + 1):
            first = bits(hits[g] & (rank == 0.0)).astype(BF16)
            second = bits(hits[g] & (rank == 1.0)).astype(BF16)
            if g % 2 == 0:
                halves.append(pick(first, plain) + pick(second, rolled))
            else:
                halves.append(pick(first, rolled) + pick(second, plain))
        out_ref[:, 128 * h : 128 * h + 128] = jnp.where(lane < GSIZE, halves[0], halves[1])


def swap(a, axes):
    return lax.all_to_all(a, axes, split_axis=0, concat_axis=0, tiled=True)


def shards(new_vectors, centroids, primary_owner, primary_row, cand_owner, cand_row):
    plane = ("y", "x")
    column = lax.axis_index(("y", "x")).astype(I32)
    me = jnp.stack([lax.axis_index("z").astype(I32), column])
    def along_z(block, step):
        return lax.ppermute(block, "z", [(z, (z - step) % NZ) for z in range(NZ)])

    with jax.named_scope("column_vectors"):
        blocks = {0: new_vectors}
        for step in (2, -2, 1, -1, 4):
            blocks[step] = along_z(new_vectors, step)
        blocks[3] = along_z(blocks[2], 1)
        blocks[-3] = along_z(blocks[-2], -1)
    with jax.named_scope("requests"):
        [sent] = call(
            request_kernel,
            [shape((PER * SHARDS, 128))],
            primary_owner.T,
            primary_row.T,
            cand_owner.T,
            cand_row,
            far_in=(0, 1, 2, 3),
            far_out=(0,),
            scratch=[
                pltpu.VMEM((1, V), I32),
                pltpu.VMEM((1, V), I32),
                pltpu.VMEM((GROUPS, V), I32),
                pltpu.VMEM((V, GROUPS * GSIZE), I32),
                pltpu.VMEM((PER * SHARDS, 128), F32),
                copies_semaphores(5),
            ],
            name="request",
        )
        arrived = swap(sent.reshape(SHARDS, 1, PER * 128), ("y", "x", "z")).reshape(PER * SHARDS, 128)
    pieces, norms = call(
        prepare_kernel, [shape((3, ROWS, D), BF16), shape((8, ROWS))], centroids, name="prepare"
    )
    with jax.named_scope("primary_rows"):
        [found] = call(
            fetch_kernel,
            [shape((COLS, 16, D))],
            arrived,
            pieces,
            *[blocks[o] for o in FIRST],
            far_in=tuple(range(2, 2 + len(FIRST))),
            far_out=(0,),
            scratch=[pltpu.VMEM((2, COLS, 8, D), F32), copies_semaphores(2)],
            name="fetch",
        )
        fetched = swap(found, plane).reshape(SLOTS, D)
    info, slots, most = call(
        slots_kernel,
        [shape((COLV, 128), I32), shape((SLOTS, COLV)), shape((8, 128), I32)],
        me,
        arrived,
        found,
        smem=(0,),
        far_in=(2,),
        scratch=[pltpu.VMEM((2, SHARDS, 128), I32)],
        name="slots",
    )
    most = most[:1, :1]
    most = jnp.maximum(most, lax.ppermute(most, "rep", [(0, 1), (1, 0)]))[0, 0]

    halves = [pltpu.VMEM((2, SLOTS // 2, D), F32), copies_semaphores(2)]
    pair = [shape((SLOTS, 2 * D))]

    def relay(base, depth):
        return call(
            relay_kernel,
            [shape((NZ * depth, SLOTS), BF16), shape((SLOTS, NZ * depth), BF16)],
            me,
            base.reshape(1),
            info,
            slots,
            smem=(0, 1),
            name="relay",
        )

    def across(base, send, *after):
        depth = send.shape[0] // NZ
        [leaving] = call(
            send_kernel,
            [shape((NZ * depth, D))],
            base.reshape(1),
            send,
            fetched,
            *after,
            smem=(0,),
            far_in=tuple(range(3, 3 + len(after))),
            far_out=(0,),
            scratch=[pltpu.VMEM((2, NZ * depth // 2, D), F32), copies_semaphores(2)],
            name="send",
        )
        return swap(leaving.reshape(NZ, depth, D), "z").reshape(NZ * depth, D)

    def add(take, got, both):
        [both] = call(
            add_kernel,
            pair,
            take,
            got,
            both,
            far_in=(2,),
            far_out=(0,),
            alias={2: 0},
            scratch=[pltpu.VMEM((SLOTS, D), F32), copies_semaphores(2)],
            name="add",
        )
        return both

    def second(state):
        base, _ = state
        return base + NEXT, across(base, next_send)

    def more(state):
        base, both = state
        send, take = relay(base, K)
        return base + K, add(take, across(base, send), both)

    with jax.named_scope("vectors_out"):
        [both] = call(
            vectors_kernel,
            pair,
            me,
            slots,
            *[blocks[o] for o in (0, 1, 2, 3, 4, -3, -2, -1)],
            smem=(0,),
            far_in=tuple(range(2, 2 + NZ)),
            far_out=(0,),
            scratch=[pltpu.VMEM((COLV, D), F32), halves[0], copies_semaphores(NZ + 2)],
            name="vectors",
        )
    with jax.named_scope("primary_across"):
        send, take = relay(jnp.int32(0), K)
        got = across(jnp.int32(0), send, *[blocks[o] for o in (4, 3, -3, 1, -1)])
        next_send, next_take = relay(jnp.int32(K), NEXT)
        got, empty = lax.optimization_barrier((got, jnp.zeros((NZ * NEXT, D), F32)))
        state = (jnp.int32(K), empty)
        base, next_got = lax.while_loop(lambda s: (s[0] == K) & (K < most), second, state)
        [both] = call(
            put_kernel,
            pair,
            take,
            got,
            next_take,
            next_got,
            both,
            far_in=(4,),
            far_out=(0,),
            alias={4: 0},
            scratch=halves,
            name="put",
        )
        _, both = lax.while_loop(lambda s: s[0] < most, more, (base, both))
    with jax.named_scope("out_to_owners"):
        both = swap(both.reshape(COLS, 16, 2 * D), plane).reshape(SLOTS, 2 * D)
    [losses] = call(
        loss_kernel, [shape((SHARDS, 128))], both, arrived, pieces, norms, name="loss"
    )
    with jax.named_scope("losses_back"):
        back = swap(losses.reshape(SHARDS, 1, 128), ("y", "x", "z")).reshape(SHARDS, 128)
    [result] = call(
        collect_kernel, [shape((V, GROUPS * GSIZE))], cand_owner, back, name="collect"
    )
    return result


def solution(mesh):
    fine = Mesh(mesh.devices.reshape(NY, NX, NZ, 2), ("y", "x", "z", "rep"))
    rows = P(("y", "x", "z", "rep"), None)
    in_specs = (rows, P(("y", "x", "z"), None), rows, rows, rows, rows)
    return jax.shard_map(shards, mesh=fine, in_specs=in_specs, out_specs=rows, check_vma=False)
```

```python
import functools

import jax
import jax.numpy as jnp
from jax import lax
from jax.experimental import pallas as pl
from jax.experimental.pallas import tpu as pltpu
from jax.sharding import Mesh, PartitionSpec as P

D = 1024
V = 32
GROUPS = 4
GSIZE = 64
ROWS = 512
NY, NX, NZ = 4, 4, 8
COLS = NY * NX
COLV = NZ * V
SLOTS = COLS * NZ * 2
SHARDS = COLS * NZ
K = 32
NEXT = 8
PER = 3
FIRST = (2, -2)
amplify = 1.0
tiny = 1e-06

F32, BF16, I32 = jnp.float32, jnp.bfloat16, jnp.int32
VMEM = pl.BlockSpec(memory_space=pltpu.VMEM)
SMEM = pl.BlockSpec(memory_space=pltpu.SMEM)
HBM = pl.BlockSpec(memory_space=pltpu.HBM)
NN = (((1,), (0,)), ((), ()))
NT = (((1,), (1,)), ((), ()))
TN = (((0,), (0,)), ((), ()))


def call(kernel, out_shape, *operands, smem=(), far_in=(), far_out=(), scratch=(), alias=None, name=None):
    specs = [SMEM if i in smem else HBM if i in far_in else VMEM for i in range(len(operands))]
    operands = [
        pltpu.with_memory_space_constraint(a, pltpu.HBM) if i in far_in else a
        for i, a in enumerate(operands)
    ]
    out_shape = [
        pltpu.HBM(o.shape, o.dtype) if i in far_out else o for i, o in enumerate(out_shape)
    ]
    return pl.pallas_call(
        kernel,
        out_shape=out_shape,
        in_specs=specs,
        out_specs=[HBM if i in far_out else VMEM for i in range(len(out_shape))],
        scratch_shapes=list(scratch),
        input_output_aliases=alias or {},
        compiler_params=pltpu.CompilerParams(vmem_limit_bytes=24 * 2**20),
        name=name,
    )(*operands)


def copies_semaphores(n):
    return pltpu.SemaphoreType.DMA((n,))


def start_all(copies):
    for copy in copies:
        copy.start()


def wait_all(copies):
    for copy in copies:
        copy.wait()


def shape(dims, dtype=F32):
    return jax.ShapeDtypeStruct(dims, dtype)


def split3(a):
    hi = a.astype(BF16)
    rest = a - hi.astype(F32)
    mid = rest.astype(BF16)
    lo = (rest - mid.astype(F32)).astype(BF16)
    return hi, mid, lo


def dot(a, b, dims=NN):
    return lax.dot_general(a, b, dims, preferred_element_type=F32)


def pick(onehot, pieces):
    hi, mid, lo = pieces
    return dot(onehot, hi) + dot(onehot, mid) + dot(onehot, lo)


def bits(mask):
    return jnp.where(mask, 1.0, 0.0)


def iota(dims, axis):
    return lax.broadcasted_iota(I32, dims, axis)


def before_same_block(rows):
    u, w = iota((rows, rows), 0), iota((rows, rows), 1)
    return bits((w < u) & ((u >> 5) == (w >> 5))).astype(BF16)


def before_all(rows):
    return bits(iota((rows, rows), 1) < iota((rows, rows), 0)).astype(BF16)


def prepare_kernel(c_ref, pieces_ref, norms_ref):
    c = c_ref[...]
    for i, piece in enumerate(split3(c)):
        pieces_ref[i] = piece
    squares = split3(c * c)
    ones = jnp.ones((8, D), BF16)
    norms_ref[...] = sum(dot(ones, s, NT) for s in squares)


def request_kernel(owner_ref, row_ref, cand_ref, rows_ref, out_ref, owner, row, cand, rows, hold, sems):
    copies = [
        pltpu.make_async_copy(a, b, sems.at[i])
        for i, (a, b) in enumerate(
            [(owner_ref, owner), (row_ref, row), (cand_ref, cand), (rows_ref, rows)]
        )
    ]
    start_all(copies)
    shard = iota((SHARDS, V), 0)
    earlier = bits(iota((V, V), 0) < iota((V, V), 1)).astype(BF16)
    lane = iota((SHARDS, 128), 1)
    wait_all(copies)
    hit = owner[...] == shard
    rank = dot(bits(hit).astype(BF16), earlier)
    asked = row[...].astype(F32)
    asks = [
        jnp.sum(jnp.where(hit & (rank == float(k)), asked, 0.0), axis=1, keepdims=True)
        for k in range(2)
    ]
    empty = jnp.zeros((1, V), I32)
    owners = jnp.concatenate([empty, owner[...], empty, empty], axis=1).astype(F32)
    line = jnp.where(lane == 0, asks[0], jnp.where(lane == 1, asks[1], 0.0)) + owners
    hold[pl.ds(0, SHARDS, stride=PER), :] = line
    line = jnp.concatenate([cand[g : g + 1, :] for g in range(GROUPS)], axis=1).astype(F32)
    hold[pl.ds(1, SHARDS, stride=PER), :] = jnp.broadcast_to(line, (SHARDS, 128))
    hits = [cand[g : g + 1, :] == shard for g in range(GROUPS)]
    any_hit = hits[0] | hits[1] | hits[2] | hits[3]
    rank = dot(bits(any_hit).astype(BF16), earlier)
    wide = [split3(rows[:, 128 * h : 128 * h + 128].astype(F32))[:2] for h in range(2)]
    lines = []
    for k in range(2):
        sides = [jnp.zeros((SHARDS, 128), F32)] * 2
        for g in range(GROUPS):
            onehot = bits(hits[g] & (rank == float(k))).astype(BF16)
            sides[g % 2] = sides[g % 2] + dot(onehot, wide[g // 2][0]) + dot(onehot, wide[g // 2][1])
        sides[1 - k] = pltpu.roll(sides[1 - k], GSIZE, 1)
        side = even_lanes if k == 0 else odd_lanes
        lines.append(side(sides[0]) + side(sides[1]))
    hold[pl.ds(2, SHARDS, stride=PER), :] = lines[0] + lines[1]
    copy = pltpu.make_async_copy(hold, out_ref, sems.at[4])
    copy.start()
    copy.wait()


def even_lanes(a):
    return jnp.where(iota(a.shape, 1) < GSIZE, a, 0.0)


def odd_lanes(a):
    return jnp.where(iota(a.shape, 1) < GSIZE, 0.0, a)


def slots_kernel(me_ref, got_ref, found_ref, info_ref, slots_ref, most_ref, hold):
    me, column = me_ref[0], me_ref[1]
    owners = got_ref[pl.ds(0, SHARDS, stride=PER), :].astype(I32)
    cands = got_ref[pl.ds(1, SHARDS, stride=PER), :].astype(I32)
    hold[0] = owners
    hold[1] = cands
    at = pl.multiple_of(column * NZ, NZ)
    tile = jnp.concatenate([hold[0, pl.ds(at, NZ), :], hold[1, pl.ds(at, NZ), :]], axis=0)
    turned = jnp.concatenate([tile, jnp.zeros((128 - NZ * 2, 128), I32)], axis=0).T
    block_lane = iota((V, 128), 1)
    for z in range(NZ):
        block = jnp.where(block_lane == 0, turned[V : 2 * V, z : z + 1], 0)
        for g in range(GROUPS):
            cand = turned[g * V : (g + 1) * V, NZ + z : NZ + z + 1]
            block = jnp.where(block_lane == 1 + g, cand, block)
        info_ref[z * V : (z + 1) * V, :] = block
    lane = iota((COLV, 128), 1)
    hit = lane < 0
    for g in range(GROUPS):
        hit = hit | (info_ref[:, 1 + g : 2 + g] == lane * NZ + me)
    hit = hit & (lane < COLS)
    rank = dot(before_same_block(COLV), bits(hit).astype(BF16))
    mine = (iota((NZ, COLV), 1) >> 5) == iota((NZ, COLV), 0)
    for k in range(2):
        turned = bits(hit & (rank == float(k))).T
        for b in range(COLS):
            part = jnp.where(mine, turned[b : b + 1, :], 0.0)
            slots_ref[b * 16 + k * 8 : b * 16 + k * 8 + 8, :] = part
    lane = iota((SHARDS, 128), 1)
    owners = jnp.where((lane >= V) & (lane < 2 * V), owners, 0)
    owners = owners + pltpu.roll(owners, 2 * V, 1)
    owners = (owners + pltpu.roll(owners, V, 1)) & 7
    parts = []
    for b in range(NZ):
        to_plane = bits((cands & 7) == b)
        to_plane = jnp.maximum(to_plane, pltpu.roll(to_plane, 2 * V, 1))
        to_plane = jnp.maximum(to_plane, pltpu.roll(to_plane, V, 1))
        for h in range(2):
            parts.append(jnp.where(owners == (lane >> 5) + 4 * h, to_plane, 0.0).astype(BF16))
    columns = bits((iota((COLS, SHARDS), 1) >> 3) == iota((COLS, SHARDS), 0)).astype(BF16)
    group = bits((iota((128, 128), 0) >> 5) == iota((128, 128), 1)).astype(BF16)
    most = 0.0
    for part in parts:
        most = jnp.maximum(most, jnp.max(dot(dot(columns, part).astype(BF16), group)))
    most_ref[...] = jnp.full((8, 128), most, F32).astype(I32)


def relay_kernel(me_ref, turn_ref, info_ref, slots_ref, send_ref, take_ref):
    me = me_ref[0]
    base = turn_ref[0].astype(F32)
    depth_of = send_ref.shape[0] // NZ
    lane = iota((COLV, 128), 1)
    u = iota((COLV, 1), 0)
    info = info_ref[...]
    owner = info[:, 0:1]
    hits = bits((owner == lane * NZ + me) & (lane < COLS))
    rank = dot(before_same_block(COLV), hits.astype(BF16))
    rank = jnp.sum(rank * hits, axis=1, keepdims=True)
    here = (owner & 7) == me
    wanted = lane < 0
    to_me = u < 0
    for g in range(GROUPS):
        plane = info[:, 1 + g : 2 + g] & 7
        wanted = wanted | (plane == lane)
        to_me = to_me | (plane == me)
    earlier = before_all(COLV)
    leaves = wanted & (lane < NZ) & here
    order = dot(earlier, bits(leaves).astype(BF16))
    place = jnp.where(leaves, order - base, -1.0).T
    depth = iota((depth_of, COLV), 0).astype(F32)
    rows = jnp.concatenate([bits(place[z : z + 1, :] == depth) for z in range(NZ)], axis=0)
    slot = (owner >> 3) * 16 + rank.astype(I32) * 8 + (u >> 5)
    held = bits((slot == iota((COLV, SLOTS), 1)) & here)
    send_ref[...] = dot(rows.astype(BF16), held.astype(BF16)).astype(BF16)
    comes = ((owner & 7) == lane) & (lane < NZ) & to_me
    order = dot(earlier, bits(comes).astype(BF16)) - base
    fits = comes & (order >= 0.0) & (order < float(depth_of))
    at = jnp.sum(jnp.where(fits, lane.astype(F32) * depth_of + order + 1.0, 0.0), axis=1, keepdims=True)
    found = bits(at == iota((COLV, NZ * depth_of), 1).astype(F32) + 1.0).astype(BF16)
    take_ref[...] = dot(slots_ref[...].astype(BF16), found).astype(BF16)


def fetch_kernel(got_ref, pieces_ref, *rest):
    out_ref, hold, sems = rest[-3:]
    column = iota((SHARDS, ROWS), 1)
    asked = got_ref[pl.ds(0, SHARDS, stride=PER), :].astype(I32)
    pieces = [pieces_ref[i] for i in range(3)]
    copies = []
    for k in range(2):
        onehot = bits(asked[:, k : k + 1] == column).astype(BF16)
        hold[k] = pick(onehot, pieces).reshape(COLS, 8, D)
        copies.append(
            pltpu.make_async_copy(hold.at[k], out_ref.at[:, pl.ds(k * 8, 8), :], sems.at[k])
        )
        copies[-1].start()
    wait_all(copies)


def send_kernel(base_ref, onehot_ref, in_ref, *rest):
    out_ref, hold, sems = rest[-3:]
    pieces = split3(in_ref[...])
    half = onehot_ref.shape[0] // 2
    copies = []
    for c in range(2):
        hold[c] = pick(onehot_ref[c * half : (c + 1) * half, :], pieces)
        copies.append(
            pltpu.make_async_copy(hold.at[c], out_ref.at[pl.ds(c * half, half), :], sems.at[c])
        )
        copies[-1].start()
    wait_all(copies)


def put_kernel(first, onehot_ref, in_ref, both_ref, out_ref, hold, sems):
    pieces = split3(in_ref[...])
    half = SLOTS // 2
    at = [out_ref.at[pl.ds(c * half, half), pl.ds(first, D)] for c in range(2)]
    copies = []
    for c in range(2):
        hold[c] = pick(onehot_ref[c * half : (c + 1) * half, :], pieces)
        copies.append(pltpu.make_async_copy(hold.at[c], at[c], sems.at[c]))
        copies[-1].start()
    wait_all(copies)


def add_kernel(onehot_ref, in_ref, both_ref, out_ref, hold, sems):
    at = out_ref.at[:, pl.ds(D, D)]
    copy = pltpu.make_async_copy(at, hold, sems.at[0])
    copy.start()
    copy.wait()
    hold[...] += pick(onehot_ref[...], split3(in_ref[...]))
    copy = pltpu.make_async_copy(hold, at, sems.at[1])
    copy.start()
    copy.wait()


def vectors_kernel(me_ref, slots_ref, *rest):
    parts, out_ref, column, hold, sems = rest[:NZ], rest[-4], rest[-3], rest[-2], rest[-1]
    me = me_ref[0]
    copies = []
    for i, part in enumerate(parts):
        at = pl.multiple_of(((me + i) & 7) * V, V)
        copies.append(pltpu.make_async_copy(part, column.at[pl.ds(at, V), :], sems.at[i]))
    start_all(copies)
    onehot = slots_ref[...].astype(BF16)
    wait_all(copies)
    pieces = split3(column[...])
    half = SLOTS // 2
    copies = []
    for c in range(2):
        hold[c] = pick(onehot[c * half : (c + 1) * half, :], pieces)
        target = out_ref.at[pl.ds(c * half, half), pl.ds(0, D)]
        copies.append(pltpu.make_async_copy(hold.at[c], target, sems.at[NZ + c]))
        copies[-1].start()
    wait_all(copies)


def lookup(table, rows):
    low, high = rows & 127, rows >> 7
    found = jnp.zeros(rows.shape, F32)
    for i in range(ROWS // 128):
        part = jnp.take_along_axis(table[:, 128 * i : 128 * i + 128], low, axis=1)
        found = jnp.where(high == i, part, found)
    return found


def scores(a, pieces_ref):
    hi, mid, lo = split3(a)
    chi, cmid, clo = (pieces_ref[i] for i in range(3))
    small = dot(mid, cmid, NT) + dot(lo, chi, NT) + dot(hi, clo, NT)
    return dot(hi, chi, NT) + (dot(hi, cmid, NT) + dot(mid, chi, NT) + small)


def loss_kernel(both_ref, got_ref, pieces_ref, norms_ref, out_ref):
    line = got_ref[pl.ds(2, SHARDS, stride=PER), :].astype(I32)
    rows = [line, pltpu.roll(line, GSIZE, 1)]
    rows = jnp.concatenate([a.reshape(COLS, 1, NZ, 128) for a in rows], axis=1).reshape(SLOTS, 128)
    rows = rows & (ROWS - 1)
    x = both_ref[:, :D]
    r = x - both_ref[:, D:]
    square = jnp.sum(x * x, axis=1, keepdims=True)
    near = square - 2.0 * scores(x, pieces_ref) + norms_ref[0:1, :]
    hi = r.astype(BF16)
    mid = (r - hi.astype(F32)).astype(BF16)
    chi, cmid = pieces_ref[0], pieces_ref[1]
    table = dot(hi, chi, NT) + (dot(hi, cmid, NT) + dot(mid, chi, NT))
    rx = jnp.sum(r * x, axis=1, keepdims=True)
    rr = jnp.sum(r * r, axis=1, keepdims=True)
    gap = rx - table
    loss = lookup((near + amplify * gap * gap / (rr + tiny)) / D, rows)
    loss = loss.reshape(COLS, 2, NZ, 128)
    second = pltpu.roll(loss[:, 1].reshape(COLS * NZ, 128), GSIZE, 1)
    first = loss[:, 0].reshape(COLS * NZ, 128)
    out_ref[...] = jnp.where(iota((COLS * NZ, 128), 1) < GSIZE, first, second)


def collect_kernel(owner_ref, in_ref, out_ref):
    lane = iota((V, 128), 1)
    hits = [owner_ref[:, g : g + 1] == lane for g in range(GROUPS)]
    rank = dot(before_same_block(V), bits(hits[0] | hits[1] | hits[2] | hits[3]).astype(BF16))
    a = in_ref[...]
    plain, rolled = split3(a), split3(pltpu.roll(a, GSIZE, 1))
    for h in range(2):
        halves = []
        for g in (2 * h, 2 * h + 1):
            first = bits(hits[g] & (rank == 0.0)).astype(BF16)
            second = bits(hits[g] & (rank == 1.0)).astype(BF16)
            if g % 2 == 0:
                halves.append(pick(first, plain) + pick(second, rolled))
            else:
                halves.append(pick(first, rolled) + pick(second, plain))
        out_ref[:, 128 * h : 128 * h + 128] = jnp.where(lane < GSIZE, halves[0], halves[1])


def swap(a, axes):
    return lax.all_to_all(a, axes, split_axis=0, concat_axis=0, tiled=True)


def shards(new_vectors, centroids, primary_owner, primary_row, cand_owner, cand_row):
    plane = ("y", "x")
    column = lax.axis_index(("y", "x")).astype(I32)
    me = jnp.stack([lax.axis_index("z").astype(I32), column])
    def along_z(block, step):
        return lax.ppermute(block, "z", [(z, (z - step) % NZ) for z in range(NZ)])

    with jax.named_scope("column_vectors"):
        blocks = {0: new_vectors}
        for step in (2, -2, 1, -1, 4):
            blocks[step] = along_z(new_vectors, step)
        blocks[3] = along_z(blocks[2], 1)
        blocks[-3] = along_z(blocks[-2], -1)
    with jax.named_scope("requests"):
        [sent] = call(
            request_kernel,
            [shape((PER * SHARDS, 128))],
            primary_owner.T,
            primary_row.T,
            cand_owner.T,
            cand_row,
            far_in=(0, 1, 2, 3),
            far_out=(0,),
            scratch=[
                pltpu.VMEM((1, V), I32),
                pltpu.VMEM((1, V), I32),
                pltpu.VMEM((GROUPS, V), I32),
                pltpu.VMEM((V, GROUPS * GSIZE), I32),
                pltpu.VMEM((PER * SHARDS, 128), F32),
                copies_semaphores(5),
            ],
            name="request",
        )
        arrived = swap(sent.reshape(SHARDS, 1, PER * 128), ("y", "x", "z")).reshape(PER * SHARDS, 128)
    pieces, norms = call(
        prepare_kernel, [shape((3, ROWS, D), BF16), shape((8, ROWS))], centroids, name="prepare"
    )
    with jax.named_scope("primary_rows"):
        [found] = call(
            fetch_kernel,
            [shape((COLS, 16, D))],
            arrived,
            pieces,
            *[blocks[o] for o in FIRST],
            far_in=tuple(range(2, 2 + len(FIRST))),
            far_out=(0,),
            scratch=[pltpu.VMEM((2, COLS, 8, D), F32), copies_semaphores(2)],
            name="fetch",
        )
        fetched = swap(found, plane).reshape(SLOTS, D)
    info, slots, most = call(
        slots_kernel,
        [shape((COLV, 128), I32), shape((SLOTS, COLV)), shape((8, 128), I32)],
        me,
        arrived,
        found,
        smem=(0,),
        far_in=(2,),
        scratch=[pltpu.VMEM((2, SHARDS, 128), I32)],
        name="slots",
    )
    most = most[:1, :1]
    most = jnp.maximum(most, lax.ppermute(most, "rep", [(0, 1), (1, 0)]))[0, 0]

    halves = [pltpu.VMEM((2, SLOTS // 2, D), F32), copies_semaphores(2)]
    pair = [shape((SLOTS, 2 * D))]

    def relay(base, depth):
        return call(
            relay_kernel,
            [shape((NZ * depth, SLOTS), BF16), shape((SLOTS, NZ * depth), BF16)],
            me,
            base.reshape(1),
            info,
            slots,
            smem=(0, 1),
            name="relay",
        )

    def across(base, send, *after):
        depth = send.shape[0] // NZ
        [leaving] = call(
            send_kernel,
            [shape((NZ * depth, D))],
            base.reshape(1),
            send,
            fetched,
            *after,
            smem=(0,),
            far_in=tuple(range(3, 3 + len(after))),
            far_out=(0,),
            scratch=[pltpu.VMEM((2, NZ * depth // 2, D), F32), copies_semaphores(2)],
            name="send",
        )
        return swap(leaving.reshape(NZ, depth, D), "z").reshape(NZ * depth, D)

    def add(take, got, both):
        [both] = call(
            add_kernel,
            pair,
            take,
            got,
            both,
            far_in=(2,),
            far_out=(0,),
            alias={2: 0},
            scratch=[pltpu.VMEM((SLOTS, D), F32), copies_semaphores(2)],
            name="add",
        )
        return both

    def second(state):
        base, both = state
        return base + NEXT, add(next_take, across(base, next_send), both)

    def more(state):
        base, both = state
        send, take = relay(base, K)
        return base + K, add(take, across(base, send), both)

    with jax.named_scope("vectors_out"):
        [both] = call(
            vectors_kernel,
            pair,
            me,
            slots,
            *[blocks[o] for o in (0, 1, 2, 3, 4, -3, -2, -1)],
            smem=(0,),
            far_in=tuple(range(2, 2 + NZ)),
            far_out=(0,),
            scratch=[pltpu.VMEM((COLV, D), F32), halves[0], copies_semaphores(NZ + 2)],
            name="vectors",
        )
    with jax.named_scope("primary_across"):
        send, take = relay(jnp.int32(0), K)
        got = across(jnp.int32(0), send, *[blocks[o] for o in (4, 3, -3)])
        next_send, next_take = relay(jnp.int32(K), NEXT)
        [both] = call(
            functools.partial(put_kernel, D),
            pair,
            take,
            got,
            both,
            far_in=(2,),
            far_out=(0,),
            alias={2: 0},
            scratch=halves,
            name="put",
        )
        state = (jnp.int32(K), both)
        state = lax.while_loop(lambda s: (s[0] == K) & (K < most), second, state)
        _, both = lax.while_loop(lambda s: s[0] < most, more, state)
    with jax.named_scope("out_to_owners"):
        both = swap(both.reshape(COLS, 16, 2 * D), plane).reshape(SLOTS, 2 * D)
    [losses] = call(
        loss_kernel, [shape((SHARDS, 128))], both, arrived, pieces, norms, name="loss"
    )
    with jax.named_scope("losses_back"):
        back = swap(losses.reshape(SHARDS, 1, 128), ("y", "x", "z")).reshape(SHARDS, 128)
    [result] = call(
        collect_kernel, [shape((V, GROUPS * GSIZE))], cand_owner, back, name="collect"
    )
    return result


def solution(mesh):
    fine = Mesh(mesh.devices.reshape(NY, NX, NZ, 2), ("y", "x", "z", "rep"))
    rows = P(("y", "x", "z", "rep"), None)
    in_specs = (rows, P(("y", "x", "z"), None), rows, rows, rows, rows)
    return jax.shard_map(shards, mesh=fine, in_specs=in_specs, out_specs=rows, check_vma=False)
```
